32 devices in a mesh: img: 8 (over y, x, core), blk: 4 (over z).
Axes of the slice: x: 2, y: 2, z: 4, core: 2. Of those that a mesh axis runs over, the one named last changes fastest.
Arguments:
- images_large: bfloat16 [32, 584, 768], P('img', 'blk'), may hold values from -6 to 6
- images_small: bfloat16 [64, 200, 768], P(('img', 'blk')), may hold values from -6 to 6
- cotan_large: bfloat16 [32, 584, 768], P('img', 'blk'), may hold values from -6 to 6
- cotan_small: bfloat16 [64, 200, 768], P(('img', 'blk')), may hold values from -6 to 6
- lengths_large: int32 [32], P('img'), may hold values from 192 to 577, as said below
- lengths_small: int32 [64], P(('img', 'blk')), may hold values from 65 to 197, as said below
- index_large: int32 [584, 584], replicated, may hold values from 0 to 2211
- index_small: int32 [200, 200], replicated, may hold values from 0 to 731
- attn_gain: bfloat16 [768], replicated, may hold values from 0.5 to 1.5
- attn_shift: bfloat16 [768], replicated, may hold values from -1.796875 to 1.796875
- qkv_weight: bfloat16 [768, 2304], replicated, may hold values from -0.21875 to 0.21875
- query_bias: bfloat16 [768], replicated, may hold values from -3 to 3
- value_bias: bfloat16 [768], replicated, may hold values from -0.8984375 to 0.8984375
- table_large: bfloat16 [2212, 12], replicated, may hold values from -4 to 4
- table_small: bfloat16 [732, 12], replicated, may hold values from -4 to 4
- proj_weight: bfloat16 [768, 768], replicated, may hold values from -1.25 to 1.25
- proj_bias: bfloat16 [768], replicated, may hold values from -1.796875 to 1.796875
- attn_scale: bfloat16 [768], replicated, may hold values from 0.5 to 1.5
- mlp_gain: bfloat16 [768], replicated, may hold values from 0.5 to 1.5
- mlp_shift: bfloat16 [768], replicated, may hold values from -1.796875 to 1.796875
- inner_weight: bfloat16 [768, 3072], replicated, may hold values from -0.21875 to 0.21875
- inner_bias: bfloat16 [3072], replicated, may hold values from -1.796875 to 1.796875
- outer_weight: bfloat16 [3072, 768], replicated, may hold values from -0.109375 to 0.109375
- outer_bias: bfloat16 [768], replicated, may hold values from -1.796875 to 1.796875
- mlp_scale: bfloat16 [768], replicated, may hold values from 0.5 to 1.5
Outputs:
- result_large: bfloat16 [32, 584, 768], P('img', 'blk')
- result_small: bfloat16 [64, 200, 768], P(('img', 'blk'))
- grad_large: bfloat16 [32, 584, 768], P('img', 'blk')
- grad_small: bfloat16 [64, 200, 768], P(('img', 'blk'))
- grad_attn_gain: float32 [768], P(('img', 'blk'))
- grad_attn_shift: float32 [768], P(('img', 'blk'))
- grad_qkv_weight: float32 [768, 2304], P(('img', 'blk'))
- grad_query_bias: float32 [768], P(('img', 'blk'))
- grad_value_bias: float32 [768], P(('img', 'blk'))
- grad_table_large: float32 [2212, 12], replicated
- grad_table_small: float32 [732, 12], replicated
- grad_proj_weight: float32 [768, 768], P(('img', 'blk'))
- grad_proj_bias: float32 [768], P(('img', 'blk'))
- grad_attn_scale: float32 [768], P(('img', 'blk'))
- grad_mlp_gain: float32 [768], P(('img', 'blk'))
- grad_mlp_shift: float32 [768], P(('img', 'blk'))
- grad_inner_weight: float32 [768, 3072], P(('img', 'blk'))
- grad_inner_bias: float32 [3072], P(('img', 'blk'))
- grad_outer_weight: float32 [3072, 768], P(('img', 'blk'))
- grad_outer_bias: float32 [768], P(('img', 'blk'))
- grad_mlp_scale: float32 [768], P(('img', 'blk'))
The draws below stay inside these ranges and needn't reach their ends.
Inputs may be any that keep to these rules, and one draw needn't show every extreme that they name: `lengths_large`: valid tokens of each 384px image; positions at or past it are padding. Among the 4 images of each index of img one has 577 and one 577 // 3. `lengths_small`: valid tokens of each 224px image; positions at or past it are padding. Among the 2 images of each device one has 197 and one 197 // 3.
All inputs are finite; a program needn't handle non-finite values.
Results may differ from the reference program's by a relative error of at most 0.024.
Values may be sent and summed in bfloat16 or wider, within the bound.
No kernel may reach another device: no remote copies, remote signals or barrier semaphores. Data moves between devices by JAX's collectives and lax.ppermute only.
A program may use at most 320 MiB of HBM per device.

```python
from functools import partial
import jax
import jax.numpy as jnp
from jax import lax

D = 768
HEADS = 12
HEAD = 64
FF = 3072
LEN_LARGE = 584
LEN_SMALL = 200
VALID_LARGE = 577
VALID_SMALL = 197
REL_LARGE = 2212
REL_SMALL = 732
PER_LARGE = 4
SMALL_DEV = 2
IMAGES_LARGE = 32
IMAGES_SMALL = 64


def ragged(key, images, per, most):
    first, second = jax.random.split(key)
    drawn = jax.random.randint(first, (images // per, per), most // 3, most + 1)
    chosen = jax.random.randint(second, (images // per, 1), 0, per)
    slots = jnp.arange(per, dtype=jnp.int32)[None, :]
    lengths = jnp.where(slots == chosen, most, drawn)
    lengths = jnp.where(slots == (chosen + 1) % per, most // 3, lengths)
    return lengths.reshape(images).astype(jnp.int32)


def draw_lengths_large(key, part):
    key = jax.random.fold_in(key, 1)
    return ragged(key, IMAGES_LARGE, PER_LARGE, VALID_LARGE)


def draw_lengths_small(key, part):
    key = jax.random.fold_in(key, 2)
    return ragged(key, IMAGES_SMALL, SMALL_DEV, VALID_SMALL)


def with_ends(values, rng, least, top_value):
    longest = values.shape.index(max(values.shape))
    spots = []
    for shift in (0, 1):
        where = [jax.random.randint(jax.random.fold_in(rng, axis), (), 0, length) for axis, length in enumerate(values.shape)]
        where[longest] = (where[longest] + shift) % values.shape[longest]
        spots.append(tuple(where))
    return values.at[spots[0]].set(least).at[spots[1]].set(top_value)


def block_levels(own_key, shape, cuts, least, top_value):
    def one(position, blocks):
        heights = jax.random.uniform(jax.random.fold_in(jax.random.fold_in(own_key, 6), position), (blocks,), jnp.float32, least / len(cuts), top_value / len(cuts))
        return jnp.repeat(jnp.exp(heights), shape[position] // blocks).reshape((-1,) + (1,) * (len(shape) - position - 1))

    loudness = one(*cuts[0])
    for cut in cuts[1:]:
        loudness = loudness * one(*cut)
    return loudness


def gaussian(stream_key, dims, scale, bound, pieces=(), held_as=jnp.bfloat16):
    level = block_levels(stream_key, dims, pieces, -0.22, 0.18) if pieces else 1.0
    values = jax.random.normal(stream_key, dims, jnp.float32) * scale * level
    return jnp.minimum(jnp.maximum(values, -bound), bound).astype(held_as)


def setup_inputs(seed: int = 0) -> dict:
    keys = jax.random.split(jax.random.key(seed), 26)
    images_large = gaussian(keys[0], (IMAGES_LARGE, LEN_LARGE, D), 1.0, 6.0, ((0, 8), (1, 4)))
    images_small = gaussian(keys[1], (IMAGES_SMALL, LEN_SMALL, D), 1.0, 6.0, ((0, 32),))
    cotan_large = gaussian(keys[2], (IMAGES_LARGE, LEN_LARGE, D), 1.0, 6.0, ((0, 8), (1, 4)))
    cotan_small = gaussian(keys[3], (IMAGES_SMALL, LEN_SMALL, D), 1.0, 6.0, ((0, 32),))
    lengths_large = draw_lengths_large(jax.random.fold_in(keys[25], 71), 0)
    lengths_small = draw_lengths_small(jax.random.fold_in(keys[25], 71), 0)
    index_large = with_ends(jax.random.randint(keys[6], (LEN_LARGE, LEN_LARGE), 0, REL_LARGE), jax.random.fold_in(keys[6], 1), 0, REL_LARGE - 1).astype(jnp.int32)
    index_small = with_ends(jax.random.randint(keys[7], (LEN_SMALL, LEN_SMALL), 0, REL_SMALL), jax.random.fold_in(keys[7], 1), 0, REL_SMALL - 1).astype(jnp.int32)
    attn_gain = jnp.clip(1.0 + 0.1 * jax.random.normal(keys[8], (D,), jnp.float32), 0.5, 1.5).astype(jnp.bfloat16)
    attn_shift = gaussian(keys[9], (D,), 0.3, 1.796875)
    qkv_weight = gaussian(keys[10], (D, 3 * D), D ** -0.5, 0.21875)
    query_bias = gaussian(keys[11], (D,), 0.5, 3.0)
    value_bias = gaussian(keys[12], (D,), 0.15, 0.8984375)
    table_large = gaussian(keys[13], (REL_LARGE, HEADS), 1.0, 4.0)
    table_small = gaussian(keys[14], (REL_SMALL, HEADS), 1.0, 4.0)
    proj_weight = gaussian(keys[15], (D, D), (D // 32) ** -0.5, 1.25)
    proj_bias = gaussian(keys[16], (D,), 0.3, 1.796875)
    attn_scale = jnp.clip(1.0 + 0.1 * jax.random.normal(keys[17], (D,), jnp.float32), 0.5, 1.5).astype(jnp.bfloat16)
    mlp_gain = jnp.clip(1.0 + 0.1 * jax.random.normal(keys[18], (D,), jnp.float32), 0.5, 1.5).astype(jnp.bfloat16)
    mlp_shift = gaussian(keys[19], (D,), 0.3, 1.796875)
    inner_weight = gaussian(keys[20], (D, FF), D ** -0.5, 0.21875)
    inner_bias = gaussian(keys[21], (FF,), 0.3, 1.796875)
    outer_weight = gaussian(keys[22], (FF, D), FF ** -0.5, 0.109375)
    outer_bias = gaussian(keys[23], (D,), 0.3, 1.796875)
    mlp_scale = jnp.clip(1.0 + 0.1 * jax.random.normal(keys[24], (D,), jnp.float32), 0.5, 1.5).astype(jnp.bfloat16)
    return {"images_large": images_large, "images_small": images_small, "cotan_large": cotan_large, "cotan_small": cotan_small, "lengths_large": lengths_large, "lengths_small": lengths_small, "index_large": index_large, "index_small": index_small, "attn_gain": attn_gain, "attn_shift": attn_shift, "qkv_weight": qkv_weight, "query_bias": query_bias, "value_bias": value_bias, "table_large": table_large, "table_small": table_small, "proj_weight": proj_weight, "proj_bias": proj_bias, "attn_scale": attn_scale, "mlp_gain": mlp_gain, "mlp_shift": mlp_shift, "inner_weight": inner_weight, "inner_bias": inner_bias, "outer_weight": outer_weight, "outer_bias": outer_bias, "mlp_scale": mlp_scale}


NEGATIVE = -1e+30
EPSILON = 1e-06
HIGHEST = lax.Precision.HIGHEST

@jax.custom_vjp
def low(v):
    return lax.optimization_barrier(v.astype(jnp.bfloat16)).astype(jnp.float32)

@jax.custom_vjp
def low_back(v):
    return v

def low_keep(v):
    return (low(v), None)

def low_pass(kept, grad):
    return (grad,)

def back_keep(v):
    return (v, None)

def back_low(kept, grad):
    return (low(grad),)
low.defvjp(low_keep, low_pass)
low_back.defvjp(back_keep, back_low)

def layer_norm(values, gain, shift):
    center = values - lax.optimization_barrier(jnp.mean(values, -1, keepdims=True))
    spread = lax.optimization_barrier(jnp.mean(center * center, -1, keepdims=True))
    return center * lax.rsqrt(spread + EPSILON) * gain + shift

def relative_bias(table, index):
    return jnp.take(table.T, index, axis=1)

def one_image(bias, item):
    token_rows, length = item
    count = token_rows.shape[0]
    parts = token_rows.reshape(count, 3, HEADS, HEAD)
    scores = jnp.einsum('qhe,khe->hqk', parts[:, 0], parts[:, 1], precision=HIGHEST) * HEAD ** (-0.5) + bias
    scores = low_back(scores)
    valid = (jnp.arange(count, dtype=jnp.int32) < length)[None, None, :]
    scores = jnp.where(valid, scores, NEGATIVE)
    weights = jnp.exp(scores - lax.optimization_barrier(jnp.max(scores, -1, keepdims=True)))
    probs = weights / lax.optimization_barrier(jnp.sum(weights, -1, keepdims=True))
    return jnp.einsum('hqk,khe->qhe', probs, parts[:, 2], precision=HIGHEST).reshape(count, HEADS * HEAD)

def attention(projected, lengths, bias):
    return lax.map(partial(jax.checkpoint(one_image), bias), (projected, lengths))

def reference(images_large, images_small, cotan_large, cotan_small, lengths_large, lengths_small, index_large, index_small, attn_gain, attn_shift, qkv_weight, query_bias, value_bias, table_large, table_small, proj_weight, proj_bias, attn_scale, mlp_gain, mlp_shift, inner_weight, inner_bias, outer_weight, outer_bias, mlp_scale):
    wide = jnp.float32

    def forward(large, small, attn_gain, attn_shift, qkv_weight, query_bias, value_bias, table_large, table_small, proj_weight, proj_bias, attn_scale, mlp_gain, mlp_shift, inner_weight, inner_bias, outer_weight, outer_bias, mlp_scale):
        width = attn_gain.shape[0]
        split_at = IMAGES_LARGE * LEN_LARGE
        flat = jnp.concatenate([large.reshape(-1, width), small.reshape(-1, width)], 0)
        normed = low(layer_norm(flat, attn_gain, attn_shift))
        bias_vector = jnp.concatenate([query_bias, jnp.zeros((width,), wide), value_bias])
        projected = low(low_back(jnp.dot(normed, qkv_weight, precision=HIGHEST) + bias_vector))
        attended_large = attention(projected[:split_at].reshape(IMAGES_LARGE, LEN_LARGE, 3 * width), lengths_large, relative_bias(table_large, index_large))
        attended_small = attention(projected[split_at:].reshape(IMAGES_SMALL, LEN_SMALL, 3 * width), lengths_small, relative_bias(table_small, index_small))
        attended = low(low_back(jnp.concatenate([attended_large.reshape(-1, width), attended_small.reshape(-1, width)], 0)))
        branch = low_back(jnp.dot(attended, proj_weight, precision=HIGHEST) + proj_bias)
        middle = flat + attn_scale * branch
        normed_mlp = low(layer_norm(middle, mlp_gain, mlp_shift))
        pre_act = low_back(jnp.dot(normed_mlp, inner_weight, precision=HIGHEST) + inner_bias)
        activated = low(jax.nn.gelu(pre_act, approximate=False))
        outer = low_back(jnp.dot(activated, outer_weight, precision=HIGHEST) + outer_bias)
        result = middle + mlp_scale * outer
        return (result[:split_at].reshape(IMAGES_LARGE, LEN_LARGE, width), result[split_at:].reshape(IMAGES_SMALL, LEN_SMALL, width))
    params = [item.astype(wide) for item in (attn_gain, attn_shift, qkv_weight, query_bias, value_bias, table_large, table_small, proj_weight, proj_bias, attn_scale, mlp_gain, mlp_shift, inner_weight, inner_bias, outer_weight, outer_bias, mlp_scale)]
    outputs, pullback = jax.vjp(forward, images_large.astype(wide), images_small.astype(wide), *params)
    grads = pullback((cotan_large.astype(wide), cotan_small.astype(wide)))
    return (outputs[0].astype(jnp.bfloat16), outputs[1].astype(jnp.bfloat16), grads[0].astype(jnp.bfloat16), grads[1].astype(jnp.bfloat16), grads[2], grads[3], grads[4], grads[5], grads[6], grads[7], grads[8], grads[9], grads[10], grads[11], grads[12], grads[13], grads[14], grads[15], grads[16], grads[17], grads[18])
```

```python
import functools

import jax
import jax.numpy as jnp
from jax import lax
from jax.experimental import pallas as pl
from jax.experimental.pallas import tpu as pltpu
from jax.sharding import PartitionSpec as P

HEAD = 64


NEGATIVE = -1e30
EPSILON = 1e-06
HIGHEST = lax.Precision.HIGHEST


def layer_norm(values, gain, shift):
    center = values - jnp.mean(values, -1, keepdims=True)
    spread = jnp.mean(center * center, -1, keepdims=True)
    return center * lax.rsqrt(spread + EPSILON) * gain + shift


def exact_gelu(values):
    return jax.nn.gelu(values, approximate=False)


def lookup(table, index_block):
    table_codes = jnp.arange(table.shape[0], dtype=jnp.int32)

    def lookup_one_query(index_row):
        selector = (index_row[:, None] == table_codes[None, :]).astype(jnp.bfloat16)
        return jnp.dot(selector, table, preferred_element_type=jnp.float32)

    picked = lax.map(lookup_one_query, index_block, batch_size=8)
    return jnp.transpose(picked, (2, 0, 1))


def table_gradient(grad_full, index_block, table_rows):
    table_codes = jnp.arange(table_rows, dtype=jnp.int32)

    def table_one_query(item):
        index_row, grad_row = item
        selector = (index_row[:, None] == table_codes[None, :]).astype(jnp.float32)
        return jnp.dot(selector.T, grad_row, precision=HIGHEST, preferred_element_type=jnp.float32)

    partials = lax.map(
        table_one_query, (index_block, jnp.transpose(grad_full, (1, 2, 0))), batch_size=8
    )
    return jnp.sum(partials, 0)


def key_mask(lengths, first, count):
    places = first + jnp.arange(count, dtype=jnp.int32)
    return (places[None, :] < lengths[:, None])[:, None, None, :]


def block_scores(queries, key_piece, bias_rows, lengths, first):
    count = key_piece.shape[1]
    scores = jnp.einsum(
        "iqhe,ikhe->ihqk", queries, key_piece, preferred_element_type=jnp.float32
    ) * HEAD ** (-0.5)
    scores = scores + lax.dynamic_slice_in_dim(bias_rows, first, count, 2)[None]
    return (scores, key_mask(lengths, first, count))


def merge_heads(values):
    return jnp.transpose(values, (0, 2, 1, 3)).reshape(-1, values.shape[1] * values.shape[3])


def local_fold(pieces):

    def visit(step, state):
        return step(state, pieces, 0)

    return visit


def forward_attention(queries, bias_rows, lengths, visit):
    images, rows, heads, width = queries.shape

    def absorb(state, pieces, first):
        top, total, summed = state
        key_piece, value_piece = pieces
        scores, valid = block_scores(queries, key_piece, bias_rows, lengths, first)
        scores = jnp.where(valid, scores, NEGATIVE)
        new_top = jnp.maximum(top, jnp.max(scores, -1))
        weights = jnp.where(valid, jnp.exp(scores - new_top[..., None]), 0.0)
        factor = jnp.exp(top - new_top)
        total = total * factor + jnp.sum(weights, -1)
        update = jnp.einsum(
            "ihqk,ikhe->ihqe", weights, value_piece.astype(jnp.float32), precision=HIGHEST
        )
        return (new_top, total, summed * factor[..., None] + update)

    start_state = (
        jnp.full((images, heads, rows), NEGATIVE, jnp.float32),
        jnp.zeros((images, heads, rows), jnp.float32),
        jnp.zeros((images, heads, rows, width), jnp.float32),
    )
    top, total, summed = visit(absorb, start_state)
    return (summed / total[..., None], top + jnp.log(total))


def key_pass(queries, bias_rows, lengths, grad_out, inner, log_total, visit):
    images, rows, heads, width = queries.shape
    length = bias_rows.shape[2]
    grad_wide = grad_out.astype(jnp.float32)

    def collect(state, pieces, first):
        key_piece, value_piece = pieces
        scores, valid = block_scores(queries, key_piece, bias_rows, lengths, first)
        probs = jnp.where(valid, jnp.exp(scores - log_total[..., None]), 0.0)
        grad_probs = jnp.einsum(
            "iqhe,ikhe->ihqk", grad_out, value_piece, preferred_element_type=jnp.float32
        )
        grad_scores = (probs * (grad_probs - inner[..., None])).astype(jnp.bfloat16)
        grad_query = state[0] + jnp.einsum(
            "ihqk,ikhe->ihqe", grad_scores, key_piece, preferred_element_type=jnp.float32
        ) * HEAD ** (-0.5)
        bias_full = lax.dynamic_update_slice_in_dim(
            state[1], jnp.sum(grad_scores.astype(jnp.float32), 0), first, 2
        )
        key_part = jnp.einsum(
            "ihqk,iqhe->ikhe", grad_scores, queries, preferred_element_type=jnp.float32
        ) * HEAD ** (-0.5)
        value_part = jnp.einsum("ihqk,iqhe->ikhe", probs, grad_wide, precision=HIGHEST)
        key_full = lax.dynamic_update_slice_in_dim(state[2], key_part, first, 1)
        value_full = lax.dynamic_update_slice_in_dim(state[3], value_part, first, 1)
        return (grad_query, bias_full, key_full, value_full)

    start_state = (
        jnp.zeros((images, heads, rows, width), jnp.float32),
        jnp.zeros((heads, rows, length), jnp.float32),
    )
    start_state = start_state + (
        jnp.zeros((images, length, heads, width), jnp.float32),
        jnp.zeros((images, length, heads, width), jnp.float32),
    )
    return visit(collect, start_state)


def on_device(
    images_large,
    images_small,
    cotan_large,
    cotan_small,
    lengths_large,
    lengths_small,
    index_large,
    index_small,
    attn_gain,
    attn_shift,
    qkv_weight,
    query_bias,
    value_bias,
    table_large,
    table_small,
    proj_weight,
    proj_bias,
    attn_scale,
    mlp_gain,
    mlp_shift,
    inner_weight,
    inner_bias,
    outer_weight,
    outer_bias,
    mlp_scale,
):
    wide = jnp.float32
    narrow = jnp.bfloat16
    width = attn_gain.shape[0]
    heads = table_large.shape[1]
    large_count, large_rows = (images_large.shape[0], images_large.shape[1])
    small_count, small_rows = (images_small.shape[0], images_small.shape[1])
    split_at = large_count * large_rows
    first_key = lax.axis_index("blk") * large_rows
    flat = jnp.concatenate(
        [images_large.reshape(-1, width), images_small.reshape(-1, width)], 0
    ).astype(wide)
    normed, attn_norm_back = jax.vjp(
        layer_norm, flat, attn_gain.astype(wide), attn_shift.astype(wide)
    )
    normed_low = normed.astype(narrow)
    bias_vector = jnp.concatenate(
        [query_bias.astype(wide), jnp.zeros((width,), wide), value_bias.astype(wide)]
    )
    projected = (jnp.dot(normed_low, qkv_weight, preferred_element_type=wide) + bias_vector).astype(
        narrow
    )
    large_parts = projected[:split_at].reshape(large_count, large_rows, 3, heads, -1)
    large_query, large_key, large_value = (
        large_parts[:, :, 0],
        large_parts[:, :, 1],
        large_parts[:, :, 2],
    )
    large_index = lax.dynamic_slice_in_dim(index_large, first_key, large_rows, 0)
    large_bias = lookup(table_large, large_index)

    def forward_visit(step, state):
        return step(
            state,
            (
                lax.all_gather(large_key, "blk", axis=1, tiled=True),
                lax.all_gather(large_value, "blk", axis=1, tiled=True),
            ),
            jnp.int32(0),
        )

    def backward_visit(step, state):
        return step(
            state,
            (
                lax.all_gather(large_key, "blk", axis=1, tiled=True),
                lax.all_gather(large_value, "blk", axis=1, tiled=True),
            ),
            jnp.int32(0),
        )

    large_attended, large_log = forward_attention(
        large_query, large_bias, lengths_large, forward_visit
    )
    small_parts = projected[split_at:].reshape(small_count, small_rows, 3, heads, -1)
    small_query, small_key, small_value = (
        small_parts[:, :, 0],
        small_parts[:, :, 1],
        small_parts[:, :, 2],
    )
    small_bias = lookup(table_small, index_small)
    small_visit = local_fold((small_key, small_value))
    small_attended, small_log = forward_attention(
        small_query, small_bias, lengths_small, small_visit
    )
    attended_low = jnp.concatenate(
        [merge_heads(large_attended), merge_heads(small_attended)], 0
    ).astype(narrow)
    branch = jnp.dot(attended_low, proj_weight, preferred_element_type=wide) + proj_bias.astype(
        wide
    )
    middle = flat + attn_scale.astype(wide) * branch
    normed_mlp, mlp_norm_back = jax.vjp(
        layer_norm, middle, mlp_gain.astype(wide), mlp_shift.astype(wide)
    )
    normed_mlp_low = normed_mlp.astype(narrow)
    pre_act = jnp.dot(
        normed_mlp_low, inner_weight, preferred_element_type=wide
    ) + inner_bias.astype(wide)
    activated, gelu_back = jax.vjp(exact_gelu, pre_act)
    activated_low = activated.astype(narrow)
    outer = jnp.dot(activated_low, outer_weight, preferred_element_type=wide) + outer_bias.astype(
        wide
    )
    result_low = (middle + mlp_scale.astype(wide) * outer).astype(narrow)
    cotan = jnp.concatenate(
        [cotan_large.reshape(-1, width), cotan_small.reshape(-1, width)], 0
    ).astype(wide)
    grad_mlp_scale = jnp.sum(cotan * outer, 0)
    grad_outer = (mlp_scale.astype(wide) * cotan).astype(narrow)
    grad_outer_bias = jnp.sum(grad_outer.astype(wide), 0)
    grad_outer_weight = jnp.dot(activated_low.T, grad_outer, preferred_element_type=wide)
    grad_activated = jnp.dot(grad_outer, outer_weight.T, preferred_element_type=wide)
    grad_pre = gelu_back(grad_activated)[0].astype(narrow)
    grad_inner_bias = jnp.sum(grad_pre.astype(wide), 0)
    grad_inner_weight = jnp.dot(normed_mlp_low.T, grad_pre, preferred_element_type=wide)
    grad_normed_mlp = jnp.dot(grad_pre, inner_weight.T, preferred_element_type=wide)
    grad_middle_part, grad_mlp_gain, grad_mlp_shift = mlp_norm_back(grad_normed_mlp)
    grad_middle = cotan + grad_middle_part
    grad_attn_scale = jnp.sum(grad_middle * branch, 0)
    grad_branch = (attn_scale.astype(wide) * grad_middle).astype(narrow)
    grad_proj_bias = jnp.sum(grad_branch.astype(wide), 0)
    grad_proj_weight = jnp.dot(attended_low.T, grad_branch, preferred_element_type=wide)
    grad_attended = jnp.dot(grad_branch, proj_weight.T, preferred_element_type=wide).astype(narrow)
    large_grad_out = grad_attended[:split_at].reshape(large_count, large_rows, heads, -1)
    large_inner = jnp.einsum("iqhe,ihqe->ihq", large_grad_out.astype(wide), large_attended)
    large_grad_query, large_bias_full, key_full, value_full = key_pass(
        large_query,
        large_bias,
        lengths_large,
        large_grad_out,
        large_inner,
        large_log,
        backward_visit,
    )
    large_key_grad, large_value_grad = (
        lax.psum_scatter(
            key_full.astype(jnp.bfloat16), "blk", scatter_dimension=1, tiled=True
        ).astype(jnp.float32),
        lax.psum_scatter(
            value_full.astype(jnp.bfloat16), "blk", scatter_dimension=1, tiled=True
        ).astype(jnp.float32),
    )
    large_grads = jnp.stack(
        [jnp.transpose(large_grad_query, (0, 2, 1, 3)), large_key_grad, large_value_grad], 2
    ).reshape(split_at, 3 * width)
    large_table_grad = table_gradient(large_bias_full, large_index, table_large.shape[0])
    small_grad_out = grad_attended[split_at:].reshape(small_count, small_rows, heads, -1)
    small_inner = jnp.einsum("iqhe,ihqe->ihq", small_grad_out.astype(wide), small_attended)
    small_grad_query, small_bias_full, small_key_grad, small_value_grad = key_pass(
        small_query, small_bias, lengths_small, small_grad_out, small_inner, small_log, small_visit
    )
    small_grads = jnp.stack(
        [jnp.transpose(small_grad_query, (0, 2, 1, 3)), small_key_grad, small_value_grad], 2
    ).reshape(small_count * small_rows, 3 * width)
    small_table_grad = table_gradient(small_bias_full, index_small, table_small.shape[0])
    grad_projected = jnp.concatenate([large_grads, small_grads], 0).astype(narrow)
    grad_query_bias = jnp.sum(grad_projected[:, :width].astype(wide), 0)
    grad_value_bias = jnp.sum(grad_projected[:, 2 * width :].astype(wide), 0)
    grad_qkv_weight = jnp.dot(normed_low.T, grad_projected, preferred_element_type=wide)
    grad_normed = jnp.dot(grad_projected, qkv_weight.T, preferred_element_type=wide)
    grad_flat_part, grad_attn_gain, grad_attn_shift = attn_norm_back(grad_normed)
    grad_flat = (grad_middle + grad_flat_part).astype(narrow)
    summed = (
        lax.psum_scatter(grad_attn_gain, ("img", "blk"), scatter_dimension=0, tiled=True),
        lax.psum_scatter(grad_attn_shift, ("img", "blk"), scatter_dimension=0, tiled=True),
        lax.psum_scatter(grad_qkv_weight, ("img", "blk"), scatter_dimension=0, tiled=True),
        lax.psum_scatter(grad_query_bias, ("img", "blk"), scatter_dimension=0, tiled=True),
        lax.psum_scatter(grad_value_bias, ("img", "blk"), scatter_dimension=0, tiled=True),
        lax.psum_scatter(grad_proj_weight, ("img", "blk"), scatter_dimension=0, tiled=True),
        lax.psum_scatter(grad_proj_bias, ("img", "blk"), scatter_dimension=0, tiled=True),
        lax.psum_scatter(grad_attn_scale, ("img", "blk"), scatter_dimension=0, tiled=True),
        lax.psum_scatter(grad_mlp_gain, ("img", "blk"), scatter_dimension=0, tiled=True),
        lax.psum_scatter(grad_mlp_shift, ("img", "blk"), scatter_dimension=0, tiled=True),
        lax.psum_scatter(grad_inner_weight, ("img", "blk"), scatter_dimension=0, tiled=True),
        lax.psum_scatter(grad_inner_bias, ("img", "blk"), scatter_dimension=0, tiled=True),
        lax.psum_scatter(grad_outer_weight, ("img", "blk"), scatter_dimension=0, tiled=True),
        lax.psum_scatter(grad_outer_bias, ("img", "blk"), scatter_dimension=0, tiled=True),
        lax.psum_scatter(grad_mlp_scale, ("img", "blk"), scatter_dimension=0, tiled=True),
    )
    table_sum_large, table_sum_small = lax.psum(
        (large_table_grad, small_table_grad), ("img", "blk")
    )
    return (
        result_low[:split_at].reshape(large_count, large_rows, width),
        result_low[split_at:].reshape(small_count, small_rows, width),
        grad_flat[:split_at].reshape(large_count, large_rows, width),
        grad_flat[split_at:].reshape(small_count, small_rows, width),
        summed[0],
        summed[1],
        summed[2],
        summed[3],
        summed[4],
        table_sum_large,
        table_sum_small,
        summed[5],
        summed[6],
        summed[7],
        summed[8],
        summed[9],
        summed[10],
        summed[11],
        summed[12],
        summed[13],
        summed[14],
    )


NT = (((1,), (1,)), ((), ()))
TN = (((0,), (0,)), ((), ()))
WIDE = jnp.float32
NARROW = jnp.bfloat16
LANES = 128
FIXED = 4096.0
MEGA = 1 << 20


def round_up(count, step):
    return -(-count // step) * step


def params(limit, *names):
    return pltpu.CompilerParams(vmem_limit_bytes=limit * MEGA, dimension_semantics=("arbitrary",))


def whole(shape):
    return pl.BlockSpec(shape, lambda i: (0,) * len(shape), pipeline_mode=pl.Buffered(1))


def row_norm(values):
    center = values - jnp.mean(values, -1, keepdims=True)
    spread = jnp.mean(center * center, -1, keepdims=True)
    inverse = lax.rsqrt(spread + EPSILON)
    return center * inverse, inverse


def norm_backward(grad, normal, inverse, gain):
    scaled = grad * gain
    first = jnp.mean(scaled, -1, keepdims=True)
    second = jnp.mean(scaled * normal, -1, keepdims=True)
    return inverse * (scaled - first - normal * second)


def bias_kernel(pairs, groups, table_ref, index_ref, out_ref):
    rows, lanes = index_ref.shape

    def one_tile(tile, carry):
        column = pl.multiple_of(tile * LANES, LANES)
        for first in range(0, rows, 16):
            found = []
            for half in (0, 8):
                index = index_ref[pl.ds(first + half, 8), pl.ds(column, LANES)]
                low = lax.bitwise_and(index, LANES - 1)
                high = lax.shift_right_logical(index, 7)
                picked = [None] * pairs
                for group in range(groups):
                    here = high == group
                    for pair in range(pairs):
                        source = table_ref[group * pairs + pair]
                        value = jnp.take_along_axis(source, low, axis=1)
                        picked[pair] = value if group == 0 else jnp.where(here, value, picked[pair])
                found.append(picked)
            for pair in range(pairs):
                both = jnp.concatenate([found[0][pair], found[1][pair]], 0)
                upper = lax.shift_right_arithmetic(both, 16)
                lower = lax.shift_right_arithmetic(lax.shift_left(both, 16), 16)
                place = (pl.ds(first, 16), pl.ds(column, LANES))
                out_ref[2 * pair, place[0], place[1]] = (upper.astype(WIDE) * (1 / FIXED)).astype(NARROW)
                out_ref[2 * pair + 1, place[0], place[1]] = (lower.astype(WIDE) * (1 / FIXED)).astype(NARROW)
        return carry

    lax.fori_loop(0, lanes // LANES, one_tile, 0)


def bias_lookup(table, index):
    heads = table.shape[1]
    pairs = heads // 2
    groups = round_up(table.shape[0], LANES) // LANES
    fixed = jnp.round(table.astype(WIDE) * FIXED).astype(jnp.int32)
    fixed = jnp.pad(fixed, ((0, groups * LANES - table.shape[0]), (0, 0)))
    packed = lax.bitwise_or(
        lax.shift_left(fixed[:, 0::2], 16), lax.bitwise_and(fixed[:, 1::2], 65535)
    )
    packed = jnp.transpose(packed.reshape(groups, LANES, pairs), (0, 2, 1)).reshape(-1, 1, LANES)
    packed = jnp.broadcast_to(packed, (groups * pairs, 8, LANES))
    rows, lanes = index.shape
    step = next(s for s in (32, 16) if rows % s == 0)
    return pl.pallas_call(
        functools.partial(bias_kernel, pairs, groups),
        grid=(rows // step,),
        in_specs=[whole((groups * pairs, 8, LANES)), pl.BlockSpec((step, lanes), lambda i: (i, 0))],
        out_specs=pl.BlockSpec((heads, step, lanes), lambda i: (0, i, 0)),
        out_shape=jax.ShapeDtypeStruct((heads, rows, lanes), NARROW),
        compiler_params=params(32),
        cost_estimate=pl.CostEstimate(
            flops=rows * lanes * groups * pairs * 60, bytes_accessed=rows * lanes * heads * 2, transcendentals=0
        ),
        name="bias_lookup",
    )(packed, index)


def qkv_kernel(x_ref, gain_ref, shift_ref, weight_ref, bias_ref, h_ref, p_ref):
    @pl.when(pl.program_id(0) == 0)
    def _():
        normal, _ = row_norm(x_ref[...].astype(WIDE))
        h_ref[...] = (normal * gain_ref[...] + shift_ref[...]).astype(NARROW)

    product = jnp.dot(h_ref[...], weight_ref[...], preferred_element_type=WIDE)
    p_ref[...] = (product + bias_ref[...]).astype(NARROW)


def qkv_forward(x, gain, shift, weight, bias):
    tokens, width = x.shape
    total = weight.shape[1]
    return pl.pallas_call(
        qkv_kernel,
        grid=(total // width,),
        in_specs=[
            whole((tokens, width)),
            whole((1, width)),
            whole((1, width)),
            pl.BlockSpec((width, width), lambda i: (0, i)),
            pl.BlockSpec((1, width), lambda i: (0, i)),
        ],
        out_specs=[whole((tokens, width)), pl.BlockSpec((tokens, width), lambda i: (0, i))],
        out_shape=[
            jax.ShapeDtypeStruct((tokens, width), NARROW),
            jax.ShapeDtypeStruct((tokens, total), NARROW),
        ],
        compiler_params=params(48),
        cost_estimate=pl.CostEstimate(
            flops=2 * tokens * width * total, bytes_accessed=2 * (tokens + width) * total, transcendentals=0
        ),
        name="qkv_forward",
    )(x, gain, shift, weight, bias)


def head_parts(first_half, value, other):
    return jnp.where(first_half, value, other), jnp.where(first_half, other, value)


def attention_forward_kernel(
    images, q_ref, k_ref, v_ref, mask_ref, large_bias_ref, small_bias_ref, o_ref, large_p_ref, small_p_ref
):
    lane = lax.broadcasted_iota(jnp.int32, (1, LANES), 1)
    first_half = lane < HEAD
    for number, (start, rows) in enumerate(images):
        place = slice(start, start + rows)
        query = q_ref[place, :] * jnp.asarray(HEAD ** (-0.5), NARROW)
        ones = jnp.where(lane % HEAD == 0, 1.0, 0.0).astype(NARROW)
        ones = jnp.broadcast_to(ones, query.shape)
        queries = head_parts(first_half, query, ones)
        keys = head_parts(first_half, k_ref[place, :], mask_ref[place, :])
        value = v_ref[place, :]
        outs = []
        for head in range(2):
            bias = large_bias_ref[head, :, :rows] if number == 0 else small_bias_ref[head, :rows, :rows]
            scores = lax.dot_general(keys[head], queries[head], NT, preferred_element_type=WIDE)
            scores = scores + bias.astype(WIDE)
            weights = jnp.exp(scores - jnp.max(scores, 0, keepdims=True))
            probs = (weights * (1.0 / jnp.sum(weights, 0, keepdims=True))).astype(NARROW)
            if number == 0:
                large_p_ref[head] = probs
            else:
                small_p_ref[head, number - 1] = probs
            outs.append(lax.dot_general(probs, value, TN, preferred_element_type=WIDE))
        o_ref[place, :] = jnp.where(first_half, outs[0], outs[1]).astype(NARROW)


def attention_forward(p, mask, large_bias, small_bias, images):
    tokens = p.shape[0]
    heads = large_bias.shape[0]
    pairs = heads // 2
    large, small, smalls = images[0][1], images[1][1], len(images) - 1
    area = large * large + smalls * small * small

    def column(offset):
        return pl.BlockSpec((tokens, LANES), lambda i: (0, offset + i))

    return pl.pallas_call(
        functools.partial(attention_forward_kernel, images),
        grid=(pairs,),
        in_specs=[
            column(0),
            column(pairs),
            column(2 * pairs),
            whole((tokens, LANES)),
            pl.BlockSpec((2,) + large_bias.shape[1:], lambda i: (i, 0, 0)),
            pl.BlockSpec((2,) + small_bias.shape[1:], lambda i: (i, 0, 0)),
        ],
        out_specs=[
            column(0),
            pl.BlockSpec((2, large, large), lambda i: (i, 0, 0)),
            pl.BlockSpec((2, smalls, small, small), lambda i: (i, 0, 0, 0)),
        ],
        out_shape=[
            jax.ShapeDtypeStruct((tokens, heads * HEAD), NARROW),
            jax.ShapeDtypeStruct((heads, large, large), NARROW),
            jax.ShapeDtypeStruct((heads, smalls, small, small), NARROW),
        ],
        compiler_params=params(48),
        cost_estimate=pl.CostEstimate(
            flops=16 * heads * area * HEAD, bytes_accessed=4 * heads * area, transcendentals=heads * area
        ),
        name="attention_forward",
    )(p, p, p, mask, large_bias, small_bias)


def attention_backward_kernel(
    images, q_ref, k_ref, v_ref, do_ref, o_ref, large_p_ref, small_p_ref, dp_ref, large_ds_ref, small_ds_ref
):
    lane = lax.broadcasted_iota(jnp.int32, (1, LANES), 1)
    first_half = lane < HEAD
    small_sum = [None, None]
    scale = HEAD ** (-0.5)
    for number, (start, rows) in enumerate(images):
        place = slice(start, start + rows)
        query = q_ref[place, :] * jnp.asarray(scale, NARROW)
        key = k_ref[place, :]
        value = v_ref[place, :]
        grad = do_ref[place, :]
        product = jnp.transpose(grad.astype(WIDE) * o_ref[place, :].astype(WIDE))
        grads = head_parts(first_half, grad, jnp.zeros_like(grad))
        parts = []
        for head in range(2):
            inner = jnp.sum(product[head * HEAD : (head + 1) * HEAD], 0, keepdims=True)
            probs = large_p_ref[head] if number == 0 else small_p_ref[head, number - 1]
            grad_probs = lax.dot_general(value, grads[head], NT, preferred_element_type=WIDE)
            grad_scores = (probs.astype(WIDE) * (grad_probs - inner)).astype(NARROW)
            if number == 0:
                large_ds_ref[head, :, :rows] = grad_scores
            elif small_sum[head] is None:
                small_sum[head] = grad_scores.astype(WIDE)
            else:
                small_sum[head] = small_sum[head] + grad_scores.astype(WIDE)
            parts.append(
                (
                    lax.dot_general(grad_scores, key, TN, preferred_element_type=WIDE) * scale,
                    jnp.dot(grad_scores, query, preferred_element_type=WIDE),
                    jnp.dot(probs, grad, preferred_element_type=WIDE),
                )
            )
        for which in range(3):
            dp_ref[which, place, :] = jnp.where(first_half, parts[0][which], parts[1][which]).astype(NARROW)
    large = images[0][1]
    small = images[1][1]
    beyond = large_ds_ref.shape[2] - large
    if beyond:
        large_ds_ref[:, :, large:] = jnp.zeros((2, large, beyond), NARROW)
    small_ds_ref[...] = jnp.zeros(small_ds_ref.shape, NARROW)
    for head in range(2):
        small_ds_ref[head, :small, :small] = small_sum[head].astype(NARROW)


def attention_backward(p, grad_out, out, large_p, small_p, images, large_pad, small_pad):
    tokens = p.shape[0]
    heads = large_p.shape[0]
    pairs = heads // 2
    large, small, smalls = images[0][1], images[1][1], len(images) - 1
    area = large * large + smalls * small * small

    def column(offset):
        return pl.BlockSpec((tokens, LANES), lambda i: (0, offset + i))

    return pl.pallas_call(
        functools.partial(attention_backward_kernel, images),
        grid=(pairs,),
        in_specs=[
            column(0),
            column(pairs),
            column(2 * pairs),
            column(0),
            column(0),
            pl.BlockSpec((2, large, large), lambda i: (i, 0, 0)),
            pl.BlockSpec((2, smalls, small, small), lambda i: (i, 0, 0, 0)),
        ],
        out_specs=[
            pl.BlockSpec((3, tokens, LANES), lambda i: (0, 0, i)),
            pl.BlockSpec((2,) + large_pad, lambda i: (i, 0, 0)),
            pl.BlockSpec((2,) + small_pad, lambda i: (i, 0, 0)),
        ],
        out_shape=[
            jax.ShapeDtypeStruct((3, tokens, heads * HEAD), NARROW),
            jax.ShapeDtypeStruct((heads,) + large_pad, NARROW),
            jax.ShapeDtypeStruct((heads,) + small_pad, NARROW),
        ],
        compiler_params=params(48),
        cost_estimate=pl.CostEstimate(
            flops=32 * heads * area * HEAD, bytes_accessed=4 * heads * area, transcendentals=0
        ),
        name="attention_backward",
    )(p, p, p, grad_out, out, large_p, small_p)


def gelu_parts(value):
    size = jnp.abs(value)
    inverse = 1.0 / (1.0 + (0.3275911 * 0.7071067811865476) * size)
    series = inverse * (
        0.127414796
        + inverse
        * (-0.142248368 + inverse * (0.7107068705 + inverse * (-0.7265760135 + inverse * 0.5307027145)))
    )
    bell = jnp.exp(-0.5 * value * value)
    tail = series * bell
    share = jnp.where(value < 0, tail, 1.0 - tail)
    return value * share, share + value * (bell * 0.3989422804014327)


def mlp_kernel(
    o_ref,
    x_ref,
    dy_ref,
    proj_ref,
    vector_ref,
    inner_ref,
    inner_bias_ref,
    outer_ref,
    result_ref,
    dm_ref,
    do_ref,
    dinner_ref,
    douter_ref,
    dproj_ref,
    dvector_ref,
    dbias_ref,
    r_ref,
    g_ref,
    dz_ref,
    z_ref,
    dg_ref,
):
    step = pl.program_id(0)
    proj_bias, attn_scale, gain, shift, outer_bias, mlp_scale = (vector_ref[i : i + 1, :] for i in range(6))
    tokens = x_ref.shape[0]
    chunk = next(c for c in (128, 64, 32, 16) if tokens % c == 0)

    @pl.when(step == 0)
    def _():
        r_ref[...] = jnp.dot(o_ref[...], proj_ref[...], preferred_element_type=WIDE) + proj_bias

        @pl.loop(0, tokens // chunk)
        def _(i):
            rows = pl.ds(pl.multiple_of(i * chunk, chunk), chunk)
            middle = x_ref[rows, :].astype(WIDE) + attn_scale * r_ref[rows, :]
            normal, _ = row_norm(middle)
            g_ref[rows, :] = (normal * gain + shift).astype(NARROW)
            dz_ref[rows, :] = (mlp_scale * dy_ref[rows, :].astype(WIDE)).astype(NARROW)

    pre = jnp.dot(g_ref[...], inner_ref[...], preferred_element_type=WIDE) + inner_bias_ref[...]
    active, slope = gelu_parts(pre)
    active = active.astype(NARROW)
    dz = dz_ref[...]
    dactive = lax.dot_general(dz, outer_ref[...], NT, preferred_element_type=WIDE)
    dpre = (dactive * slope).astype(NARROW)
    douter_ref[...] = lax.dot_general(active, dz, TN, preferred_element_type=WIDE).astype(NARROW)
    dinner_ref[...] = lax.dot_general(g_ref[...], dpre, TN, preferred_element_type=WIDE).astype(NARROW)
    dbias_ref[...] = jnp.sum(dpre.astype(WIDE), 0, keepdims=True)
    z = jnp.dot(active, outer_ref[...], preferred_element_type=WIDE)
    dg = lax.dot_general(dpre, inner_ref[...], NT, preferred_element_type=WIDE)

    @pl.when(step == 0)
    def _():
        z_ref[...] = z
        dg_ref[...] = dg

    @pl.when(step > 0)
    def _():
        z_ref[...] += z
        dg_ref[...] += dg

    @pl.when(step == pl.num_programs(0) - 1)
    def _():
        dvector_ref[...] = jnp.zeros_like(dvector_ref)

        @pl.loop(0, tokens // chunk)
        def _(i):
            rows = pl.ds(pl.multiple_of(i * chunk, chunk), chunk)
            branch = r_ref[rows, :]
            middle = x_ref[rows, :].astype(WIDE) + attn_scale * branch
            normal, inverse = row_norm(middle)
            outer = z_ref[rows, :] + outer_bias
            dy = dy_ref[rows, :].astype(WIDE)
            result_ref[rows, :] = (middle + mlp_scale * outer).astype(NARROW)
            grad = dg_ref[rows, :]
            dm = dy + norm_backward(grad, normal, inverse, gain)
            dm_ref[rows, :] = dm
            dr = (attn_scale * dm).astype(NARROW)
            g_ref[rows, :] = dr
            sums = [
                dy * outer,
                dz_ref[rows, :].astype(WIDE),
                grad * normal,
                grad,
                dm * branch,
                dr.astype(WIDE),
            ]
            for place, term in enumerate(sums):
                dvector_ref[place : place + 1, :] += jnp.sum(term, 0, keepdims=True)

        dr = g_ref[...]
        dproj_ref[...] = lax.dot_general(o_ref[...], dr, TN, preferred_element_type=WIDE).astype(NARROW)
        do_ref[...] = lax.dot_general(dr, proj_ref[...], NT, preferred_element_type=WIDE).astype(NARROW)


def mlp_pass(out, x, dy, proj, vectors, inner, inner_bias, outer):
    tokens, width = x.shape
    hidden = inner.shape[1]
    block = next(b for b in (512, 256, 128) if hidden % b == 0)
    return pl.pallas_call(
        mlp_kernel,
        grid=(hidden // block,),
        in_specs=[
            whole((tokens, width)),
            whole((tokens, width)),
            whole((tokens, width)),
            whole((width, width)),
            whole((8, width)),
            pl.BlockSpec((width, block), lambda i: (0, i)),
            pl.BlockSpec((1, block), lambda i: (0, i)),
            pl.BlockSpec((block, width), lambda i: (i, 0)),
        ],
        out_specs=[
            whole((tokens, width)),
            whole((tokens, width)),
            whole((tokens, width)),
            pl.BlockSpec((width, block), lambda i: (0, i)),
            pl.BlockSpec((block, width), lambda i: (i, 0)),
            whole((width, width)),
            whole((8, width)),
            pl.BlockSpec((1, block), lambda i: (0, i)),
        ],
        out_shape=[
            jax.ShapeDtypeStruct((tokens, width), NARROW),
            jax.ShapeDtypeStruct((tokens, width), WIDE),
            jax.ShapeDtypeStruct((tokens, width), NARROW),
            jax.ShapeDtypeStruct((width, hidden), NARROW),
            jax.ShapeDtypeStruct((hidden, width), NARROW),
            jax.ShapeDtypeStruct((width, width), NARROW),
            jax.ShapeDtypeStruct((8, width), WIDE),
            jax.ShapeDtypeStruct((1, hidden), WIDE),
        ],
        scratch_shapes=[
            pltpu.VMEM((tokens, width), WIDE),
            pltpu.VMEM((tokens, width), NARROW),
            pltpu.VMEM((tokens, width), NARROW),
            pltpu.VMEM((tokens, width), WIDE),
            pltpu.VMEM((tokens, width), WIDE),
        ],
        compiler_params=params(60),
        cost_estimate=pl.CostEstimate(
            flops=12 * tokens * width * hidden, bytes_accessed=8 * hidden * width, transcendentals=tokens * hidden
        ),
        name="mlp_pass",
    )(out, x, dy, proj, vectors, inner, inner_bias, outer)


def qkv_backward_kernel(dp_ref, h_ref, x_ref, dm_ref, gain_ref, weight_ref, dweight_ref, dx_ref, dvector_ref, dh_ref):
    step = pl.program_id(0)
    grad = dp_ref[0]
    dweight_ref[0] = lax.dot_general(h_ref[...], grad, TN, preferred_element_type=WIDE).astype(NARROW)
    term = lax.dot_general(grad, weight_ref[...], NT, preferred_element_type=WIDE)
    column_sum = jnp.sum(grad.astype(WIDE), 0, keepdims=True)
    tokens = x_ref.shape[0]
    chunk = next(c for c in (128, 64, 32, 16) if tokens % c == 0)

    @pl.when(step == 0)
    def _():
        dvector_ref[...] = jnp.zeros_like(dvector_ref)
        dh_ref[...] = term
        dvector_ref[0:1, :] = column_sum

    @pl.when(step > 0)
    def _():
        dh_ref[...] += term

    @pl.when(step == pl.num_programs(0) - 1)
    def _():
        dvector_ref[1:2, :] = column_sum

        @pl.loop(0, tokens // chunk)
        def _(i):
            rows = pl.ds(pl.multiple_of(i * chunk, chunk), chunk)
            normal, inverse = row_norm(x_ref[rows, :].astype(WIDE))
            dh = dh_ref[rows, :]
            dx = dm_ref[rows, :] + norm_backward(dh, normal, inverse, gain_ref[...])
            dx_ref[rows, :] = dx.astype(NARROW)
            dvector_ref[2:3, :] += jnp.sum(dh * normal, 0, keepdims=True)
            dvector_ref[3:4, :] += jnp.sum(dh, 0, keepdims=True)


def qkv_backward(dp, h, x, dm, gain, weight):
    tokens, width = x.shape
    return pl.pallas_call(
        qkv_backward_kernel,
        grid=(3,),
        in_specs=[
            pl.BlockSpec((1, tokens, width), lambda i: (i, 0, 0)),
            whole((tokens, width)),
            whole((tokens, width)),
            whole((tokens, width)),
            whole((1, width)),
            pl.BlockSpec((width, width), lambda i: (0, i)),
        ],
        out_specs=[
            pl.BlockSpec((1, width, width), lambda i: (i, 0, 0)),
            whole((tokens, width)),
            whole((8, width)),
        ],
        out_shape=[
            jax.ShapeDtypeStruct((3, width, width), NARROW),
            jax.ShapeDtypeStruct((tokens, width), NARROW),
            jax.ShapeDtypeStruct((8, width), WIDE),
        ],
        scratch_shapes=[pltpu.VMEM((tokens, width), WIDE)],
        compiler_params=params(48),
        cost_estimate=pl.CostEstimate(
            flops=12 * tokens * width * width, bytes_accessed=20 * tokens * width, transcendentals=0
        ),
        name="qkv_backward",
    )(dp, h, x, dm, gain, weight)


def table_kernel(heads, groups, batch, own_ref, other_ref, index_ref, out_ref, turned_ref, left_ref, right_ref):
    @pl.when(pl.program_id(0) == 0)
    def _():
        out_ref[...] = jnp.zeros_like(out_ref)
        turned_ref[...] = jnp.zeros_like(turned_ref)

    rows, lanes = index_ref.shape
    for head in range(heads):
        turned_ref[:, head, :] = own_ref[head].astype(WIDE) + other_ref[head].astype(WIDE)
    zero = jnp.zeros((), NARROW)
    one = jnp.ones((), NARROW)
    codes = lax.broadcasted_iota(jnp.int32, (LANES, LANES), 0).astype(WIDE).astype(NARROW)

    def some_rows(part, carry):
        for within in range(batch):
            row = part * batch + within
            index = index_ref[pl.ds(row, 1), :]
            low = lax.bitwise_and(index, LANES - 1).astype(WIDE).astype(NARROW)
            high = lax.shift_right_logical(index, 7).astype(WIDE).astype(NARROW)
            for first in range(0, lanes, LANES):
                here = slice(first, first + LANES)
                there = slice(within * lanes + first, within * lanes + first + LANES)
                right_ref[:, there] = jnp.where(codes == low[:, here], one, zero)
                value = turned_ref[row, :, here].astype(NARROW)
                wide_high = jnp.broadcast_to(high[:, here], value.shape)
                for group in range(groups):
                    left_ref[group * 16 : group * 16 + 16, there] = jnp.where(
                        wide_high == jnp.asarray(group, NARROW), value, zero
                    )
        out_ref[...] += lax.dot_general(left_ref[...], right_ref[...], NT, preferred_element_type=WIDE)
        return carry

    lax.fori_loop(0, rows // batch, some_rows, 0)


def table_gradient_sum(own, other, index, table_rows):
    heads, rows, lanes = own.shape
    groups = round_up(table_rows, LANES) // LANES
    batch = 4
    step = 16
    return pl.pallas_call(
        functools.partial(table_kernel, heads, groups, batch),
        grid=(rows // step,),
        in_specs=[
            pl.BlockSpec((heads, step, lanes), lambda i: (0, i, 0)),
            pl.BlockSpec((heads, step, lanes), lambda i: (0, i, 0)),
            pl.BlockSpec((step, lanes), lambda i: (i, 0)),
        ],
        out_specs=whole((groups * 16, LANES)),
        out_shape=jax.ShapeDtypeStruct((groups * 16, LANES), WIDE),
        scratch_shapes=[
            pltpu.VMEM((step, 16, lanes), WIDE),
            pltpu.VMEM((groups * 16, batch * lanes), NARROW),
            pltpu.VMEM((LANES, batch * lanes), NARROW),
        ],
        compiler_params=params(48),
        cost_estimate=pl.CostEstimate(
            flops=rows * lanes * 200 * 1000, bytes_accessed=4 * heads * rows * lanes, transcendentals=0
        ),
        name="table_gradient",
    )(own, other, index)


def rotate(value, axis, size, shift):
    return lax.ppermute(value, axis, [(i, (i + shift) % size) for i in range(size)])


def swap_bit(value, size, bit):
    return lax.ppermute(value, "img", [(i, i ^ (1 << bit)) for i in range(size)])


def exchange_images(pieces, size):
    me = lax.axis_index("blk")
    held = jnp.zeros_like(pieces)
    held = lax.dynamic_update_index_in_dim(held, lax.dynamic_index_in_dim(pieces, me, 0, False), me, 0)
    for shift in range(1, size):
        target = lax.rem(me + shift, size)
        source = lax.rem(me + size - shift, size)
        got = rotate(lax.dynamic_index_in_dim(pieces, target, 0, False), "blk", size, shift)
        held = lax.dynamic_update_index_in_dim(held, got, source, 0)
    return held


def halve(value, size, bit, position):
    mine = lax.rem(lax.div(lax.axis_index("img"), 1 << bit), 2)
    keep = lax.dynamic_index_in_dim(value, mine, position, False)
    send = lax.dynamic_index_in_dim(value, 1 - mine, position, False)
    got = swap_bit(send, size, bit)
    return (keep.astype(WIDE) + got.astype(WIDE)).astype(NARROW)


def scatter_sum(values, img, blk):
    bits = img.bit_length() - 1
    parts = []
    for number, value in enumerate(values):
        value = value.reshape((2,) * bits + (blk,) + value.shape[1:])
        order = list(range(bits))
        if number % 2 and bits > 2:
            order = order[:1] + order[:0:-1]
        left = list(range(bits))
        for bit in order:
            value = halve(value, img, bit, len(left) - 1 - left.index(bit))
            left.remove(bit)
        parts.append(value)
    joined = jnp.concatenate(parts, 1)
    me = lax.axis_index("blk")
    total = lax.dynamic_index_in_dim(joined, me, 0, False).astype(WIDE)
    for shift in range(1, blk):
        target = lax.rem(me + shift, blk)
        got = rotate(lax.dynamic_index_in_dim(joined, target, 0, False), "blk", blk, shift)
        total = total + got.astype(WIDE)
    outs = []
    first = 0
    for value in parts:
        outs.append(total[first : first + value.shape[1]])
        first += value.shape[1]
    return outs


def sum_all(value, img, blk):
    for bit in range(img.bit_length() - 1):
        value = value + swap_bit(value, img, bit)
    bit = 1
    while bit < blk:
        value = value + lax.ppermute(value, "blk", [(i, i ^ bit) for i in range(blk)])
        bit *= 2
    return value


def image_on_device(
    img,
    blk,
    images_large,
    images_small,
    cotan_large,
    cotan_small,
    lengths_large,
    lengths_small,
    index_large,
    index_small,
    attn_gain,
    attn_shift,
    qkv_weight,
    query_bias,
    value_bias,
    table_large,
    table_small,
    proj_weight,
    proj_bias,
    attn_scale,
    mlp_gain,
    mlp_shift,
    inner_weight,
    inner_bias,
    outer_weight,
    outer_bias,
    mlp_scale,
):
    width = attn_gain.shape[0]
    heads = table_large.shape[1]
    hidden = inner_bias.shape[0]
    rows = images_large.shape[1]
    smalls, small_rows = images_small.shape[:2]
    part = round_up(rows, 8)
    while part * blk % 16:
        part += 8
    large = part * blk
    small = round_up(small_rows, 16)
    tokens = large + smalls * small
    images = ((0, large),) + tuple((large + i * small, small) for i in range(smalls))
    lanes_large = round_up(large, LANES)
    lanes_small = round_up(small, LANES)
    double = round_up(small, 32)
    blk_me = lax.axis_index("blk")
    core = lax.rem(lax.axis_index("img"), 2)

    def gather_tokens(large_pieces, small_pieces):
        padded = jnp.pad(large_pieces, ((0, 0), (0, part - rows), (0, 0)))
        moved = exchange_images(padded, blk).reshape(large, width)
        still = jnp.pad(small_pieces, ((0, 0), (0, small - small_rows), (0, 0)))
        return jnp.concatenate([moved, still.reshape(smalls * small, width)], 0)

    def return_tokens(values):
        moved = exchange_images(values[:large].reshape(blk, part, width), blk)
        still = values[large:].reshape(smalls, small, width)
        return moved[:, :rows], still[:, :small_rows]

    def spread_index(index, length, pieces, piece, lanes):
        turned = jnp.transpose(index).reshape(pieces, length, pieces, length)
        turned = jnp.pad(turned, ((0, 0), (0, piece - length), (0, 0), (0, piece - length)))
        turned = turned.reshape(pieces * piece, pieces * piece)
        return jnp.pad(turned, ((0, 0), (0, lanes - pieces * piece)))

    x = gather_tokens(images_large, images_small)
    dy = gather_tokens(cotan_large, cotan_small)
    spread_large = spread_index(index_large, rows, blk, part, lanes_large)
    spread_small = spread_index(index_small, small_rows, 1, small, lanes_small)

    half = heads // 2
    large_half = bias_lookup(lax.dynamic_slice_in_dim(table_large, core * half, half, 1), spread_large)
    other_half = swap_bit(large_half, img, 0)
    is_first = core == 0
    large_bias = jnp.concatenate(
        [jnp.where(is_first, large_half, other_half), jnp.where(is_first, other_half, large_half)], 0
    )
    small_bias = bias_lookup(table_small, spread_small)

    place = jnp.arange(large, dtype=jnp.int32)
    own_length = lax.dynamic_index_in_dim(lengths_large, blk_me, 0, False)
    inside = (place % part < rows) & (place // part * rows + place % part < own_length)
    small_place = jnp.arange(small, dtype=jnp.int32)
    small_inside = (small_place[None, :] < lengths_small[:, None]).reshape(-1)
    mask = jnp.where(jnp.concatenate([inside, small_inside]), 0.0, NEGATIVE).astype(NARROW)
    mask = jnp.broadcast_to(mask[:, None], (tokens, LANES))

    def row(vector):
        return vector.astype(WIDE)[None, :]

    bias_row = row(jnp.concatenate([query_bias, jnp.zeros_like(query_bias), value_bias]))
    h, p = qkv_forward(x, row(attn_gain), row(attn_shift), qkv_weight, bias_row)
    out, large_p, small_p = attention_forward(p, mask, large_bias, small_bias, images)
    zeros = jnp.zeros_like(proj_bias)
    vectors = jnp.stack(
        [proj_bias, attn_scale, mlp_gain, mlp_shift, outer_bias, mlp_scale, zeros, zeros]
    ).astype(WIDE)
    result, dm, grad_out, dinner, douter, dproj, mlp_sums, dinner_bias = mlp_pass(
        out, x, dy, proj_weight, vectors, inner_weight, row(inner_bias), outer_weight
    )
    result_large, result_small = return_tokens(result)
    devices = img * blk
    outer_sum, inner_sum = scatter_sum(
        [
            douter.reshape(devices, hidden // devices, width),
            dinner.reshape(devices, width // devices, hidden).reshape(devices, hidden // devices, width),
        ],
        img,
        blk,
    )
    dp, large_ds, small_ds = attention_backward(
        p, grad_out, out, large_p, small_p, images, (large, lanes_large), (double, lanes_small)
    )
    dqkv, dx, qkv_sums = qkv_backward(dp, h, x, dm, row(attn_gain), qkv_weight)
    grad_large, grad_small = return_tokens(dx)
    pieces = [value.reshape(devices, width // devices, width) for value in (dqkv[0], dqkv[1], dqkv[2], dproj)]
    first_sum, second_sum = scatter_sum(
        [jnp.concatenate(pieces[:2], 1), jnp.concatenate(pieces[2:], 1)], img, blk
    )

    def core_share(value, axis, which):
        size = value.shape[axis] // 2
        return lax.dynamic_slice_in_dim(value, which * size, size, axis)

    tables = []
    for grad, index, table in ((large_ds, spread_large, table_large), (small_ds, spread_small, table_small)):
        if index.shape[0] < grad.shape[1]:
            index = jnp.pad(index, ((0, grad.shape[1] - index.shape[0]), (0, 0)))
        other = swap_bit(core_share(grad, 1, 1 - core), img, 0)
        tables.append(
            table_gradient_sum(core_share(grad, 1, core), other, core_share(index, 0, core), table.shape[0])
        )
    sums = jnp.concatenate([mlp_sums[:6], qkv_sums[:4], dinner_bias.reshape(-1, width)], 0)
    joined = jnp.concatenate(tables + [sums.reshape(-1, LANES)], 0)
    joined = sum_all(joined, img, blk)
    outs = []
    first = 0
    for table, total in ((table_large, tables[0]), (table_small, tables[1])):
        value = joined[first : first + total.shape[0]].reshape(-1, 16, LANES)[:, :heads]
        outs.append(jnp.transpose(value, (0, 2, 1)).reshape(-1, heads)[: table.shape[0]])
        first += total.shape[0]
    sums = joined[first:].reshape(-1)
    me = lax.axis_index("img") * blk + blk_me
    share = width // devices

    def own(place, length=1):
        return lax.dynamic_slice_in_dim(sums, place * width + me * share * length, share * length, 0)

    return (
        result_large,
        result_small,
        grad_large,
        grad_small,
        own(8),
        own(9),
        jnp.concatenate([first_sum[:share], first_sum[share:], second_sum[:share]], 1),
        own(6),
        own(7),
        outs[0],
        outs[1],
        second_sum[share:],
        own(5),
        own(4),
        own(2),
        own(3),
        inner_sum.reshape(share, hidden),
        own(10, hidden // width),
        outer_sum,
        own(1),
        own(0),
    )


def solution(mesh):
    img, blk = mesh.shape["img"], mesh.shape["blk"]

    def by_device(*args):
        if args[0].shape[0] == blk:
            return image_on_device(img, blk, *args)
        return on_device(*args)

    return jax.shard_map(
        by_device,
        mesh=mesh,
        in_specs=(
            P("img", "blk", None),
            P(("img", "blk"), None, None),
            P("img", "blk", None),
            P(("img", "blk"), None, None),
            P("img"),
            P(("img", "blk")),
            P(),
            P(),
            P(),
            P(),
            P(),
            P(),
            P(),
            P(),
            P(),
            P(),
            P(),
            P(),
            P(),
            P(),
            P(),
            P(),
            P(),
            P(),
            P(),
        ),
        out_specs=(
            P("img", "blk", None),
            P(("img", "blk"), None, None),
            P("img", "blk", None),
            P(("img", "blk"), None, None),
            P(("img", "blk")),
            P(("img", "blk")),
            P(("img", "blk"), None),
            P(("img", "blk")),
            P(("img", "blk")),
            P(),
            P(),
            P(("img", "blk"), None),
            P(("img", "blk")),
            P(("img", "blk")),
            P(("img", "blk")),
            P(("img", "blk")),
            P(("img", "blk"), None),
            P(("img", "blk")),
            P(("img", "blk"), None),
            P(("img", "blk")),
            P(("img", "blk")),
        ),
        check_vma=False,
    )
```

```python
import functools

import jax
import jax.numpy as jnp
from jax import lax
from jax.experimental import pallas as pl
from jax.experimental.pallas import tpu as pltpu
from jax.sharding import PartitionSpec as P

HEAD = 64


NEGATIVE = -1e30
EPSILON = 1e-06
HIGHEST = lax.Precision.HIGHEST


def layer_norm(values, gain, shift):
    center = values - jnp.mean(values, -1, keepdims=True)
    spread = jnp.mean(center * center, -1, keepdims=True)
    return center * lax.rsqrt(spread + EPSILON) * gain + shift


def exact_gelu(values):
    return jax.nn.gelu(values, approximate=False)


def lookup(table, index_block):
    table_codes = jnp.arange(table.shape[0], dtype=jnp.int32)

    def lookup_one_query(index_row):
        selector = (index_row[:, None] == table_codes[None, :]).astype(jnp.bfloat16)
        return jnp.dot(selector, table, preferred_element_type=jnp.float32)

    picked = lax.map(lookup_one_query, index_block, batch_size=8)
    return jnp.transpose(picked, (2, 0, 1))


def table_gradient(grad_full, index_block, table_rows):
    table_codes = jnp.arange(table_rows, dtype=jnp.int32)

    def table_one_query(item):
        index_row, grad_row = item
        selector = (index_row[:, None] == table_codes[None, :]).astype(jnp.float32)
        return jnp.dot(selector.T, grad_row, precision=HIGHEST, preferred_element_type=jnp.float32)

    partials = lax.map(
        table_one_query, (index_block, jnp.transpose(grad_full, (1, 2, 0))), batch_size=8
    )
    return jnp.sum(partials, 0)


def key_mask(lengths, first, count):
    places = first + jnp.arange(count, dtype=jnp.int32)
    return (places[None, :] < lengths[:, None])[:, None, None, :]


def block_scores(queries, key_piece, bias_rows, lengths, first):
    count = key_piece.shape[1]
    scores = jnp.einsum(
        "iqhe,ikhe->ihqk", queries, key_piece, preferred_element_type=jnp.float32
    ) * HEAD ** (-0.5)
    scores = scores + lax.dynamic_slice_in_dim(bias_rows, first, count, 2)[None]
    return (scores, key_mask(lengths, first, count))


def merge_heads(values):
    return jnp.transpose(values, (0, 2, 1, 3)).reshape(-1, values.shape[1] * values.shape[3])


def local_fold(pieces):

    def visit(step, state):
        return step(state, pieces, 0)

    return visit


def forward_attention(queries, bias_rows, lengths, visit):
    images, rows, heads, width = queries.shape

    def absorb(state, pieces, first):
        top, total, summed = state
        key_piece, value_piece = pieces
        scores, valid = block_scores(queries, key_piece, bias_rows, lengths, first)
        scores = jnp.where(valid, scores, NEGATIVE)
        new_top = jnp.maximum(top, jnp.max(scores, -1))
        weights = jnp.where(valid, jnp.exp(scores - new_top[..., None]), 0.0)
        factor = jnp.exp(top - new_top)
        total = total * factor + jnp.sum(weights, -1)
        update = jnp.einsum(
            "ihqk,ikhe->ihqe", weights, value_piece.astype(jnp.float32), precision=HIGHEST
        )
        return (new_top, total, summed * factor[..., None] + update)

    start_state = (
        jnp.full((images, heads, rows), NEGATIVE, jnp.float32),
        jnp.zeros((images, heads, rows), jnp.float32),
        jnp.zeros((images, heads, rows, width), jnp.float32),
    )
    top, total, summed = visit(absorb, start_state)
    return (summed / total[..., None], top + jnp.log(total))


def key_pass(queries, bias_rows, lengths, grad_out, inner, log_total, visit):
    images, rows, heads, width = queries.shape
    length = bias_rows.shape[2]
    grad_wide = grad_out.astype(jnp.float32)

    def collect(state, pieces, first):
        key_piece, value_piece = pieces
        scores, valid = block_scores(queries, key_piece, bias_rows, lengths, first)
        probs = jnp.where(valid, jnp.exp(scores - log_total[..., None]), 0.0)
        grad_probs = jnp.einsum(
            "iqhe,ikhe->ihqk", grad_out, value_piece, preferred_element_type=jnp.float32
        )
        grad_scores = (probs * (grad_probs - inner[..., None])).astype(jnp.bfloat16)
        grad_query = state[0] + jnp.einsum(
            "ihqk,ikhe->ihqe", grad_scores, key_piece, preferred_element_type=jnp.float32
        ) * HEAD ** (-0.5)
        bias_full = lax.dynamic_update_slice_in_dim(
            state[1], jnp.sum(grad_scores.astype(jnp.float32), 0), first, 2
        )
        key_part = jnp.einsum(
            "ihqk,iqhe->ikhe", grad_scores, queries, preferred_element_type=jnp.float32
        ) * HEAD ** (-0.5)
        value_part = jnp.einsum("ihqk,iqhe->ikhe", probs, grad_wide, precision=HIGHEST)
        key_full = lax.dynamic_update_slice_in_dim(state[2], key_part, first, 1)
        value_full = lax.dynamic_update_slice_in_dim(state[3], value_part, first, 1)
        return (grad_query, bias_full, key_full, value_full)

    start_state = (
        jnp.zeros((images, heads, rows, width), jnp.float32),
        jnp.zeros((heads, rows, length), jnp.float32),
    )
    start_state = start_state + (
        jnp.zeros((images, length, heads, width), jnp.float32),
        jnp.zeros((images, length, heads, width), jnp.float32),
    )
    return visit(collect, start_state)


def on_device(
    images_large,
    images_small,
    cotan_large,
    cotan_small,
    lengths_large,
    lengths_small,
    index_large,
    index_small,
    attn_gain,
    attn_shift,
    qkv_weight,
    query_bias,
    value_bias,
    table_large,
    table_small,
    proj_weight,
    proj_bias,
    attn_scale,
    mlp_gain,
    mlp_shift,
    inner_weight,
    inner_bias,
    outer_weight,
    outer_bias,
    mlp_scale,
):
    wide = jnp.float32
    narrow = jnp.bfloat16
    width = attn_gain.shape[0]
    heads = table_large.shape[1]
    large_count, large_rows = (images_large.shape[0], images_large.shape[1])
    small_count, small_rows = (images_small.shape[0], images_small.shape[1])
    split_at = large_count * large_rows
    first_key = lax.axis_index("blk") * large_rows
    flat = jnp.concatenate(
        [images_large.reshape(-1, width), images_small.reshape(-1, width)], 0
    ).astype(wide)
    normed, attn_norm_back = jax.vjp(
        layer_norm, flat, attn_gain.astype(wide), attn_shift.astype(wide)
    )
    normed_low = normed.astype(narrow)
    bias_vector = jnp.concatenate(
        [query_bias.astype(wide), jnp.zeros((width,), wide), value_bias.astype(wide)]
    )
    projected = (jnp.dot(normed_low, qkv_weight, preferred_element_type=wide) + bias_vector).astype(
        narrow
    )
    large_parts = projected[:split_at].reshape(large_count, large_rows, 3, heads, -1)
    large_query, large_key, large_value = (
        large_parts[:, :, 0],
        large_parts[:, :, 1],
        large_parts[:, :, 2],
    )
    large_index = lax.dynamic_slice_in_dim(index_large, first_key, large_rows, 0)
    large_bias = lookup(table_large, large_index)

    def forward_visit(step, state):
        return step(
            state,
            (
                lax.all_gather(large_key, "blk", axis=1, tiled=True),
                lax.all_gather(large_value, "blk", axis=1, tiled=True),
            ),
            jnp.int32(0),
        )

    def backward_visit(step, state):
        return step(
            state,
            (
                lax.all_gather(large_key, "blk", axis=1, tiled=True),
                lax.all_gather(large_value, "blk", axis=1, tiled=True),
            ),
            jnp.int32(0),
        )

    large_attended, large_log = forward_attention(
        large_query, large_bias, lengths_large, forward_visit
    )
    small_parts = projected[split_at:].reshape(small_count, small_rows, 3, heads, -1)
    small_query, small_key, small_value = (
        small_parts[:, :, 0],
        small_parts[:, :, 1],
        small_parts[:, :, 2],
    )
    small_bias = lookup(table_small, index_small)
    small_visit = local_fold((small_key, small_value))
    small_attended, small_log = forward_attention(
        small_query, small_bias, lengths_small, small_visit
    )
    attended_low = jnp.concatenate(
        [merge_heads(large_attended), merge_heads(small_attended)], 0
    ).astype(narrow)
    branch = jnp.dot(attended_low, proj_weight, preferred_element_type=wide) + proj_bias.astype(
        wide
    )
    middle = flat + attn_scale.astype(wide) * branch
    normed_mlp, mlp_norm_back = jax.vjp(
        layer_norm, middle, mlp_gain.astype(wide), mlp_shift.astype(wide)
    )
    normed_mlp_low = normed_mlp.astype(narrow)
    pre_act = jnp.dot(
        normed_mlp_low, inner_weight, preferred_element_type=wide
    ) + inner_bias.astype(wide)
    activated, gelu_back = jax.vjp(exact_gelu, pre_act)
    activated_low = activated.astype(narrow)
    outer = jnp.dot(activated_low, outer_weight, preferred_element_type=wide) + outer_bias.astype(
        wide
    )
    result_low = (middle + mlp_scale.astype(wide) * outer).astype(narrow)
    cotan = jnp.concatenate(
        [cotan_large.reshape(-1, width), cotan_small.reshape(-1, width)], 0
    ).astype(wide)
    grad_mlp_scale = jnp.sum(cotan * outer, 0)
    grad_outer = (mlp_scale.astype(wide) * cotan).astype(narrow)
    grad_outer_bias = jnp.sum(grad_outer.astype(wide), 0)
    grad_outer_weight = jnp.dot(activated_low.T, grad_outer, preferred_element_type=wide)
    grad_activated = jnp.dot(grad_outer, outer_weight.T, preferred_element_type=wide)
    grad_pre = gelu_back(grad_activated)[0].astype(narrow)
    grad_inner_bias = jnp.sum(grad_pre.astype(wide), 0)
    grad_inner_weight = jnp.dot(normed_mlp_low.T, grad_pre, preferred_element_type=wide)
    grad_normed_mlp = jnp.dot(grad_pre, inner_weight.T, preferred_element_type=wide)
    grad_middle_part, grad_mlp_gain, grad_mlp_shift = mlp_norm_back(grad_normed_mlp)
    grad_middle = cotan + grad_middle_part
    grad_attn_scale = jnp.sum(grad_middle * branch, 0)
    grad_branch = (attn_scale.astype(wide) * grad_middle).astype(narrow)
    grad_proj_bias = jnp.sum(grad_branch.astype(wide), 0)
    grad_proj_weight = jnp.dot(attended_low.T, grad_branch, preferred_element_type=wide)
    grad_attended = jnp.dot(grad_branch, proj_weight.T, preferred_element_type=wide).astype(narrow)
    large_grad_out = grad_attended[:split_at].reshape(large_count, large_rows, heads, -1)
    large_inner = jnp.einsum("iqhe,ihqe->ihq", large_grad_out.astype(wide), large_attended)
    large_grad_query, large_bias_full, key_full, value_full = key_pass(
        large_query,
        large_bias,
        lengths_large,
        large_grad_out,
        large_inner,
        large_log,
        backward_visit,
    )
    large_key_grad, large_value_grad = (
        lax.psum_scatter(
            key_full.astype(jnp.bfloat16), "blk", scatter_dimension=1, tiled=True
        ).astype(jnp.float32),
        lax.psum_scatter(
            value_full.astype(jnp.bfloat16), "blk", scatter_dimension=1, tiled=True
        ).astype(jnp.float32),
    )
    large_grads = jnp.stack(
        [jnp.transpose(large_grad_query, (0, 2, 1, 3)), large_key_grad, large_value_grad], 2
    ).reshape(split_at, 3 * width)
    large_table_grad = table_gradient(large_bias_full, large_index, table_large.shape[0])
    small_grad_out = grad_attended[split_at:].reshape(small_count, small_rows, heads, -1)
    small_inner = jnp.einsum("iqhe,ihqe->ihq", small_grad_out.astype(wide), small_attended)
    small_grad_query, small_bias_full, small_key_grad, small_value_grad = key_pass(
        small_query, small_bias, lengths_small, small_grad_out, small_inner, small_log, small_visit
    )
    small_grads = jnp.stack(
        [jnp.transpose(small_grad_query, (0, 2, 1, 3)), small_key_grad, small_value_grad], 2
    ).reshape(small_count * small_rows, 3 * width)
    small_table_grad = table_gradient(small_bias_full, index_small, table_small.shape[0])
    grad_projected = jnp.concatenate([large_grads, small_grads], 0).astype(narrow)
    grad_query_bias = jnp.sum(grad_projected[:, :width].astype(wide), 0)
    grad_value_bias = jnp.sum(grad_projected[:, 2 * width :].astype(wide), 0)
    grad_qkv_weight = jnp.dot(normed_low.T, grad_projected, preferred_element_type=wide)
    grad_normed = jnp.dot(grad_projected, qkv_weight.T, preferred_element_type=wide)
    grad_flat_part, grad_attn_gain, grad_attn_shift = attn_norm_back(grad_normed)
    grad_flat = (grad_middle + grad_flat_part).astype(narrow)
    summed = (
        lax.psum_scatter(grad_attn_gain, ("img", "blk"), scatter_dimension=0, tiled=True),
        lax.psum_scatter(grad_attn_shift, ("img", "blk"), scatter_dimension=0, tiled=True),
        lax.psum_scatter(grad_qkv_weight, ("img", "blk"), scatter_dimension=0, tiled=True),
        lax.psum_scatter(grad_query_bias, ("img", "blk"), scatter_dimension=0, tiled=True),
        lax.psum_scatter(grad_value_bias, ("img", "blk"), scatter_dimension=0, tiled=True),
        lax.psum_scatter(grad_proj_weight, ("img", "blk"), scatter_dimension=0, tiled=True),
        lax.psum_scatter(grad_proj_bias, ("img", "blk"), scatter_dimension=0, tiled=True),
        lax.psum_scatter(grad_attn_scale, ("img", "blk"), scatter_dimension=0, tiled=True),
        lax.psum_scatter(grad_mlp_gain, ("img", "blk"), scatter_dimension=0, tiled=True),
        lax.psum_scatter(grad_mlp_shift, ("img", "blk"), scatter_dimension=0, tiled=True),
        lax.psum_scatter(grad_inner_weight, ("img", "blk"), scatter_dimension=0, tiled=True),
        lax.psum_scatter(grad_inner_bias, ("img", "blk"), scatter_dimension=0, tiled=True),
        lax.psum_scatter(grad_outer_weight, ("img", "blk"), scatter_dimension=0, tiled=True),
        lax.psum_scatter(grad_outer_bias, ("img", "blk"), scatter_dimension=0, tiled=True),
        lax.psum_scatter(grad_mlp_scale, ("img", "blk"), scatter_dimension=0, tiled=True),
    )
    table_sum_large, table_sum_small = lax.psum(
        (large_table_grad, small_table_grad), ("img", "blk")
    )
    return (
        result_low[:split_at].reshape(large_count, large_rows, width),
        result_low[split_at:].reshape(small_count, small_rows, width),
        grad_flat[:split_at].reshape(large_count, large_rows, width),
        grad_flat[split_at:].reshape(small_count, small_rows, width),
        summed[0],
        summed[1],
        summed[2],
        summed[3],
        summed[4],
        table_sum_large,
        table_sum_small,
        summed[5],
        summed[6],
        summed[7],
        summed[8],
        summed[9],
        summed[10],
        summed[11],
        summed[12],
        summed[13],
        summed[14],
    )


NT = (((1,), (1,)), ((), ()))
TN = (((0,), (0,)), ((), ()))
WIDE = jnp.float32
NARROW = jnp.bfloat16
LANES = 128
FIXED = 4096.0
MEGA = 1 << 20


def round_up(count, step):
    return -(-count // step) * step


def params(limit, *names):
    return pltpu.CompilerParams(vmem_limit_bytes=limit * MEGA, dimension_semantics=("arbitrary",))


def cost(micros):
    return pl.CostEstimate(flops=int(micros * 1.15e9), bytes_accessed=int(micros * 3.2e6), transcendentals=0)


def whole(shape):
    return pl.BlockSpec(shape, lambda i: (0,) * len(shape), pipeline_mode=pl.Buffered(1))


def row_norm(values):
    center = values - jnp.mean(values, -1, keepdims=True)
    spread = jnp.mean(center * center, -1, keepdims=True)
    inverse = lax.rsqrt(spread + EPSILON)
    return center * inverse, inverse


def norm_backward(grad, normal, inverse, gain):
    scaled = grad * gain
    first = jnp.mean(scaled, -1, keepdims=True)
    second = jnp.mean(scaled * normal, -1, keepdims=True)
    return inverse * (scaled - first - normal * second)


def bias_kernel(pairs, groups, table_ref, index_ref, out_ref):
    rows, lanes = index_ref.shape

    def one_tile(tile, carry):
        column = pl.multiple_of(tile * LANES, LANES)
        for first in range(0, rows, 16):
            found = []
            for half in (0, 8):
                index = index_ref[pl.ds(first + half, 8), pl.ds(column, LANES)]
                low = lax.bitwise_and(index, LANES - 1)
                high = lax.shift_right_logical(index, 7)
                picked = [None] * pairs
                for group in range(groups):
                    here = high == group
                    for pair in range(pairs):
                        source = table_ref[group * pairs + pair]
                        value = jnp.take_along_axis(source, low, axis=1)
                        picked[pair] = value if group == 0 else jnp.where(here, value, picked[pair])
                found.append(picked)
            for pair in range(pairs):
                both = jnp.concatenate([found[0][pair], found[1][pair]], 0)
                upper = lax.shift_right_arithmetic(both, 16)
                lower = lax.shift_right_arithmetic(lax.shift_left(both, 16), 16)
                place = (pl.ds(first, 16), pl.ds(column, LANES))
                out_ref[2 * pair, place[0], place[1]] = (upper.astype(WIDE) * (1 / FIXED)).astype(NARROW)
                out_ref[2 * pair + 1, place[0], place[1]] = (lower.astype(WIDE) * (1 / FIXED)).astype(NARROW)
        return carry

    lax.fori_loop(0, lanes // LANES, one_tile, 0)


def spread_kernel(pieces, length, piece, index_ref, out_ref):
    out_ref[...] = jnp.zeros_like(out_ref)
    turned = jnp.transpose(index_ref[...])
    for key in range(pieces):
        for query in range(pieces):
            out_ref[key * piece : key * piece + length, query * piece : query * piece + length] = turned[
                key * length : (key + 1) * length, query * length : (query + 1) * length
            ]


def spread_index(index, pieces, piece, rows, lanes):
    length = index.shape[0] // pieces
    return pl.pallas_call(
        functools.partial(spread_kernel, pieces, length, piece),
        out_shape=jax.ShapeDtypeStruct((rows, lanes), jnp.int32),
        compiler_params=pltpu.CompilerParams(vmem_limit_bytes=32 * MEGA),
        cost_estimate=cost(rows * lanes * 1e-5),
        name="spread_index",
    )(index)


def bias_lookup(table, index):
    heads = table.shape[1]
    pairs = heads // 2
    groups = round_up(table.shape[0], LANES) // LANES
    fixed = jnp.round(table.astype(WIDE) * FIXED).astype(jnp.int32)
    fixed = jnp.pad(fixed, ((0, groups * LANES - table.shape[0]), (0, 0)))
    packed = lax.bitwise_or(
        lax.shift_left(fixed[:, 0::2], 16), lax.bitwise_and(fixed[:, 1::2], 65535)
    )
    packed = jnp.transpose(packed.reshape(groups, LANES, pairs), (0, 2, 1)).reshape(-1, 1, LANES)
    packed = jnp.broadcast_to(packed, (groups * pairs, 8, LANES))
    rows, lanes = index.shape
    step = next(s for s in (32, 16) if rows % s == 0)
    return pl.pallas_call(
        functools.partial(bias_kernel, pairs, groups),
        grid=(rows // step,),
        in_specs=[whole((groups * pairs, 8, LANES)), pl.BlockSpec((step, lanes), lambda i: (i, 0))],
        out_specs=pl.BlockSpec((heads, step, lanes), lambda i: (0, i, 0)),
        out_shape=jax.ShapeDtypeStruct((heads, rows, lanes), NARROW),
        compiler_params=params(32),
        cost_estimate=cost(rows * lanes * groups * pairs * 1.5e-6),
        name="bias_lookup",
    )(packed, index)


def qkv_kernel(x_ref, gain_ref, shift_ref, weight_ref, bias_ref, h_ref, p_ref):
    @pl.when(pl.program_id(0) == 0)
    def _():
        normal, _ = row_norm(x_ref[...].astype(WIDE))
        h_ref[...] = (normal * gain_ref[...] + shift_ref[...]).astype(NARROW)

    product = jnp.dot(h_ref[...], weight_ref[...], preferred_element_type=WIDE)
    p_ref[...] = (product + bias_ref[...]).astype(NARROW)


def qkv_forward(x, gain, shift, weight, bias):
    tokens, width = x.shape
    total = weight.shape[1]
    return pl.pallas_call(
        qkv_kernel,
        grid=(total // width,),
        in_specs=[
            whole((tokens, width)),
            whole((1, width)),
            whole((1, width)),
            pl.BlockSpec((width, width), lambda i: (0, i)),
            pl.BlockSpec((1, width), lambda i: (0, i)),
        ],
        out_specs=[whole((tokens, width)), pl.BlockSpec((tokens, width), lambda i: (0, i))],
        out_shape=[
            jax.ShapeDtypeStruct((tokens, width), NARROW),
            jax.ShapeDtypeStruct((tokens, total), NARROW),
        ],
        compiler_params=params(48),
        cost_estimate=cost(tokens * width * total * 5e-9),
        name="qkv_forward",
    )(x, gain, shift, weight, bias)


def head_parts(first_half, value, other):
    return jnp.where(first_half, value, other), jnp.where(first_half, other, value)


def attention_forward_kernel(
    images,
    core_ref,
    q_ref,
    k_ref,
    v_ref,
    mask_ref,
    own_bias_ref,
    other_bias_ref,
    small_bias_ref,
    o_ref,
    large_p_ref,
    small_p_ref,
):
    is_own = pl.program_id(0) < pl.num_programs(0) // 2
    lane = lax.broadcasted_iota(jnp.int32, (1, LANES), 1)
    first_half = lane < HEAD
    for number, (start, rows) in enumerate(images):
        place = slice(start, start + rows)
        query = q_ref[place, :] * jnp.asarray(HEAD ** (-0.5), NARROW)
        ones = jnp.where(lane % HEAD == 0, 1.0, 0.0).astype(NARROW)
        ones = jnp.broadcast_to(ones, query.shape)
        queries = head_parts(first_half, query, ones)
        keys = head_parts(first_half, k_ref[place, :], mask_ref[place, :])
        value = v_ref[place, :]
        outs = []
        for head in range(2):
            if number == 0:
                bias = jnp.where(is_own, own_bias_ref[head, :, :rows], other_bias_ref[head, :, :rows])
            else:
                bias = small_bias_ref[head, :rows, :rows]
            scores = lax.dot_general(keys[head], queries[head], NT, preferred_element_type=WIDE)
            scores = scores + bias.astype(WIDE)
            weights = jnp.exp(scores - jnp.max(scores, 0, keepdims=True))
            probs = (weights * (1.0 / jnp.sum(weights, 0, keepdims=True))).astype(NARROW)
            if number == 0:
                large_p_ref[head] = probs
            else:
                small_p_ref[head, number - 1] = probs
            outs.append(lax.dot_general(probs, value, TN, preferred_element_type=WIDE))
        o_ref[place, :] = jnp.where(first_half, outs[0], outs[1]).astype(NARROW)


def attention_forward(core, p, mask, own_bias, other_bias, small_bias, images):
    tokens = p.shape[0]
    heads = small_bias.shape[0]
    pairs = heads // 2
    half = pairs // 2
    large, small, smalls = images[0][1], images[1][1], len(images) - 1
    area = large * large + smalls * small * small

    def pair(i, core):
        return lax.rem(i + half * core[0], pairs)

    def column(offset):
        return pl.BlockSpec((tokens, LANES), lambda i, core: (0, offset + pair(i, core)))

    bias_block = (2,) + own_bias.shape[1:]
    return pl.pallas_call(
        functools.partial(attention_forward_kernel, images),
        grid_spec=pltpu.PrefetchScalarGridSpec(
            num_scalar_prefetch=1,
            grid=(pairs,),
            in_specs=[
                column(0),
                column(pairs),
                column(2 * pairs),
                pl.BlockSpec((tokens, LANES), lambda i, core: (0, 0)),
                pl.BlockSpec(bias_block, lambda i, core: (jnp.minimum(i, half - 1), 0, 0)),
                pl.BlockSpec(bias_block, lambda i, core: (jnp.maximum(i - half, 0), 0, 0)),
                pl.BlockSpec((2,) + small_bias.shape[1:], lambda i, core: (pair(i, core), 0, 0)),
            ],
            out_specs=[
                column(0),
                pl.BlockSpec((2, large, large), lambda i, core: (pair(i, core), 0, 0)),
                pl.BlockSpec((2, smalls, small, small), lambda i, core: (pair(i, core), 0, 0, 0)),
            ],
        ),
        out_shape=[
            jax.ShapeDtypeStruct((tokens, heads * HEAD), NARROW),
            jax.ShapeDtypeStruct((heads, large, large), NARROW),
            jax.ShapeDtypeStruct((heads, smalls, small, small), NARROW),
        ],
        compiler_params=params(48),
        cost_estimate=cost(heads * area * 3.8e-6),
        name="attention_forward",
    )(core, p, p, p, mask, own_bias, other_bias, small_bias)


def attention_backward_kernel(
    images,
    core_ref,
    q_ref,
    k_ref,
    v_ref,
    do_ref,
    o_ref,
    large_p_ref,
    small_p_ref,
    dp_ref,
    large_mine_ref,
    large_theirs_ref,
    small_mine_ref,
    small_theirs_ref,
):
    is_first = core_ref[0] == 0

    def deal(head, grad_scores, mine_ref, theirs_ref):
        half = mine_ref.shape[1]
        count, lanes = grad_scores.shape
        lower = grad_scores[:half]
        upper = grad_scores[half:]
        rest = count - half
        mine_ref[head, :rest, :lanes] = jnp.where(is_first, lower[:rest], upper)
        theirs_ref[head, :rest, :lanes] = jnp.where(is_first, upper, lower[:rest])
        if rest < half:
            zeros = jnp.zeros((half - rest, lanes), NARROW)
            mine_ref[head, rest:, :lanes] = jnp.where(is_first, lower[rest:], zeros)
            theirs_ref[head, rest:, :lanes] = jnp.where(is_first, zeros, lower[rest:])
        beyond = mine_ref.shape[2] - lanes
        if beyond:
            mine_ref[head, :, lanes:] = jnp.zeros((half, beyond), NARROW)
            theirs_ref[head, :, lanes:] = jnp.zeros((half, beyond), NARROW)

    lane = lax.broadcasted_iota(jnp.int32, (1, LANES), 1)
    first_half = lane < HEAD
    small_sum = [None, None]
    scale = HEAD ** (-0.5)
    for number, (start, rows) in enumerate(images):
        place = slice(start, start + rows)
        query = q_ref[place, :] * jnp.asarray(scale, NARROW)
        key = k_ref[place, :]
        value = v_ref[place, :]
        grad = do_ref[place, :]
        product = jnp.transpose(grad.astype(WIDE) * o_ref[place, :].astype(WIDE))
        grads = head_parts(first_half, grad, jnp.zeros_like(grad))
        parts = []
        for head in range(2):
            inner = jnp.sum(product[head * HEAD : (head + 1) * HEAD], 0, keepdims=True)
            probs = large_p_ref[head] if number == 0 else small_p_ref[head, number - 1]
            grad_probs = lax.dot_general(value, grads[head], NT, preferred_element_type=WIDE)
            grad_scores = (probs.astype(WIDE) * (grad_probs - inner)).astype(NARROW)
            if number == 0:
                deal(head, grad_scores, large_mine_ref, large_theirs_ref)
            elif small_sum[head] is None:
                small_sum[head] = grad_scores.astype(WIDE)
            else:
                small_sum[head] = small_sum[head] + grad_scores.astype(WIDE)
            parts.append(
                (
                    lax.dot_general(grad_scores, key, TN, preferred_element_type=WIDE) * scale,
                    jnp.dot(grad_scores, query, preferred_element_type=WIDE),
                    jnp.dot(probs, grad, preferred_element_type=WIDE),
                )
            )
        for which in range(3):
            dp_ref[which, place, :] = jnp.where(first_half, parts[0][which], parts[1][which]).astype(NARROW)
    for head in range(2):
        deal(head, small_sum[head].astype(NARROW), small_mine_ref, small_theirs_ref)


def attention_backward(core, p, grad_out, out, large_p, small_p, images, large_pad, small_pad):
    tokens = p.shape[0]
    heads = large_p.shape[0]
    pairs = heads // 2
    large, small, smalls = images[0][1], images[1][1], len(images) - 1
    area = large * large + smalls * small * small

    def column(offset):
        return pl.BlockSpec((tokens, LANES), lambda i, core: (0, offset + i))

    def by_pair(*shape):
        return pl.BlockSpec((2,) + shape, lambda i, core: (i,) + (0,) * len(shape))

    shares = (large_pad, large_pad, small_pad, small_pad)
    return pl.pallas_call(
        functools.partial(attention_backward_kernel, images),
        grid_spec=pltpu.PrefetchScalarGridSpec(
            num_scalar_prefetch=1,
            grid=(pairs,),
            in_specs=[
                column(0),
                column(pairs),
                column(2 * pairs),
                column(0),
                column(0),
                by_pair(large, large),
                by_pair(smalls, small, small),
            ],
            out_specs=[pl.BlockSpec((3, tokens, LANES), lambda i, core: (0, 0, i))]
            + [by_pair(*share) for share in shares],
        ),
        out_shape=[jax.ShapeDtypeStruct((3, tokens, heads * HEAD), NARROW)]
        + [jax.ShapeDtypeStruct((heads,) + share, NARROW) for share in shares],
        compiler_params=params(48),
        cost_estimate=cost(heads * area * 4.2e-6),
        name="attention_backward",
    )(core, p, p, p, grad_out, out, large_p, small_p)


def gelu_parts(value):
    size = jnp.abs(value)
    inverse = 1.0 / (1.0 + (0.3275911 * 0.7071067811865476) * size)
    series = inverse * (
        0.127414796
        + inverse
        * (-0.142248368 + inverse * (0.7107068705 + inverse * (-0.7265760135 + inverse * 0.5307027145)))
    )
    bell = jnp.exp(-0.5 * value * value)
    tail = series * bell
    share = jnp.where(value < 0, tail, 1.0 - tail)
    return value * share, share + value * (bell * 0.3989422804014327)


def mlp_kernel(
    o_ref,
    x_ref,
    dy_ref,
    proj_ref,
    vector_ref,
    inner_ref,
    inner_bias_ref,
    outer_ref,
    result_ref,
    dm_ref,
    do_ref,
    dinner_ref,
    douter_ref,
    dproj_ref,
    dvector_ref,
    dbias_ref,
    r_ref,
    g_ref,
    dz_ref,
    z_ref,
    dg_ref,
):
    step = pl.program_id(0)
    proj_bias, attn_scale, gain, shift, outer_bias, mlp_scale = (vector_ref[i : i + 1, :] for i in range(6))
    tokens = x_ref.shape[0]
    chunk = next(c for c in (128, 64, 32, 16) if tokens % c == 0)

    @pl.when(step == 0)
    def _():
        r_ref[...] = jnp.dot(o_ref[...], proj_ref[...], preferred_element_type=WIDE) + proj_bias

        @pl.loop(0, tokens // chunk)
        def _(i):
            rows = pl.ds(pl.multiple_of(i * chunk, chunk), chunk)
            middle = x_ref[rows, :].astype(WIDE) + attn_scale * r_ref[rows, :]
            normal, _ = row_norm(middle)
            g_ref[rows, :] = (normal * gain + shift).astype(NARROW)
            dz_ref[rows, :] = (mlp_scale * dy_ref[rows, :].astype(WIDE)).astype(NARROW)

    pre = jnp.dot(g_ref[...], inner_ref[...], preferred_element_type=WIDE) + inner_bias_ref[...]
    active, slope = gelu_parts(pre)
    active = active.astype(NARROW)
    dz = dz_ref[...]
    dactive = lax.dot_general(dz, outer_ref[...], NT, preferred_element_type=WIDE)
    dpre = (dactive * slope).astype(NARROW)
    douter_ref[...] = lax.dot_general(active, dz, TN, preferred_element_type=WIDE).astype(NARROW)
    dinner_ref[0] = lax.dot_general(g_ref[...], dpre, TN, preferred_element_type=WIDE).astype(NARROW)
    dbias_ref[...] = jnp.sum(dpre.astype(WIDE), 0, keepdims=True)
    z = jnp.dot(active, outer_ref[...], preferred_element_type=WIDE)
    dg = lax.dot_general(dpre, inner_ref[...], NT, preferred_element_type=WIDE)

    @pl.when(step == 0)
    def _():
        z_ref[...] = z
        dg_ref[...] = dg

    @pl.when(step > 0)
    def _():
        z_ref[...] += z
        dg_ref[...] += dg

    @pl.when(step == pl.num_programs(0) - 1)
    def _():
        dvector_ref[...] = jnp.zeros_like(dvector_ref)

        @pl.loop(0, tokens // chunk)
        def _(i):
            rows = pl.ds(pl.multiple_of(i * chunk, chunk), chunk)
            branch = r_ref[rows, :]
            middle = x_ref[rows, :].astype(WIDE) + attn_scale * branch
            normal, inverse = row_norm(middle)
            outer = z_ref[rows, :] + outer_bias
            dy = dy_ref[rows, :].astype(WIDE)
            result_ref[rows, :] = (middle + mlp_scale * outer).astype(NARROW)
            grad = dg_ref[rows, :]
            dm = dy + norm_backward(grad, normal, inverse, gain)
            dm_ref[rows, :] = dm
            dr = (attn_scale * dm).astype(NARROW)
            g_ref[rows, :] = dr
            sums = [
                dy * outer,
                dz_ref[rows, :].astype(WIDE),
                grad * normal,
                grad,
                dm * branch,
                dr.astype(WIDE),
            ]
            for place, term in enumerate(sums):
                dvector_ref[place : place + 1, :] += jnp.sum(term, 0, keepdims=True)

        dr = g_ref[...]
        dproj_ref[...] = lax.dot_general(o_ref[...], dr, TN, preferred_element_type=WIDE).astype(NARROW)
        do_ref[...] = lax.dot_general(dr, proj_ref[...], NT, preferred_element_type=WIDE).astype(NARROW)


def mlp_pass(out, x, dy, proj, vectors, inner, inner_bias, outer):
    tokens, width = x.shape
    hidden = inner.shape[1]
    block = width
    return pl.pallas_call(
        mlp_kernel,
        grid=(hidden // block,),
        in_specs=[
            whole((tokens, width)),
            whole((tokens, width)),
            whole((tokens, width)),
            whole((width, width)),
            whole((8, width)),
            pl.BlockSpec((width, block), lambda i: (0, i)),
            pl.BlockSpec((1, block), lambda i: (0, i)),
            pl.BlockSpec((block, width), lambda i: (i, 0)),
        ],
        out_specs=[
            whole((tokens, width)),
            whole((tokens, width)),
            whole((tokens, width)),
            pl.BlockSpec((1, width, block), lambda i: (i, 0, 0)),
            pl.BlockSpec((block, width), lambda i: (i, 0)),
            whole((width, width)),
            whole((8, width)),
            pl.BlockSpec((1, block), lambda i: (0, i)),
        ],
        out_shape=[
            jax.ShapeDtypeStruct((tokens, width), NARROW),
            jax.ShapeDtypeStruct((tokens, width), WIDE),
            jax.ShapeDtypeStruct((tokens, width), NARROW),
            jax.ShapeDtypeStruct((hidden // block, width, block), NARROW),
            jax.ShapeDtypeStruct((hidden, width), NARROW),
            jax.ShapeDtypeStruct((width, width), NARROW),
            jax.ShapeDtypeStruct((8, width), WIDE),
            jax.ShapeDtypeStruct((1, hidden), WIDE),
        ],
        scratch_shapes=[
            pltpu.VMEM((tokens, width), WIDE),
            pltpu.VMEM((tokens, width), NARROW),
            pltpu.VMEM((tokens, width), NARROW),
            pltpu.VMEM((tokens, width), WIDE),
            pltpu.VMEM((tokens, width), WIDE),
        ],
        compiler_params=params(60),
        cost_estimate=cost(tokens * width * hidden * 2.4e-8),
        name="mlp_pass",
    )(out, x, dy, proj, vectors, inner, inner_bias, outer)


def qkv_backward_kernel(dp_ref, h_ref, x_ref, dm_ref, gain_ref, weight_ref, dweight_ref, dx_ref, dvector_ref, dh_ref):
    step = pl.program_id(0)
    grad = dp_ref[0]
    dweight_ref[0] = lax.dot_general(h_ref[...], grad, TN, preferred_element_type=WIDE).astype(NARROW)
    term = lax.dot_general(grad, weight_ref[...], NT, preferred_element_type=WIDE)
    column_sum = jnp.sum(grad.astype(WIDE), 0, keepdims=True)
    tokens = x_ref.shape[0]
    chunk = next(c for c in (128, 64, 32, 16) if tokens % c == 0)

    @pl.when(step == 0)
    def _():
        dvector_ref[...] = jnp.zeros_like(dvector_ref)
        dh_ref[...] = term
        dvector_ref[0:1, :] = column_sum

    @pl.when(step > 0)
    def _():
        dh_ref[...] += term

    @pl.when(step == pl.num_programs(0) - 1)
    def _():
        dvector_ref[1:2, :] = column_sum

        @pl.loop(0, tokens // chunk)
        def _(i):
            rows = pl.ds(pl.multiple_of(i * chunk, chunk), chunk)
            normal, inverse = row_norm(x_ref[rows, :].astype(WIDE))
            dh = dh_ref[rows, :]
            dx = dm_ref[rows, :] + norm_backward(dh, normal, inverse, gain_ref[...])
            dx_ref[rows, :] = dx.astype(NARROW)
            dvector_ref[2:3, :] += jnp.sum(dh * normal, 0, keepdims=True)
            dvector_ref[3:4, :] += jnp.sum(dh, 0, keepdims=True)


def qkv_backward(dp, h, x, dm, gain, weight):
    tokens, width = x.shape
    return pl.pallas_call(
        qkv_backward_kernel,
        grid=(3,),
        in_specs=[
            pl.BlockSpec((1, tokens, width), lambda i: (i, 0, 0)),
            whole((tokens, width)),
            whole((tokens, width)),
            whole((tokens, width)),
            whole((1, width)),
            pl.BlockSpec((width, width), lambda i: (0, i)),
        ],
        out_specs=[
            pl.BlockSpec((1, width, width), lambda i: (i, 0, 0)),
            whole((tokens, width)),
            whole((8, width)),
        ],
        out_shape=[
            jax.ShapeDtypeStruct((3, width, width), NARROW),
            jax.ShapeDtypeStruct((tokens, width), NARROW),
            jax.ShapeDtypeStruct((8, width), WIDE),
        ],
        scratch_shapes=[pltpu.VMEM((tokens, width), WIDE)],
        compiler_params=params(48),
        cost_estimate=cost(tokens * width * width * 2.5e-8),
        name="qkv_backward",
    )(dp, h, x, dm, gain, weight)


def table_kernel(
    heads, groups, batch, core_ref, own_ref, other_ref, index_ref, out_ref, turned_ref, left_ref, right_ref
):
    @pl.when(pl.program_id(0) == 0)
    def _():
        out_ref[...] = jnp.zeros_like(out_ref)
        turned_ref[...] = jnp.zeros_like(turned_ref)

    rows, lanes = index_ref.shape
    for head in range(heads):
        turned_ref[:, head, :] = own_ref[head].astype(WIDE) + other_ref[head].astype(WIDE)
    zero = jnp.zeros((), NARROW)
    one = jnp.ones((), NARROW)
    codes = lax.broadcasted_iota(jnp.int32, (LANES, LANES), 0).astype(WIDE).astype(NARROW)

    def some_rows(part, carry):
        for within in range(batch):
            row = part * batch + within
            index = index_ref[pl.ds(row, 1), :]
            low = lax.bitwise_and(index, LANES - 1).astype(WIDE).astype(NARROW)
            high = lax.shift_right_logical(index, 7).astype(WIDE).astype(NARROW)
            for first in range(0, lanes, LANES):
                here = slice(first, first + LANES)
                there = slice(within * lanes + first, within * lanes + first + LANES)
                right_ref[:, there] = jnp.where(codes == low[:, here], one, zero)
                value = turned_ref[row, :, here].astype(NARROW)
                wide_high = jnp.broadcast_to(high[:, here], value.shape)
                for group in range(groups):
                    left_ref[group * 16 : group * 16 + 16, there] = jnp.where(
                        wide_high == jnp.asarray(group, NARROW), value, zero
                    )
        out_ref[...] += lax.dot_general(left_ref[...], right_ref[...], NT, preferred_element_type=WIDE)
        return carry

    lax.fori_loop(0, rows // batch, some_rows, 0)


def table_gradient_sum(core, own, other, index, table_rows, parts=1, part=0):
    heads, share, lanes = own.shape
    groups = round_up(table_rows, LANES) // LANES
    batch = 4
    step = 16
    steps = share // step
    first = steps * part // parts
    count = steps * (part + 1) // parts - first
    return pl.pallas_call(
        functools.partial(table_kernel, heads, groups, batch),
        grid_spec=pltpu.PrefetchScalarGridSpec(
            num_scalar_prefetch=1,
            grid=(count,),
            in_specs=[
                pl.BlockSpec((heads, step, lanes), lambda i, core: (0, first + i, 0)),
                pl.BlockSpec((heads, step, lanes), lambda i, core: (0, first + i, 0)),
                pl.BlockSpec((step, lanes), lambda i, core: (first + i + core[0] * steps, 0)),
            ],
            out_specs=pl.BlockSpec((groups * 16, LANES), lambda i, core: (0, 0)),
            scratch_shapes=[
                pltpu.VMEM((step, 16, lanes), WIDE),
                pltpu.VMEM((groups * 16, batch * lanes), NARROW),
                pltpu.VMEM((LANES, batch * lanes), NARROW),
            ],
        ),
        out_shape=jax.ShapeDtypeStruct((groups * 16, LANES), WIDE),
        compiler_params=params(48),
        cost_estimate=cost(count * step * lanes * 2.8e-4),
        name="table_gradient",
    )(core, own, other, index)


def rotate(value, axis, size, shift):
    return lax.ppermute(value, axis, [(i, (i + shift) % size) for i in range(size)])


def swap_bit(value, size, bit):
    return lax.ppermute(value, "img", [(i, i ^ (1 << bit)) for i in range(size)])


def exchange(pieces, size):
    me = lax.axis_index("blk")
    got = [lax.dynamic_index_in_dim(pieces, me, 0, False)]
    for shift in range(1, size):
        target = lax.rem(me + shift, size)
        got.append(rotate(lax.dynamic_index_in_dim(pieces, target, 0, False), "blk", size, shift))
    return [lax.select_n(lax.rem(me + size - place, size), *got) for place in range(size)]


def halves(value, bit, position):
    mine = lax.rem(lax.div(lax.axis_index("img"), 1 << bit), 2)
    keep = lax.dynamic_index_in_dim(value, mine, position, False)
    send = lax.dynamic_index_in_dim(value, 1 - mine, position, False)
    return keep, send


def add_low(first, second):
    return (first.astype(WIDE) + second.astype(WIDE)).astype(NARROW)


def sum_all(value, img, blk):
    rows = value.shape[0]
    value = jnp.pad(value, ((0, -rows % 32), (0, 0))).astype(NARROW)
    keep, send = halves(value.reshape((2, -1) + value.shape[1:]), 0, 0)
    value = add_low(keep, swap_bit(send, img, 0))
    for bit in range(1, img.bit_length() - 1):
        value = add_low(value, swap_bit(value, img, bit))
    bit = 1
    while bit < blk:
        value = add_low(value, lax.ppermute(value, "blk", [(i, i ^ bit) for i in range(blk)]))
        bit *= 2
    other = swap_bit(value, img, 0)
    first = lax.rem(lax.axis_index("img"), 2) == 0
    value = jnp.concatenate([jnp.where(first, value, other), jnp.where(first, other, value)], 0)
    return value[:rows].astype(WIDE)


def scatter_offloaded(value):
    value = lax.psum_scatter(value, "img", scatter_dimension=0, tiled=True)
    return lax.psum_scatter(value, "blk", scatter_dimension=0, tiled=True)[0].astype(WIDE)


def together(*values):
    return lax.optimization_barrier(values)


def image_on_device(
    img,
    blk,
    images_large,
    images_small,
    cotan_large,
    cotan_small,
    lengths_large,
    lengths_small,
    index_large,
    index_small,
    attn_gain,
    attn_shift,
    qkv_weight,
    query_bias,
    value_bias,
    table_large,
    table_small,
    proj_weight,
    proj_bias,
    attn_scale,
    mlp_gain,
    mlp_shift,
    inner_weight,
    inner_bias,
    outer_weight,
    outer_bias,
    mlp_scale,
):
    width = attn_gain.shape[0]
    heads = table_large.shape[1]
    hidden = inner_bias.shape[0]
    rows = images_large.shape[1]
    smalls, small_rows = images_small.shape[:2]
    part = round_up(rows, 8)
    while part * blk % 16:
        part += 8
    large = part * blk
    small = round_up(small_rows, 16)
    tokens = large + smalls * small
    images = ((0, large),) + tuple((large + i * small, small) for i in range(smalls))
    lanes_large = round_up(large, LANES)
    lanes_small = round_up(small, LANES)
    double = round_up(small, 32)
    blk_me = lax.axis_index("blk")
    core = lax.rem(lax.axis_index("img"), 2)

    def gather_tokens(moved, still):
        still = jnp.pad(still, ((0, 0), (0, small - small_rows), (0, 0)))
        return jnp.concatenate(moved + [still.reshape(smalls * small, width)], 0)

    def small_rows_of(values):
        return values[large:].reshape(smalls, small, width)[:, :small_rows]

    spread_large = spread_index(index_large, blk, part, large, lanes_large)
    spread_small = spread_index(index_small, 1, small, double, lanes_small)
    core_list = core.reshape(1)

    def to_pieces(values):
        return jnp.pad(values, ((0, 0), (0, part - rows), (0, 0)))

    moved = exchange(to_pieces(images_large), blk)
    half = heads // 2
    small_bias = bias_lookup(table_small, spread_small)
    own_bias = bias_lookup(
        lax.dynamic_slice_in_dim(table_large, core * half, half, 1), together(spread_large, small_bias)[0]
    )
    moved, own_bias, images_small, cotan_large, cotan_small, lengths_large, lengths_small = together(
        moved, own_bias, images_small, cotan_large, cotan_small, lengths_large, lengths_small
    )
    other_bias = swap_bit(own_bias, img, 0)
    x = gather_tokens(moved, images_small)

    place = jnp.arange(large, dtype=jnp.int32)
    own_length = lax.dynamic_index_in_dim(lengths_large, blk_me, 0, False)
    inside = (place % part < rows) & (place // part * rows + place % part < own_length)
    small_place = jnp.arange(small, dtype=jnp.int32)
    small_inside = (small_place[None, :] < lengths_small[:, None]).reshape(-1)
    mask = jnp.where(jnp.concatenate([inside, small_inside]), 0.0, NEGATIVE).astype(NARROW)
    mask = jnp.broadcast_to(mask[:, None], (tokens, LANES))

    def row(vector):
        return vector.astype(WIDE)[None, :]

    bias_row = row(jnp.concatenate([query_bias, jnp.zeros_like(query_bias), value_bias]))
    h, p = qkv_forward(x, row(attn_gain), row(attn_shift), qkv_weight, bias_row)
    h, p, other_bias, cotan_large, cotan_small = together(h, p, other_bias, cotan_large, cotan_small)
    moved = exchange(to_pieces(cotan_large), blk)
    out, large_p, small_p = attention_forward(core_list, p, mask, own_bias, other_bias, small_bias, images)
    out, large_p, small_p, moved, cotan_small = together(out, large_p, small_p, moved, cotan_small)
    dy = gather_tokens(moved, cotan_small)
    zeros = jnp.zeros_like(proj_bias)
    vectors = jnp.stack(
        [proj_bias, attn_scale, mlp_gain, mlp_shift, outer_bias, mlp_scale, zeros, zeros]
    ).astype(WIDE)
    result, dm, grad_out, dinner, douter, dproj, mlp_sums, dinner_bias = mlp_pass(
        out, x, dy, proj_weight, vectors, inner_weight, row(inner_bias), outer_weight
    )
    devices = img * blk
    share = width // devices
    blocks = hidden // width
    feed = jnp.concatenate(
        [
            douter.reshape(devices, blocks * share, width),
            jnp.transpose(dinner.reshape(blocks, devices, share, width), (1, 0, 2, 3)).reshape(
                devices, blocks * share, width
            ),
        ],
        1,
    )
    grad_out, feed, result = together(grad_out, feed, result)
    feed_sum = scatter_offloaded(feed)
    result_back = exchange(result[:large].reshape(blk, part, width), blk)
    dp, large_mine, large_theirs, small_mine, small_theirs = attention_backward(
        core_list,
        p,
        grad_out,
        out,
        large_p,
        small_p,
        images,
        (large // 2, lanes_large),
        (double // 2, lanes_small),
    )
    dp, large_mine, large_theirs, small_mine, small_theirs, result_back, dm, dproj, mlp_sums, dinner_bias = together(
        dp, large_mine, large_theirs, small_mine, small_theirs, result_back, dm, dproj, mlp_sums, dinner_bias
    )
    large_other = swap_bit(large_theirs, img, 0)
    small_other = swap_bit(small_theirs, img, 0)
    dqkv, dx, qkv_sums = qkv_backward(dp, h, x, dm, row(attn_gain), qkv_weight)
    dqkv, dx, qkv_sums, large_other, small_other, result_back, dproj = together(
        dqkv, dx, qkv_sums, large_other, small_other, result_back, dproj
    )

    table_parts = 4

    def table_part(index, part):
        return table_gradient_sum(
            core_list, large_mine, large_other, index, table_large.shape[0], table_parts, part
        )

    bits = img.bit_length() - 1
    pieces = [value.reshape(devices, share, width) for value in (dqkv[0], dqkv[1], dqkv[2], dproj)]
    trees = [jnp.concatenate(pieces[:2], 1), jnp.concatenate(pieces[2:], 1)]
    trees = [value.reshape((2,) * bits + (blk, 2 * share, width)) for value in trees]
    orders = [list(range(bits)), [0] + list(range(bits - 1, 0, -1))]
    lefts = [list(range(bits)), list(range(bits))]
    parts = []
    small_table = None
    for level in range(bits):
        keeps, sends, gots = [], [], []
        for tree in range(2):
            bit = orders[tree][level]
            left = lefts[tree]
            keep, send = halves(trees[tree], bit, len(left) - 1 - left.index(bit))
            left.remove(bit)
            keeps.append(keep)
            sends.append(send)
        keeps, sends, spread_large, spread_small, dx, parts = together(
            keeps, sends, spread_large, spread_small, dx, parts
        )
        for tree in range(2):
            gots.append(swap_bit(sends[tree], img, orders[tree][level]))
        if level == 0:
            small_table = table_gradient_sum(core_list, small_mine, small_other, spread_small, table_small.shape[0])
        elif level < table_parts - 1:
            parts.append(table_part(spread_large, level - 1))
        keeps, gots, spread_large, dx, parts, small_table = together(
            keeps, gots, spread_large, dx, parts, small_table
        )
        trees = [add_low(keep, got) for keep, got in zip(keeps, gots)]
    joined = jnp.concatenate(trees, 1)
    sends = [lax.dynamic_index_in_dim(joined, lax.rem(blk_me + shift, blk), 0, False) for shift in range(1, blk)]
    total = lax.dynamic_index_in_dim(joined, blk_me, 0, False).astype(WIDE)
    total, sends, spread_large, dx, parts = together(total, sends, spread_large, dx, parts)
    gots = [rotate(send, "blk", blk, shift + 1) for shift, send in enumerate(sends)]
    while len(parts) < table_parts - 1:
        parts.append(table_part(spread_large, len(parts)))
    total, gots, spread_large, dx, parts = together(total, gots, spread_large, dx, parts)
    total = sum([got.astype(WIDE) for got in gots], total)
    first_sum, second_sum = total[: 2 * share], total[2 * share :]
    total, dx, spread_large = together(total, dx, spread_large)
    grad_back = exchange(dx[:large].reshape(blk, part, width), blk)
    parts.append(table_part(spread_large, table_parts - 1))
    grad_back, parts, first_sum, second_sum, dx, result, result_back = together(
        grad_back, parts, first_sum, second_sum, dx, result, result_back
    )
    tables = [sum(parts[1:], parts[0]), small_table]
    result_large = jnp.stack([piece[:rows] for piece in result_back])
    grad_large = jnp.stack([piece[:rows] for piece in grad_back])
    sums = jnp.concatenate([mlp_sums[:6], qkv_sums[:4], dinner_bias.reshape(-1, width)], 0)
    joined = jnp.concatenate(tables + [sums.reshape(-1, LANES)], 0)
    joined = sum_all(joined, img, blk)
    outs = []
    first = 0
    for table, total in ((table_large, tables[0]), (table_small, tables[1])):
        value = joined[first : first + total.shape[0]].reshape(-1, 16, LANES)[:, :heads]
        outs.append(jnp.transpose(value, (0, 2, 1)).reshape(-1, heads)[: table.shape[0]])
        first += total.shape[0]
    sums = joined[first:].reshape(-1)
    me = lax.axis_index("img") * blk + blk_me

    def own(place, length=1):
        return lax.dynamic_slice_in_dim(sums, place * width + me * share * length, share * length, 0)

    return (
        result_large,
        small_rows_of(result),
        grad_large,
        small_rows_of(dx),
        own(8),
        own(9),
        jnp.concatenate([first_sum[:share], first_sum[share:], second_sum[:share]], 1),
        own(6),
        own(7),
        outs[0],
        outs[1],
        second_sum[share:],
        own(5),
        own(4),
        own(2),
        own(3),
        jnp.transpose(feed_sum[blocks * share :].reshape(blocks, share, width), (1, 0, 2)).reshape(share, hidden),
        own(10, blocks),
        feed_sum[: blocks * share],
        own(1),
        own(0),
    )


def solution(mesh):
    img, blk = mesh.shape["img"], mesh.shape["blk"]

    def by_device(*args):
        if args[0].shape[0] == blk:
            return image_on_device(img, blk, *args)
        return on_device(*args)

    return jax.shard_map(
        by_device,
        mesh=mesh,
        in_specs=(
            P("img", "blk", None),
            P(("img", "blk"), None, None),
            P("img", "blk", None),
            P(("img", "blk"), None, None),
            P("img"),
            P(("img", "blk")),
            P(),
            P(),
            P(),
            P(),
            P(),
            P(),
            P(),
            P(),
            P(),
            P(),
            P(),
            P(),
            P(),
            P(),
            P(),
            P(),
            P(),
            P(),
            P(),
        ),
        out_specs=(
            P("img", "blk", None),
            P(("img", "blk"), None, None),
            P("img", "blk", None),
            P(("img", "blk"), None, None),
            P(("img", "blk")),
            P(("img", "blk")),
            P(("img", "blk"), None),
            P(("img", "blk")),
            P(("img", "blk")),
            P(),
            P(),
            P(("img", "blk"), None),
            P(("img", "blk")),
            P(("img", "blk")),
            P(("img", "blk")),
            P(("img", "blk")),
            P(("img", "blk"), None),
            P(("img", "blk")),
            P(("img", "blk"), None),
            P(("img", "blk")),
            P(("img", "blk")),
        ),
        check_vma=False,
    )
```

```python
import functools

import jax
import jax.numpy as jnp
from jax import lax
from jax.experimental import pallas as pl
from jax.experimental.pallas import tpu as pltpu
from jax.sharding import PartitionSpec as P

HEAD = 64


NEGATIVE = -1e30
EPSILON = 1e-06
HIGHEST = lax.Precision.HIGHEST


def layer_norm(values, gain, shift):
    center = values - jnp.mean(values, -1, keepdims=True)
    spread = jnp.mean(center * center, -1, keepdims=True)
    return center * lax.rsqrt(spread + EPSILON) * gain + shift


def exact_gelu(values):
    return jax.nn.gelu(values, approximate=False)


def lookup(table, index_block):
    table_codes = jnp.arange(table.shape[0], dtype=jnp.int32)

    def lookup_one_query(index_row):
        selector = (index_row[:, None] == table_codes[None, :]).astype(jnp.bfloat16)
        return jnp.dot(selector, table, preferred_element_type=jnp.float32)

    picked = lax.map(lookup_one_query, index_block, batch_size=8)
    return jnp.transpose(picked, (2, 0, 1))


def table_gradient(grad_full, index_block, table_rows):
    table_codes = jnp.arange(table_rows, dtype=jnp.int32)

    def table_one_query(item):
        index_row, grad_row = item
        selector = (index_row[:, None] == table_codes[None, :]).astype(jnp.float32)
        return jnp.dot(selector.T, grad_row, precision=HIGHEST, preferred_element_type=jnp.float32)

    partials = lax.map(
        table_one_query, (index_block, jnp.transpose(grad_full, (1, 2, 0))), batch_size=8
    )
    return jnp.sum(partials, 0)


def key_mask(lengths, first, count):
    places = first + jnp.arange(count, dtype=jnp.int32)
    return (places[None, :] < lengths[:, None])[:, None, None, :]


def block_scores(queries, key_piece, bias_rows, lengths, first):
    count = key_piece.shape[1]
    scores = jnp.einsum(
        "iqhe,ikhe->ihqk", queries, key_piece, preferred_element_type=jnp.float32
    ) * HEAD ** (-0.5)
    scores = scores + lax.dynamic_slice_in_dim(bias_rows, first, count, 2)[None]
    return (scores, key_mask(lengths, first, count))


def merge_heads(values):
    return jnp.transpose(values, (0, 2, 1, 3)).reshape(-1, values.shape[1] * values.shape[3])


def local_fold(pieces):

    def visit(step, state):
        return step(state, pieces, 0)

    return visit


def forward_attention(queries, bias_rows, lengths, visit):
    images, rows, heads, width = queries.shape

    def absorb(state, pieces, first):
        top, total, summed = state
        key_piece, value_piece = pieces
        scores, valid = block_scores(queries, key_piece, bias_rows, lengths, first)
        scores = jnp.where(valid, scores, NEGATIVE)
        new_top = jnp.maximum(top, jnp.max(scores, -1))
        weights = jnp.where(valid, jnp.exp(scores - new_top[..., None]), 0.0)
        factor = jnp.exp(top - new_top)
        total = total * factor + jnp.sum(weights, -1)
        update = jnp.einsum(
            "ihqk,ikhe->ihqe", weights, value_piece.astype(jnp.float32), precision=HIGHEST
        )
        return (new_top, total, summed * factor[..., None] + update)

    start_state = (
        jnp.full((images, heads, rows), NEGATIVE, jnp.float32),
        jnp.zeros((images, heads, rows), jnp.float32),
        jnp.zeros((images, heads, rows, width), jnp.float32),
    )
    top, total, summed = visit(absorb, start_state)
    return (summed / total[..., None], top + jnp.log(total))


def key_pass(queries, bias_rows, lengths, grad_out, inner, log_total, visit):
    images, rows, heads, width = queries.shape
    length = bias_rows.shape[2]
    grad_wide = grad_out.astype(jnp.float32)

    def collect(state, pieces, first):
        key_piece, value_piece = pieces
        scores, valid = block_scores(queries, key_piece, bias_rows, lengths, first)
        probs = jnp.where(valid, jnp.exp(scores - log_total[..., None]), 0.0)
        grad_probs = jnp.einsum(
            "iqhe,ikhe->ihqk", grad_out, value_piece, preferred_element_type=jnp.float32
        )
        grad_scores = (probs * (grad_probs - inner[..., None])).astype(jnp.bfloat16)
        grad_query = state[0] + jnp.einsum(
            "ihqk,ikhe->ihqe", grad_scores, key_piece, preferred_element_type=jnp.float32
        ) * HEAD ** (-0.5)
        bias_full = lax.dynamic_update_slice_in_dim(
            state[1], jnp.sum(grad_scores.astype(jnp.float32), 0), first, 2
        )
        key_part = jnp.einsum(
            "ihqk,iqhe->ikhe", grad_scores, queries, preferred_element_type=jnp.float32
        ) * HEAD ** (-0.5)
        value_part = jnp.einsum("ihqk,iqhe->ikhe", probs, grad_wide, precision=HIGHEST)
        key_full = lax.dynamic_update_slice_in_dim(state[2], key_part, first, 1)
        value_full = lax.dynamic_update_slice_in_dim(state[3], value_part, first, 1)
        return (grad_query, bias_full, key_full, value_full)

    start_state = (
        jnp.zeros((images, heads, rows, width), jnp.float32),
        jnp.zeros((heads, rows, length), jnp.float32),
    )
    start_state = start_state + (
        jnp.zeros((images, length, heads, width), jnp.float32),
        jnp.zeros((images, length, heads, width), jnp.float32),
    )
    return visit(collect, start_state)


def on_device(
    images_large,
    images_small,
    cotan_large,
    cotan_small,
    lengths_large,
    lengths_small,
    index_large,
    index_small,
    attn_gain,
    attn_shift,
    qkv_weight,
    query_bias,
    value_bias,
    table_large,
    table_small,
    proj_weight,
    proj_bias,
    attn_scale,
    mlp_gain,
    mlp_shift,
    inner_weight,
    inner_bias,
    outer_weight,
    outer_bias,
    mlp_scale,
):
    wide = jnp.float32
    narrow = jnp.bfloat16
    width = attn_gain.shape[0]
    heads = table_large.shape[1]
    large_count, large_rows = (images_large.shape[0], images_large.shape[1])
    small_count, small_rows = (images_small.shape[0], images_small.shape[1])
    split_at = large_count * large_rows
    first_key = lax.axis_index("blk") * large_rows
    flat = jnp.concatenate(
        [images_large.reshape(-1, width), images_small.reshape(-1, width)], 0
    ).astype(wide)
    normed, attn_norm_back = jax.vjp(
        layer_norm, flat, attn_gain.astype(wide), attn_shift.astype(wide)
    )
    normed_low = normed.astype(narrow)
    bias_vector = jnp.concatenate(
        [query_bias.astype(wide), jnp.zeros((width,), wide), value_bias.astype(wide)]
    )
    projected = (jnp.dot(normed_low, qkv_weight, preferred_element_type=wide) + bias_vector).astype(
        narrow
    )
    large_parts = projected[:split_at].reshape(large_count, large_rows, 3, heads, -1)
    large_query, large_key, large_value = (
        large_parts[:, :, 0],
        large_parts[:, :, 1],
        large_parts[:, :, 2],
    )
    large_index = lax.dynamic_slice_in_dim(index_large, first_key, large_rows, 0)
    large_bias = lookup(table_large, large_index)

    def forward_visit(step, state):
        return step(
            state,
            (
                lax.all_gather(large_key, "blk", axis=1, tiled=True),
                lax.all_gather(large_value, "blk", axis=1, tiled=True),
            ),
            jnp.int32(0),
        )

    def backward_visit(step, state):
        return step(
            state,
            (
                lax.all_gather(large_key, "blk", axis=1, tiled=True),
                lax.all_gather(large_value, "blk", axis=1, tiled=True),
            ),
            jnp.int32(0),
        )

    large_attended, large_log = forward_attention(
        large_query, large_bias, lengths_large, forward_visit
    )
    small_parts = projected[split_at:].reshape(small_count, small_rows, 3, heads, -1)
    small_query, small_key, small_value = (
        small_parts[:, :, 0],
        small_parts[:, :, 1],
        small_parts[:, :, 2],
    )
    small_bias = lookup(table_small, index_small)
    small_visit = local_fold((small_key, small_value))
    small_attended, small_log = forward_attention(
        small_query, small_bias, lengths_small, small_visit
    )
    attended_low = jnp.concatenate(
        [merge_heads(large_attended), merge_heads(small_attended)], 0
    ).astype(narrow)
    branch = jnp.dot(attended_low, proj_weight, preferred_element_type=wide) + proj_bias.astype(
        wide
    )
    middle = flat + attn_scale.astype(wide) * branch
    normed_mlp, mlp_norm_back = jax.vjp(
        layer_norm, middle, mlp_gain.astype(wide), mlp_shift.astype(wide)
    )
    normed_mlp_low = normed_mlp.astype(narrow)
    pre_act = jnp.dot(
        normed_mlp_low, inner_weight, preferred_element_type=wide
    ) + inner_bias.astype(wide)
    activated, gelu_back = jax.vjp(exact_gelu, pre_act)
    activated_low = activated.astype(narrow)
    outer = jnp.dot(activated_low, outer_weight, preferred_element_type=wide) + outer_bias.astype(
        wide
    )
    result_low = (middle + mlp_scale.astype(wide) * outer).astype(narrow)
    cotan = jnp.concatenate(
        [cotan_large.reshape(-1, width), cotan_small.reshape(-1, width)], 0
    ).astype(wide)
    grad_mlp_scale = jnp.sum(cotan * outer, 0)
    grad_outer = (mlp_scale.astype(wide) * cotan).astype(narrow)
    grad_outer_bias = jnp.sum(grad_outer.astype(wide), 0)
    grad_outer_weight = jnp.dot(activated_low.T, grad_outer, preferred_element_type=wide)
    grad_activated = jnp.dot(grad_outer, outer_weight.T, preferred_element_type=wide)
    grad_pre = gelu_back(grad_activated)[0].astype(narrow)
    grad_inner_bias = jnp.sum(grad_pre.astype(wide), 0)
    grad_inner_weight = jnp.dot(normed_mlp_low.T, grad_pre, preferred_element_type=wide)
    grad_normed_mlp = jnp.dot(grad_pre, inner_weight.T, preferred_element_type=wide)
    grad_middle_part, grad_mlp_gain, grad_mlp_shift = mlp_norm_back(grad_normed_mlp)
    grad_middle = cotan + grad_middle_part
    grad_attn_scale = jnp.sum(grad_middle * branch, 0)
    grad_branch = (attn_scale.astype(wide) * grad_middle).astype(narrow)
    grad_proj_bias = jnp.sum(grad_branch.astype(wide), 0)
    grad_proj_weight = jnp.dot(attended_low.T, grad_branch, preferred_element_type=wide)
    grad_attended = jnp.dot(grad_branch, proj_weight.T, preferred_element_type=wide).astype(narrow)
    large_grad_out = grad_attended[:split_at].reshape(large_count, large_rows, heads, -1)
    large_inner = jnp.einsum("iqhe,ihqe->ihq", large_grad_out.astype(wide), large_attended)
    large_grad_query, large_bias_full, key_full, value_full = key_pass(
        large_query,
        large_bias,
        lengths_large,
        large_grad_out,
        large_inner,
        large_log,
        backward_visit,
    )
    large_key_grad, large_value_grad = (
        lax.psum_scatter(
            key_full.astype(jnp.bfloat16), "blk", scatter_dimension=1, tiled=True
        ).astype(jnp.float32),
        lax.psum_scatter(
            value_full.astype(jnp.bfloat16), "blk", scatter_dimension=1, tiled=True
        ).astype(jnp.float32),
    )
    large_grads = jnp.stack(
        [jnp.transpose(large_grad_query, (0, 2, 1, 3)), large_key_grad, large_value_grad], 2
    ).reshape(split_at, 3 * width)
    large_table_grad = table_gradient(large_bias_full, large_index, table_large.shape[0])
    small_grad_out = grad_attended[split_at:].reshape(small_count, small_rows, heads, -1)
    small_inner = jnp.einsum("iqhe,ihqe->ihq", small_grad_out.astype(wide), small_attended)
    small_grad_query, small_bias_full, small_key_grad, small_value_grad = key_pass(
        small_query, small_bias, lengths_small, small_grad_out, small_inner, small_log, small_visit
    )
    small_grads = jnp.stack(
        [jnp.transpose(small_grad_query, (0, 2, 1, 3)), small_key_grad, small_value_grad], 2
    ).reshape(small_count * small_rows, 3 * width)
    small_table_grad = table_gradient(small_bias_full, index_small, table_small.shape[0])
    grad_projected = jnp.concatenate([large_grads, small_grads], 0).astype(narrow)
    grad_query_bias = jnp.sum(grad_projected[:, :width].astype(wide), 0)
    grad_value_bias = jnp.sum(grad_projected[:, 2 * width :].astype(wide), 0)
    grad_qkv_weight = jnp.dot(normed_low.T, grad_projected, preferred_element_type=wide)
    grad_normed = jnp.dot(grad_projected, qkv_weight.T, preferred_element_type=wide)
    grad_flat_part, grad_attn_gain, grad_attn_shift = attn_norm_back(grad_normed)
    grad_flat = (grad_middle + grad_flat_part).astype(narrow)
    summed = (
        lax.psum_scatter(grad_attn_gain, ("img", "blk"), scatter_dimension=0, tiled=True),
        lax.psum_scatter(grad_attn_shift, ("img", "blk"), scatter_dimension=0, tiled=True),
        lax.psum_scatter(grad_qkv_weight, ("img", "blk"), scatter_dimension=0, tiled=True),
        lax.psum_scatter(grad_query_bias, ("img", "blk"), scatter_dimension=0, tiled=True),
        lax.psum_scatter(grad_value_bias, ("img", "blk"), scatter_dimension=0, tiled=True),
        lax.psum_scatter(grad_proj_weight, ("img", "blk"), scatter_dimension=0, tiled=True),
        lax.psum_scatter(grad_proj_bias, ("img", "blk"), scatter_dimension=0, tiled=True),
        lax.psum_scatter(grad_attn_scale, ("img", "blk"), scatter_dimension=0, tiled=True),
        lax.psum_scatter(grad_mlp_gain, ("img", "blk"), scatter_dimension=0, tiled=True),
        lax.psum_scatter(grad_mlp_shift, ("img", "blk"), scatter_dimension=0, tiled=True),
        lax.psum_scatter(grad_inner_weight, ("img", "blk"), scatter_dimension=0, tiled=True),
        lax.psum_scatter(grad_inner_bias, ("img", "blk"), scatter_dimension=0, tiled=True),
        lax.psum_scatter(grad_outer_weight, ("img", "blk"), scatter_dimension=0, tiled=True),
        lax.psum_scatter(grad_outer_bias, ("img", "blk"), scatter_dimension=0, tiled=True),
        lax.psum_scatter(grad_mlp_scale, ("img", "blk"), scatter_dimension=0, tiled=True),
    )
    table_sum_large, table_sum_small = lax.psum(
        (large_table_grad, small_table_grad), ("img", "blk")
    )
    return (
        result_low[:split_at].reshape(large_count, large_rows, width),
        result_low[split_at:].reshape(small_count, small_rows, width),
        grad_flat[:split_at].reshape(large_count, large_rows, width),
        grad_flat[split_at:].reshape(small_count, small_rows, width),
        summed[0],
        summed[1],
        summed[2],
        summed[3],
        summed[4],
        table_sum_large,
        table_sum_small,
        summed[5],
        summed[6],
        summed[7],
        summed[8],
        summed[9],
        summed[10],
        summed[11],
        summed[12],
        summed[13],
        summed[14],
    )


NT = (((1,), (1,)), ((), ()))
TN = (((0,), (0,)), ((), ()))
WIDE = jnp.float32
NARROW = jnp.bfloat16
LANES = 128
TERM = jnp.float8_e4m3fn
MEGA = 1 << 20


def round_up(count, step):
    return -(-count // step) * step


def params(limit, *names):
    return pltpu.CompilerParams(vmem_limit_bytes=limit * MEGA, dimension_semantics=("arbitrary",))


def cost(micros):
    return pl.CostEstimate(flops=int(micros * 1.15e9), bytes_accessed=int(micros * 3.2e6), transcendentals=0)


def whole(*shape):
    return pl.BlockSpec(shape, lambda *steps: (0,) * len(shape), pipeline_mode=pl.Buffered(1))


def whole_of(value):
    return whole(*value.shape)


BLK, CORE = 0, 1


def assemble(held_ref, me, part, mine, gots, small_ref, large, small):
    held_ref[...] = jnp.zeros_like(held_ref)
    size = len(gots) + 1
    for shift, piece in enumerate([mine] + [got[...] for got in gots]):
        start = pl.multiple_of(lax.rem(me + (size - shift), size) * part, 8)
        held_ref[pl.ds(start, piece.shape[0]), :] = piece.astype(WIDE)
    for number in range(small_ref.shape[0]):
        start = large + number * small
        held_ref[start : start + small_ref.shape[1], :] = small_ref[number].astype(WIDE)


def dismantle(held_ref, me, part, piece_refs, small_ref, large):
    size = len(piece_refs)
    for shift, piece_ref in enumerate(piece_refs):
        start = pl.multiple_of(lax.rem(me + shift, size) * part, 8)
        piece_ref[...] = held_ref[pl.ds(start, part), :].astype(NARROW)
    small_ref[...] = held_ref[large:, :].astype(NARROW)


def deal_rows(value, half, is_first, mine_ref, theirs_ref):
    for number in range(value.shape[0] // (2 * half)):
        start = 2 * half * number
        first, second = value[start : start + half], value[start + half : start + 2 * half]
        rows = slice(half * number, half * number + half)
        mine_ref[rows, :] = jnp.where(is_first, first, second)
        theirs_ref[rows, :] = jnp.where(is_first, second, first)


def row_norm(values):
    center = values - jnp.mean(values, -1, keepdims=True)
    spread = jnp.mean(center * center, -1, keepdims=True)
    inverse = lax.rsqrt(spread + EPSILON)
    return center * inverse, inverse


def norm_backward(grad, normal, inverse, gain):
    scaled = grad * gain
    first = jnp.mean(scaled, -1, keepdims=True)
    second = jnp.mean(scaled * normal, -1, keepdims=True)
    return inverse * (scaled - first - normal * second)


def bias_kernel(heads, groups, place_ref, table_ref, index_ref, out_ref):
    rows = index_ref.shape[0]
    for first in range(0, rows, 16):
        found = []
        for half in (0, 8):
            index = index_ref[first + half : first + half + 8, :]
            low = lax.bitwise_and(index, LANES - 1)
            high = lax.shift_right_logical(index, 7)
            picked = [None] * heads
            for group in range(groups):
                here = high == group
                for head in range(heads):
                    value = jnp.take_along_axis(table_ref[group * heads + head], low, axis=1)
                    picked[head] = value if group == 0 else jnp.where(here, value, picked[head])
            found.append(picked)
        for head in range(heads):
            both = jnp.concatenate([found[0][head], found[1][head]], 0)
            out_ref[head, first : first + 16, :] = both.astype(NARROW)


def spread_kernel(pieces, length, piece, index_ref, out_ref):
    out_ref[...] = jnp.zeros_like(out_ref)
    turned = jnp.transpose(index_ref[...])
    for key in range(pieces):
        for query in range(pieces):
            out_ref[key * piece : key * piece + length, query * piece : query * piece + length] = turned[
                key * length : (key + 1) * length, query * length : (query + 1) * length
            ]


def spread_index(index, pieces, piece, rows, lanes):
    length = index.shape[0] // pieces
    return pl.pallas_call(
        functools.partial(spread_kernel, pieces, length, piece),
        out_shape=jax.ShapeDtypeStruct((rows, lanes), jnp.int32),
        compiler_params=pltpu.CompilerParams(vmem_limit_bytes=32 * MEGA),
        cost_estimate=cost(rows * lanes * 1e-5),
        name="spread_index",
    )(index)


def bias_lookup(place, table, index, shares):
    heads = table.shape[1]
    groups = round_up(table.shape[0], LANES) // LANES
    table = jnp.pad(table.astype(WIDE), ((0, groups * LANES - table.shape[0]), (0, 0)))
    table = jnp.transpose(table.reshape(groups, LANES, heads), (0, 2, 1)).reshape(-1, 1, LANES)
    table = jnp.broadcast_to(table, (groups * heads, 8, LANES))
    rows, lanes = index.shape
    rows //= shares
    return pl.pallas_call(
        functools.partial(bias_kernel, heads, groups),
        grid_spec=pltpu.PrefetchScalarGridSpec(
            num_scalar_prefetch=1,
            grid=(lanes // LANES,),
            in_specs=[
                pl.BlockSpec((groups * heads, 8, LANES), lambda i, place: (0, 0, 0)),
                pl.BlockSpec((rows, LANES), lambda i, place: (place[CORE] if shares > 1 else 0, i)),
            ],
            out_specs=pl.BlockSpec((heads, rows, LANES), lambda i, place: (0, 0, i)),
        ),
        out_shape=jax.ShapeDtypeStruct((heads, rows, lanes), NARROW),
        compiler_params=params(32),
        cost_estimate=cost(rows * lanes * groups * heads * 6e-7),
        name="bias_lookup",
    )(place, table, index)


def qkv_kernel(
    part,
    large,
    small,
    gots,
    place_ref,
    mine_ref,
    *refs,
):
    got_refs = refs[:gots]
    small_ref, gain_ref, shift_ref, weight_ref, bias_ref, x_ref, h_ref, p_ref, held_ref = refs[gots:]

    @pl.when(pl.program_id(0) == 0)
    def _():
        assemble(held_ref, place_ref[BLK], part, mine_ref[...], got_refs, small_ref, large, small)
        x = held_ref[...]
        x_ref[...] = x.astype(NARROW)
        normal, _ = row_norm(x)
        h_ref[...] = (normal * gain_ref[...] + shift_ref[...]).astype(NARROW)

    product = jnp.dot(h_ref[...], weight_ref[...], preferred_element_type=WIDE)
    p_ref[...] = (product + bias_ref[...]).astype(NARROW)


def qkv_forward(place, pieces, gots, smalls, gain, shift, weight, bias, part, large, small):
    width = smalls.shape[2]
    tokens = large + smalls.shape[0] * small
    total = weight.shape[1]
    return pl.pallas_call(
        functools.partial(qkv_kernel, part, large, small, len(gots)),
        grid_spec=pltpu.PrefetchScalarGridSpec(
            num_scalar_prefetch=1,
            grid=(total // width,),
            in_specs=[pl.BlockSpec((None,) + pieces.shape[1:], lambda i, place: (place[BLK], 0, 0))]
            + [whole_of(got) for got in gots]
            + [
                whole_of(smalls),
                whole(1, width),
                whole(1, width),
                pl.BlockSpec((width, width), lambda i, place: (0, i)),
                pl.BlockSpec((1, width), lambda i, place: (0, i)),
            ],
            out_specs=[
                whole(tokens, width),
                whole(tokens, width),
                pl.BlockSpec((tokens, width), lambda i, place: (0, i)),
            ],
            scratch_shapes=[pltpu.VMEM((tokens, width), WIDE)],
        ),
        out_shape=[
            jax.ShapeDtypeStruct((tokens, width), NARROW),
            jax.ShapeDtypeStruct((tokens, width), NARROW),
            jax.ShapeDtypeStruct((tokens, total), NARROW),
        ],
        compiler_params=params(48),
        cost_estimate=cost(tokens * width * total * 5e-9),
        name="qkv_forward",
    )(place, pieces, *gots, smalls, gain, shift, weight, bias)


def head_parts(first_half, value, other):
    return jnp.where(first_half, value, other), jnp.where(first_half, other, value)


def attention_forward_kernel(
    images,
    place_ref,
    q_ref,
    k_ref,
    v_ref,
    mask_ref,
    own_bias_ref,
    other_bias_ref,
    small_bias_ref,
    o_ref,
    large_p_ref,
    small_p_ref,
):
    is_first = place_ref[CORE] == 0
    lane = lax.broadcasted_iota(jnp.int32, (1, LANES), 1)
    first_half = lane < HEAD
    for number, (start, rows) in enumerate(images):
        here = slice(start, start + rows)
        query = q_ref[here, :] * jnp.asarray(HEAD ** (-0.5), NARROW)
        ones = jnp.where(lane % HEAD == 0, 1.0, 0.0).astype(NARROW)
        ones = jnp.broadcast_to(ones, query.shape)
        queries = head_parts(first_half, query, ones)
        keys = head_parts(first_half, k_ref[here, :], mask_ref[here, :])
        value = v_ref[here, :]
        outs = []
        for head in range(2):
            if number == 0:
                own, other = own_bias_ref[head, :, :rows], other_bias_ref[head, :, :rows]
                bias = jnp.concatenate([jnp.where(is_first, own, other), jnp.where(is_first, other, own)], 0)
            else:
                bias = small_bias_ref[head, :rows, :rows]
            scores = lax.dot_general(keys[head], queries[head], NT, preferred_element_type=WIDE)
            scores = scores + bias.astype(WIDE)
            weights = jnp.exp(scores - jnp.max(scores, 0, keepdims=True))
            probs = (weights * (1.0 / jnp.sum(weights, 0, keepdims=True))).astype(NARROW)
            if number == 0:
                large_p_ref[head] = probs
            else:
                small_p_ref[head, number - 1] = probs
            outs.append(lax.dot_general(probs, value, TN, preferred_element_type=WIDE))
        o_ref[here, :] = jnp.where(first_half, outs[0], outs[1]).astype(NARROW)


def attention_forward(place, p, mask, own_bias, other_bias, small_bias, images):
    tokens = p.shape[0]
    heads = small_bias.shape[0]
    pairs = heads // 2
    large, small, smalls = images[0][1], images[1][1], len(images) - 1
    area = large * large + smalls * small * small

    def column(offset):
        return pl.BlockSpec((tokens, LANES), lambda i, place: (0, offset + i))

    def by_pair(*shape):
        return pl.BlockSpec((2,) + shape, lambda i, place: (i,) + (0,) * len(shape))

    return pl.pallas_call(
        functools.partial(attention_forward_kernel, images),
        grid_spec=pltpu.PrefetchScalarGridSpec(
            num_scalar_prefetch=1,
            grid=(pairs,),
            in_specs=[
                column(0),
                column(pairs),
                column(2 * pairs),
                pl.BlockSpec((tokens, LANES), lambda i, place: (0, 0)),
                by_pair(*own_bias.shape[1:]),
                by_pair(*other_bias.shape[1:]),
                by_pair(*small_bias.shape[1:]),
            ],
            out_specs=[
                column(0),
                by_pair(large, large),
                by_pair(smalls, small, small),
            ],
        ),
        out_shape=[
            jax.ShapeDtypeStruct((tokens, heads * HEAD), NARROW),
            jax.ShapeDtypeStruct((heads, large, large), NARROW),
            jax.ShapeDtypeStruct((heads, smalls, small, small), NARROW),
        ],
        compiler_params=params(60),
        cost_estimate=cost(heads * area * 3.8e-6),
        name="attention_forward",
    )(place, p, p, p, mask, own_bias, other_bias, small_bias)


def attention_backward_kernel(
    images,
    place_ref,
    q_ref,
    k_ref,
    v_ref,
    do_ref,
    o_ref,
    large_p_ref,
    small_p_ref,
    dp_ref,
    mine_ref,
    theirs_ref,
):
    is_first = place_ref[CORE] == 0
    mine_ref[...] = jnp.zeros_like(mine_ref)
    theirs_ref[...] = jnp.zeros_like(theirs_ref)
    large_half = images[0][1] // 2

    def deal(head, grad_scores, start, half):
        count, lanes = grad_scores.shape
        lower = grad_scores[:half]
        upper = grad_scores[half:]
        rest = count - half
        rows = slice(start, start + rest)
        mine_ref[head, rows, :lanes] = jnp.where(is_first, lower[:rest], upper)
        theirs_ref[head, rows, :lanes] = jnp.where(is_first, upper, lower[:rest])
        if rest < half:
            zeros = jnp.zeros((half - rest, lanes), NARROW)
            rows = slice(start + rest, start + half)
            mine_ref[head, rows, :lanes] = jnp.where(is_first, lower[rest:], zeros)
            theirs_ref[head, rows, :lanes] = jnp.where(is_first, zeros, lower[rest:])

    lane = lax.broadcasted_iota(jnp.int32, (1, LANES), 1)
    first_half = lane < HEAD
    small_sum = [None, None]
    scale = HEAD ** (-0.5)
    for number, (start, rows) in enumerate(images):
        here = slice(start, start + rows)
        query = q_ref[here, :] * jnp.asarray(scale, NARROW)
        key = k_ref[here, :]
        value = v_ref[here, :]
        grad = do_ref[here, :]
        product = jnp.transpose(grad.astype(WIDE) * o_ref[here, :].astype(WIDE))
        grads = head_parts(first_half, grad, jnp.zeros_like(grad))
        parts = []
        for head in range(2):
            inner = jnp.sum(product[head * HEAD : (head + 1) * HEAD], 0, keepdims=True)
            probs = large_p_ref[head] if number == 0 else small_p_ref[head, number - 1]
            grad_probs = lax.dot_general(value, grads[head], NT, preferred_element_type=WIDE)
            grad_scores = (probs.astype(WIDE) * (grad_probs - inner)).astype(NARROW)
            if number == 0:
                deal(head, grad_scores, 0, large_half)
            elif small_sum[head] is None:
                small_sum[head] = grad_scores.astype(WIDE)
            else:
                small_sum[head] = small_sum[head] + grad_scores.astype(WIDE)
            parts.append(
                (
                    lax.dot_general(grad_scores, key, TN, preferred_element_type=WIDE) * scale,
                    jnp.dot(grad_scores, query, preferred_element_type=WIDE),
                    jnp.dot(probs, grad, preferred_element_type=WIDE),
                )
            )
        for which in range(3):
            dp_ref[which, here, :] = jnp.where(first_half, parts[0][which], parts[1][which]).astype(NARROW)
    for head in range(2):
        deal(head, small_sum[head].astype(NARROW), large_half, mine_ref.shape[1] - large_half)


def attention_backward(place, p, grad_out, out, large_p, small_p, images, share, first, count):
    tokens = p.shape[0]
    pairs = large_p.shape[0] // 2
    large, small, smalls = images[0][1], images[1][1], len(images) - 1
    area = large * large + smalls * small * small

    def column(offset):
        return pl.BlockSpec((tokens, LANES), lambda i, place: (0, offset + first + i))

    def by_pair(*shape):
        return pl.BlockSpec((2,) + shape, lambda i, place: (first + i,) + (0,) * len(shape))

    share_spec = pl.BlockSpec((2,) + share, lambda i, place: (i, 0, 0))
    return pl.pallas_call(
        functools.partial(attention_backward_kernel, images),
        grid_spec=pltpu.PrefetchScalarGridSpec(
            num_scalar_prefetch=1,
            grid=(count,),
            in_specs=[
                column(0),
                column(pairs),
                column(2 * pairs),
                column(0),
                column(0),
                by_pair(large, large),
                by_pair(smalls, small, small),
            ],
            out_specs=[pl.BlockSpec((3, tokens, LANES), lambda i, place: (0, 0, i)), share_spec, share_spec],
        ),
        out_shape=[jax.ShapeDtypeStruct((3, tokens, count * LANES), NARROW)]
        + [jax.ShapeDtypeStruct((2 * count,) + share, NARROW)] * 2,
        compiler_params=params(60),
        cost_estimate=cost(2 * count * area * 4.2e-6),
        name="attention_backward",
    )(place, p, p, p, grad_out, out, large_p, small_p)


def gelu_parts(value):
    size = jnp.abs(value)
    inverse = 1.0 / (1.0 + (0.3275911 * 0.7071067811865476) * size)
    series = inverse * (
        0.127414796
        + inverse
        * (-0.142248368 + inverse * (0.7107068705 + inverse * (-0.7265760135 + inverse * 0.5307027145)))
    )
    bell = jnp.exp(-0.5 * value * value)
    tail = series * bell
    share = jnp.where(value < 0, tail, 1.0 - tail)
    return value * share, share + value * (bell * 0.3989422804014327)


def mlp_kernel(
    part,
    large,
    small,
    share,
    gots,
    place_ref,
    mine_ref,
    *refs,
):
    got_refs, refs = refs[:gots], refs[gots:]
    small_ref, o_ref, x_ref, proj_ref, vector_ref, inner_ref, inner_bias_ref, outer_ref = refs[:8]
    back_refs, refs = refs[8 : 9 + gots], refs[9 + gots :]
    small_back_ref, dm_ref, do_ref, weights_ref, dvector_ref, dbias_ref = refs[:6]
    r_ref, g_ref, dy_ref, dz_ref, z_ref, dg_ref, wide_ref, tall_ref, sems = refs[6:]
    step = pl.program_id(0)
    steps = pl.num_programs(0) - 1
    me = place_ref[BLK]
    proj_bias, attn_scale, gain, shift, outer_bias, mlp_scale = (vector_ref[i : i + 1, :] for i in range(6))
    tokens = x_ref.shape[0]
    chunk = next(c for c in (128, 64, 32, 16) if tokens % c == 0)
    width = x_ref.shape[1]
    pieces = tall_ref.shape[1] // width

    def wide_copy(number):
        columns = pl.ds(pl.multiple_of(number * width, LANES), width)
        return pltpu.make_async_copy(wide_ref, weights_ref.at[:, columns], sems.at[0])

    def tall_copy(number):
        count = tall_ref.shape[0]
        rows = pl.ds(pl.multiple_of(number * count, 16), count)
        columns = slice(weights_ref.shape[1] - tall_ref.shape[1], weights_ref.shape[1])
        return pltpu.make_async_copy(tall_ref, weights_ref.at[rows, columns], sems.at[1])

    @pl.when(step == 0)
    def _():
        r_ref[...] = jnp.dot(o_ref[...], proj_ref[...], preferred_element_type=WIDE) + proj_bias
        assemble(z_ref, me, part, mine_ref[...], got_refs, small_ref, large, small)

        @pl.loop(0, tokens // chunk)
        def _(i):
            rows = pl.ds(pl.multiple_of(i * chunk, chunk), chunk)
            middle = x_ref[rows, :].astype(WIDE) + attn_scale * r_ref[rows, :]
            normal, _ = row_norm(middle)
            g_ref[rows, :] = (normal * gain + shift).astype(NARROW)
            dy = z_ref[rows, :]
            dy_ref[rows, :] = dy.astype(NARROW)
            dz_ref[rows, :] = (mlp_scale * dy).astype(NARROW)

    @pl.when(step < pl.num_programs(0) - 1)
    def _():
        pre = jnp.dot(g_ref[...], inner_ref[...], preferred_element_type=WIDE) + inner_bias_ref[...]
        active, slope = gelu_parts(pre)
        active = active.astype(NARROW)
        dz = dz_ref[...]
        dactive = lax.dot_general(dz, outer_ref[...], NT, preferred_element_type=WIDE)
        dpre = (dactive * slope).astype(NARROW)
        douter = lax.dot_general(active, dz, TN, preferred_element_type=WIDE)
        dinner = lax.dot_general(g_ref[...], dpre, TN, preferred_element_type=WIDE).astype(NARROW)

        @pl.when(step > 0)
        def _():
            wide_copy(step - 1).wait()
            tall_copy(step - 1).wait()

        wide_ref[...] = dinner
        wide_copy(step).start()
        douter = douter.reshape(-1, pieces, share, width)
        for piece in range(pieces):
            tall_ref[:, piece * width : (piece + 1) * width] = (
                douter[:, piece].reshape(tall_ref.shape[0], width).astype(NARROW)
            )
        tall_copy(step).start()
        dbias_ref[...] = jnp.sum(dpre.astype(WIDE), 0, keepdims=True)
        z = jnp.dot(active, outer_ref[...], preferred_element_type=WIDE)
        dg = lax.dot_general(dpre, inner_ref[...], NT, preferred_element_type=WIDE)

        @pl.when(step == 0)
        def _():
            z_ref[...] = z
            dg_ref[...] = dg

        @pl.when(step > 0)
        def _():
            z_ref[...] += z
            dg_ref[...] += dg

    @pl.when(step == pl.num_programs(0) - 1)
    def _():
        dvector_ref[...] = jnp.zeros_like(dvector_ref)

        @pl.loop(0, tokens // chunk)
        def _(i):
            rows = pl.ds(pl.multiple_of(i * chunk, chunk), chunk)
            branch = r_ref[rows, :]
            middle = x_ref[rows, :].astype(WIDE) + attn_scale * branch
            normal, inverse = row_norm(middle)
            outer = z_ref[rows, :] + outer_bias
            dy = dy_ref[rows, :].astype(WIDE)
            r_ref[rows, :] = middle + mlp_scale * outer
            grad = dg_ref[rows, :]
            dm = dy + norm_backward(grad, normal, inverse, gain)
            dm_ref[rows, :] = dm
            dr = (attn_scale * dm).astype(NARROW)
            g_ref[rows, :] = dr
            sums = [
                dy * outer,
                dz_ref[rows, :].astype(WIDE),
                grad * normal,
                grad,
                dm * branch,
                dr.astype(WIDE),
            ]
            for place, term in enumerate(sums):
                dvector_ref[place : place + 1, :] += jnp.sum(term, 0, keepdims=True)

        dr = g_ref[...]
        dproj = lax.dot_general(o_ref[...], dr, TN, preferred_element_type=WIDE).astype(NARROW)
        wide_copy(steps - 1).wait()
        tall_copy(steps - 1).wait()
        wide_ref[...] = dproj
        wide_copy(steps).start()
        do_ref[...] = lax.dot_general(dr, proj_ref[...], NT, preferred_element_type=WIDE).astype(NARROW)
        dismantle(r_ref, me, part, back_refs, small_back_ref, large)
        wide_copy(steps).wait()


def mlp_pass(place, pieces, gots, smalls, out, x, proj, vectors, inner, inner_bias, outer, part, large, small, devices):
    tokens, width = x.shape
    hidden = inner.shape[1]
    steps = hidden // width
    blk = len(gots) + 1
    share = width // devices
    tall = steps * width

    def feed(i):
        return jnp.minimum(i, steps - 1)

    shapes = [jax.ShapeDtypeStruct((part, width), NARROW)] * blk + [
        jax.ShapeDtypeStruct((tokens - large, width), NARROW),
        jax.ShapeDtypeStruct((tokens, width), WIDE),
        jax.ShapeDtypeStruct((tokens, width), NARROW),
        jax.ShapeDtypeStruct((width, hidden + width + tall), NARROW),
        jax.ShapeDtypeStruct((8, width), WIDE),
        jax.ShapeDtypeStruct((1, hidden), WIDE),
    ]
    return pl.pallas_call(
        functools.partial(mlp_kernel, part, large, small, share, len(gots)),
        grid_spec=pltpu.PrefetchScalarGridSpec(
            num_scalar_prefetch=1,
            grid=(steps + 1,),
            in_specs=[
                pl.BlockSpec(
                    (None,) + pieces.shape[1:],
                    lambda i, place: (place[BLK], 0, 0),
                    pipeline_mode=pl.Buffered(1),
                )
            ]
            + [whole_of(got) for got in gots]
            + [
                whole_of(smalls),
                whole(tokens, width),
                whole(tokens, width),
                whole(width, width),
                whole(8, width),
                pl.BlockSpec((width, width), lambda i, place: (0, feed(i))),
                pl.BlockSpec((1, width), lambda i, place: (0, feed(i))),
                pl.BlockSpec((width, width), lambda i, place: (feed(i), 0)),
            ],
            out_specs=[whole(part, width)] * blk
            + [
                whole(tokens - large, width),
                whole(tokens, width),
                whole(tokens, width),
                pl.BlockSpec(memory_space=pl.ANY),
                whole(8, width),
                pl.BlockSpec((1, width), lambda i, place: (0, feed(i))),
            ],
            scratch_shapes=[
                pltpu.VMEM((tokens, width), WIDE),
                pltpu.VMEM((tokens, width), NARROW),
                pltpu.VMEM((tokens, width), NARROW),
                pltpu.VMEM((tokens, width), NARROW),
                pltpu.VMEM((tokens, width), WIDE),
                pltpu.VMEM((tokens, width), WIDE),
                pltpu.VMEM((width, width), NARROW),
                pltpu.VMEM((width // steps, tall), NARROW),
                pltpu.SemaphoreType.DMA((2,)),
            ],
        ),
        out_shape=shapes,
        compiler_params=params(60),
        cost_estimate=cost(tokens * width * hidden * 2.4e-8),
        name="mlp_pass",
    )(place, pieces, *gots, smalls, out, x, proj, vectors, inner, inner_bias, outer)


def qkv_backward_kernel(part, large, half, pieces, place_ref, *refs):
    result_refs, refs = refs[:pieces], refs[pieces:]
    dp_ref, h_ref, x_ref, dm_ref, gain_ref, weight_ref, mine_ref, theirs_ref = refs[:8]
    back_refs = refs[8 : 8 + pieces]
    small_back_ref, dvector_ref, dh_ref = refs[8 + pieces :]
    step = pl.program_id(0)
    grad = dp_ref[0]
    dweight = lax.dot_general(h_ref[...], grad, TN, preferred_element_type=WIDE).astype(NARROW)
    deal_rows(dweight, half, place_ref[CORE] == 0, mine_ref, theirs_ref)
    term = lax.dot_general(grad, weight_ref[...], NT, preferred_element_type=WIDE)
    column_sum = jnp.sum(grad.astype(WIDE), 0, keepdims=True)
    tokens = x_ref.shape[0]
    chunk = next(c for c in (128, 64, 32, 16) if tokens % c == 0)

    @pl.when(step == 0)
    def _():
        dvector_ref[...] = jnp.zeros_like(dvector_ref)
        dh_ref[...] = term
        dvector_ref[0:1, :] = column_sum

    @pl.when(step > 0)
    def _():
        dh_ref[...] += term

    @pl.when(step == pl.num_programs(0) - 1)
    def _():
        dvector_ref[1:2, :] = column_sum

        @pl.loop(0, tokens // chunk)
        def _(i):
            rows = pl.ds(pl.multiple_of(i * chunk, chunk), chunk)
            normal, inverse = row_norm(x_ref[rows, :].astype(WIDE))
            dh = dh_ref[rows, :]
            dh_ref[rows, :] = dm_ref[rows, :] + norm_backward(dh, normal, inverse, gain_ref[...])
            dvector_ref[2:3, :] += jnp.sum(dh * normal, 0, keepdims=True)
            dvector_ref[3:4, :] += jnp.sum(dh, 0, keepdims=True)

        for back_ref, result_ref in zip(back_refs, result_refs):
            back_ref[0] = result_ref[...]
        dismantle(dh_ref, place_ref[BLK], part, [back_ref.at[1] for back_ref in back_refs], small_back_ref, large)


def qkv_backward(place, results, dp, h, x, dm, gain, weight, part, large, devices):
    blk = len(results)
    tokens, width = x.shape
    half_spec = pl.BlockSpec((width // 2, width), lambda i, place: (0, i))
    return pl.pallas_call(
        functools.partial(qkv_backward_kernel, part, large, blk * width // devices, blk),
        grid_spec=pltpu.PrefetchScalarGridSpec(
            num_scalar_prefetch=1,
            grid=(3,),
            in_specs=[whole_of(result) for result in results]
            + [
                pl.BlockSpec((1, tokens, width), lambda i, place: (i, 0, 0)),
                whole(tokens, width),
                whole(tokens, width),
                whole(tokens, width),
                whole(1, width),
                pl.BlockSpec((width, width), lambda i, place: (0, i)),
            ],
            out_specs=[half_spec, half_spec]
            + [whole(2, part, width)] * blk
            + [whole(tokens - large, width), whole(8, width)],
            scratch_shapes=[pltpu.VMEM((tokens, width), WIDE)],
        ),
        out_shape=[jax.ShapeDtypeStruct((width // 2, 3 * width), NARROW)] * 2
        + [jax.ShapeDtypeStruct((2, part, width), NARROW)] * blk
        + [
            jax.ShapeDtypeStruct((tokens - large, width), NARROW),
            jax.ShapeDtypeStruct((8, width), WIDE),
        ],
        compiler_params=params(48),
        cost_estimate=cost(tokens * width * width * 2.5e-8),
        name="qkv_backward",
    )(place, *results, dp, h, x, dm, gain, weight)


def place_kernel(rows, small, smalls, pieces, place_ref, *refs):
    backs, refs = refs[:pieces], refs[pieces:]
    still, outs = refs[:2], refs[2:]
    me = place_ref[BLK]
    for which in range(2):
        for shift in range(pieces):
            source = lax.rem(me + (pieces - shift), pieces)
            outs[2 * which][pl.ds(source, 1)] = backs[shift][which, :rows, :][None]
        for number in range(smalls):
            out_ref = outs[2 * which + 1]
            out_ref[number] = still[which][number * small : number * small + out_ref.shape[1], :]


def place_results(place, backs, still, rows, small, smalls, small_rows):
    width = still[0].shape[1]
    pieces = len(backs)
    shapes = [(pieces, rows, width), (smalls, small_rows, width)] * 2
    return pl.pallas_call(
        functools.partial(place_kernel, rows, small, smalls, pieces),
        grid_spec=pltpu.PrefetchScalarGridSpec(
            num_scalar_prefetch=1,
            grid=(1,),
            in_specs=[whole_of(value) for value in backs + still],
            out_specs=[whole(*shape) for shape in shapes],
        ),
        out_shape=[jax.ShapeDtypeStruct(shape, NARROW) for shape in shapes],
        compiler_params=params(32),
        cost_estimate=cost(3),
        name="place_results",
    )(place, *backs, *still)


TABLE_LANES = 256


def table_rows(shares, index_ref, out_ref, turned_ref, left_ref, right_ref, batch):
    rows, lanes = index_ref.shape
    groups = out_ref.shape[0] // 32
    top = jnp.zeros((8, lanes), WIDE)
    head = 0
    for own_ref, other_ref in shares:
        for number in range(own_ref.shape[0]):
            value = own_ref[number].astype(WIDE) + other_ref[number].astype(WIDE)
            turned_ref[:, head, :lanes] = value
            size = jnp.abs(value)
            for first in range(0, rows, 8):
                top = jnp.maximum(top, size[first : first + 8])
            head += 1
    peak = jnp.maximum(jnp.max(top, keepdims=True), 1e-30)
    scale = 256.0 / peak
    back = peak * (1.0 / 256.0)
    zero = jnp.zeros((), TERM)
    one = jnp.ones((), TERM)
    codes = (lax.broadcasted_iota(jnp.int32, (TABLE_LANES, LANES), 0) - 128).astype(jnp.int8)
    columns = slice(0, batch * lanes)

    def some_rows(part, carry):
        for within in range(batch):
            row = part * batch + within
            index = index_ref[pl.ds(row, 1), :]
            low = lax.bitwise_and(index, TABLE_LANES - 1) - 128
            high = lax.shift_right_logical(index, 8)
            for first in range(0, lanes, LANES):
                here = slice(first, first + LANES)
                there = slice(within * lanes + first, within * lanes + first + LANES)
                chosen = jnp.broadcast_to(low[:, here], (TABLE_LANES, LANES)).astype(jnp.int8)
                right_ref[:, there] = jnp.where(codes == chosen, one, zero)
                value = turned_ref[row, :, here] * scale
                upper = value.astype(TERM)
                lower = ((value - upper.astype(WIDE)) * 16.0).astype(TERM)
                both = jnp.concatenate([upper, lower], 0)
                wide_high = jnp.broadcast_to(high[:, here], both.shape).astype(jnp.int8)
                for group in range(groups):
                    left_ref[group * 32 : group * 32 + 32, there] = jnp.where(
                        wide_high == jnp.int8(group), both, zero
                    )
        left = left_ref[: groups * 32, columns]
        term = lax.dot_general(left, right_ref[:, columns], NT, preferred_element_type=WIDE)
        out_ref[...] += term * back
        return carry

    lax.fori_loop(0, rows // batch, some_rows, 0)


def table_jobs(counts, batch, ins, outs, turned_ref, left_ref, right_ref):
    step = pl.program_id(0)
    start = 0
    for job, count in enumerate(counts):
        own_ref, other_ref, index_ref = ins[3 * job : 3 * job + 3]

        @pl.when((step >= start) & (step < start + count))
        def _():
            table_rows([(own_ref, other_ref)], index_ref, outs[job], turned_ref, left_ref, right_ref, batch)

        start += count


def table_kernel(counts, batch, place_ref, *refs):
    ins, outs, scratch = refs[: 3 * len(counts)], refs[3 * len(counts) : 4 * len(counts)], refs[4 * len(counts) :]

    @pl.when(pl.program_id(0) == 0)
    def _():
        scratch[0][...] = jnp.zeros_like(scratch[0])
        for out_ref in outs:
            out_ref[...] = jnp.zeros_like(out_ref)

    table_jobs(counts, batch, ins, outs, *scratch)


def joined_terms(value):
    value = value.reshape(-1, 2, 16, TABLE_LANES)
    return (value[:, 0] + value[:, 1] * (1 / 16)).reshape(-1, TABLE_LANES)


def table_last_kernel(counts, batch, place_ref, *refs):
    own_ref, other_ref, index_ref, large_ref, small_ref, vector_ref, mine_ref, theirs_ref = refs[:8]
    total_ref, scratch = refs[8], refs[9:]

    @pl.when(pl.program_id(0) == 0)
    def _():
        scratch[0][...] = jnp.zeros_like(scratch[0])
        total_ref[...] = large_ref[...]

    table_jobs(counts, batch, (own_ref, other_ref, index_ref), [total_ref], *scratch)

    @pl.when(pl.program_id(0) == pl.num_programs(0) - 1)
    def _():
        rows = [joined_terms(total_ref[...]), joined_terms(small_ref[...]), vector_ref[...]]
        rows = jnp.concatenate(rows, 0).astype(NARROW).astype(WIDE)
        half = rows.shape[0] // 2
        is_first = place_ref[CORE] == 0
        mine_ref[...] = jnp.where(is_first, rows[:half], rows[half:]).astype(NARROW)
        theirs_ref[...] = jnp.where(is_first, rows[half:], rows[:half]).astype(NARROW)


def table_gradient_sum(place, own, other, jobs, last=None):
    step, batch = 16, 8
    heads = own.shape[0]
    in_specs, args = [], []
    lanes = [index.shape[1] for index, *_ in jobs]
    groups = [round_up(rows, TABLE_LANES) // TABLE_LANES for _, rows, *_ in jobs]
    counts = [job[-1] for job in jobs]
    start = 0
    for (index, _, share_first, index_first, count), width in zip(jobs, lanes):
        total = index.shape[0] // 2 // step

        def local(i, start=start, count=count):
            return jnp.clip(i - start, 0, count - 1)

        for value in (own, other):
            in_specs.append(
                pl.BlockSpec(
                    (heads, step, width),
                    lambda i, place, local=local, first=share_first: (0, first + local(i), 0),
                )
            )
        in_specs.append(
            pl.BlockSpec(
                (step, width),
                lambda i, place, local=local, first=index_first, total=total: (
                    first + local(i) + place[CORE] * total,
                    0,
                ),
            )
        )
        args += [own, other, index]
        start += count
    scratch = [
        pltpu.VMEM((step, 16, max(lanes)), WIDE),
        pltpu.VMEM((max(groups) * 32, batch * max(lanes)), TERM),
        pltpu.VMEM((TABLE_LANES, batch * max(lanes)), TERM),
    ]
    if last is None:
        kernel = table_kernel
        out_shape = [jax.ShapeDtypeStruct((group * 32, TABLE_LANES), WIDE) for group in groups]
    else:
        kernel = table_last_kernel
        in_specs += [whole_of(value) for value in last]
        args += last
        rows = last[0].shape[0] // 2 + last[1].shape[0] // 2 + last[2].shape[0]
        out_shape = [jax.ShapeDtypeStruct((rows // 2, TABLE_LANES), NARROW)] * 2
        scratch.insert(0, pltpu.VMEM(last[0].shape, WIDE))
    return pl.pallas_call(
        functools.partial(kernel, counts, batch),
        grid_spec=pltpu.PrefetchScalarGridSpec(
            num_scalar_prefetch=1,
            grid=(start,),
            in_specs=in_specs,
            out_specs=[whole_of(value) for value in out_shape],
            scratch_shapes=scratch,
        ),
        out_shape=out_shape,
        compiler_params=params(48),
        cost_estimate=cost(start * step * max(lanes) * 1.6e-4),
        name="table_gradient",
    )(place, *args)


def rotate(value, axis, size, shift):
    return lax.ppermute(value, axis, [(i, (i + shift) % size) for i in range(size)])


def swap_bit(value, size, bit):
    return lax.ppermute(value, "img", [(i, i ^ (1 << bit)) for i in range(size)])


def send_round(pieces, size):
    return [rotate(piece, "blk", size, shift + 1) for shift, piece in enumerate(pieces)]


def other_pieces(value, size):
    me = lax.axis_index("blk")
    return [lax.dynamic_index_in_dim(value, lax.rem(me + shift, size), 0, False) for shift in range(1, size)]


def add_low(first, second):
    return (first.astype(WIDE) + second.astype(WIDE)).astype(NARROW)


def sum_group(value, axis, patterns, size):
    terms = [value.astype(WIDE)]
    for pattern in patterns:
        got = lax.ppermute(value, axis, [(i, i ^ pattern) for i in range(size)])
        terms.append(got.astype(WIDE))
    while len(terms) > 1:
        terms = [one + two for one, two in zip(terms[::2], terms[1::2])]
    return terms[0].astype(NARROW)


class Tree:
    def __init__(self, terms, bits):
        self.bits = list(bits)
        cuts = (2,) * len(self.bits)
        self.terms = [
            term if term.shape[:-2] == cuts else term.reshape(cuts + (-1, term.shape[-1])) for term in terms
        ]

    def cut(self, axis, bit):
        position = self.bits.index((axis, bit))
        mine = lax.rem(lax.div(lax.axis_index(axis), 1 << bit), 2)
        send = [lax.dynamic_index_in_dim(term, 1 - mine, position, False) for term in self.terms]
        self.terms = [lax.dynamic_index_in_dim(term, mine, position, False) for term in self.terms]
        self.bits.remove((axis, bit))
        if len(send) == 1:
            return send[0]
        return sum([term.astype(WIDE) for term in send[1:]], send[0].astype(WIDE)).astype(NARROW)

    def total(self):
        return sum([term.astype(WIDE) for term in self.terms[1:]], self.terms[0].astype(WIDE))


def swap(value, axis, bit, sizes):
    return lax.ppermute(value, axis, [(i, i ^ (1 << bit)) for i in range(sizes[axis])])


def together(*values):
    return lax.optimization_barrier(values)


def image_on_device(
    img,
    blk,
    images_large,
    images_small,
    cotan_large,
    cotan_small,
    lengths_large,
    lengths_small,
    index_large,
    index_small,
    attn_gain,
    attn_shift,
    qkv_weight,
    query_bias,
    value_bias,
    table_large,
    table_small,
    proj_weight,
    proj_bias,
    attn_scale,
    mlp_gain,
    mlp_shift,
    inner_weight,
    inner_bias,
    outer_weight,
    outer_bias,
    mlp_scale,
):
    width = attn_gain.shape[0]
    heads = table_large.shape[1]
    hidden = inner_bias.shape[0]
    rows = images_large.shape[1]
    smalls, small_rows = images_small.shape[:2]
    part = round_up(rows, 8)
    while part * blk % 16:
        part += 8
    large = part * blk
    small = round_up(small_rows, 16)
    tokens = large + smalls * small
    images = ((0, large),) + tuple((large + i * small, small) for i in range(smalls))
    lanes_large = round_up(large, LANES)
    lanes_small = round_up(small, LANES)
    double = round_up(small, 32)
    blk_me = lax.axis_index("blk")
    core = lax.rem(lax.axis_index("img"), 2)
    place = jnp.stack([blk_me, core])
    shape = (part, large, small)

    sends = other_pieces(images_large, blk)
    gots = send_round(sends, blk)
    spread_large = spread_index(index_large, blk, part, large, lanes_large)
    spread_small = spread_index(index_small, 1, small, double, lanes_small)
    small_bias = bias_lookup(place, table_small, spread_small, 1)
    own_bias = bias_lookup(place, table_large, together(spread_large, small_bias)[0], 2)
    gots, own_bias, images_small, cotan_large, cotan_small, lengths_large, lengths_small = together(
        gots, own_bias, images_small, cotan_large, cotan_small, lengths_large, lengths_small
    )
    other_bias = swap_bit(own_bias, img, 0)

    token = jnp.arange(large, dtype=jnp.int32)
    own_length = lax.dynamic_index_in_dim(lengths_large, blk_me, 0, False)
    inside = (token % part < rows) & (token // part * rows + token % part < own_length)
    small_token = jnp.arange(small, dtype=jnp.int32)
    small_inside = (small_token[None, :] < lengths_small[:, None]).reshape(-1)
    mask = jnp.where(jnp.concatenate([inside, small_inside]), 0.0, NEGATIVE).astype(NARROW)
    mask = jnp.broadcast_to(mask[:, None], (tokens, LANES))

    def row(vector):
        return vector.astype(WIDE)[None, :]

    bias_row = row(jnp.concatenate([query_bias, jnp.zeros_like(query_bias), value_bias]))
    x, h, p = qkv_forward(
        place, images_large, gots, images_small, row(attn_gain), row(attn_shift), qkv_weight, bias_row, *shape
    )
    sends = other_pieces(cotan_large, blk)
    x, h, p, other_bias, sends = together(x, h, p, other_bias, sends)
    gots = send_round(sends, blk)
    out, large_p, small_p = attention_forward(place, p, mask, own_bias, other_bias, small_bias, images)
    out, large_p, small_p, gots = together(out, large_p, small_p, gots)
    zeros = jnp.zeros_like(proj_bias)
    vectors = jnp.stack(
        [proj_bias, attn_scale, mlp_gain, mlp_shift, outer_bias, mlp_scale, zeros, zeros]
    ).astype(WIDE)
    devices = img * blk
    share = width // devices
    found = mlp_pass(
        place,
        cotan_large,
        gots,
        cotan_small,
        out,
        x,
        proj_weight,
        vectors,
        inner_weight,
        row(inner_bias),
        outer_weight,
        *shape,
        devices,
    )
    results, found = list(found[:blk]), found[blk:]
    result_small, dm, grad_out, feed, mlp_sums, dinner_bias = found
    sizes = {"img": img, "blk": blk}
    bits = [("img", bit) for bit in range(1, img.bit_length() - 1)]
    blk_bits = [("blk", bit) for bit in range(blk.bit_length() - 1)]
    dims = bits[::-1] + blk_bits[::-1]
    orders = [bits + blk_bits, bits[::-1] + blk_bits]

    def cut(trees, level):
        return [tree.cut(*order[level]) for tree, order in zip(trees, orders)]

    def move(level, sends):
        return [swap(send, *order[level], sizes) for order, send in zip(orders, sends)]

    def add(trees, gots):
        for tree, got in zip(trees, gots):
            tree.terms.append(got)

    grad_out, feed = together(grad_out, feed)
    feed_part = lax.psum_scatter(feed, "img", scatter_dimension=0, tiled=True)
    share_rows = large // 2 + double // 2
    dp, own_share, theirs = attention_backward(
        place, p, grad_out, out, large_p, small_p, images, (share_rows, lanes_large), 0, heads // 2
    )
    other_share = swap_bit(theirs, img, 0)
    found = qkv_backward(place, results, dp, h, x, dm, row(attn_gain), qkv_weight, part, large, devices)
    qkv_mine, qkv_theirs, backs, grad_small, qkv_sums = found[0], found[1], list(found[2:-2]), found[-2], found[-1]
    qkv_mine, qkv_theirs, backs, qkv_sums, other_share, spread_large, spread_small = together(
        qkv_mine, qkv_theirs, backs, qkv_sums, other_share, spread_large, spread_small
    )

    qkv_got = swap_bit(qkv_theirs, img, 0)
    backs[1:] = send_round(backs[1:], blk)
    middle = 3 * width // 2
    columns = (slice(0, middle), slice(middle, None))
    last = [Tree([qkv_mine[:, part], qkv_got[:, part]], dims) for part in columns]
    sums = jnp.concatenate([mlp_sums[:6], qkv_sums[:4], dinner_bias.reshape(-1, width)], 0).reshape(-1, TABLE_LANES)
    table_sizes = [round_up(table.shape[0], TABLE_LANES) // TABLE_LANES * 16 for table in (table_large, table_small)]
    sums = jnp.pad(sums, ((0, -(sums.shape[0] + sum(table_sizes)) % 32), (0, 0)))
    steps = large // 32
    mark = steps * 2 // 5

    sends = cut(last, 0)
    sends, sums, spread_large, spread_small = together(sends, sums, spread_large, spread_small)
    gots = move(0, sends)
    large_sum, small_sum = table_gradient_sum(
        place,
        own_share,
        other_share,
        [
            (spread_large, table_large.shape[0], 0, 0, mark),
            (spread_small, table_small.shape[0], steps, 0, double // 32),
        ],
    )
    large_sum, small_sum, gots, spread_large, feed_part = together(large_sum, small_sum, gots, spread_large, feed_part)
    add(last, gots)
    sends = cut(last, 1)
    feed_tree = Tree([feed_part], blk_bits[::-1])
    feed_send = feed_tree.cut(*blk_bits[0])
    sends, feed_send, spread_large = together(sends, feed_send, spread_large)
    gots = move(1, sends)
    feed_got = swap(feed_send, *blk_bits[0], sizes)
    mine, theirs = table_gradient_sum(
        place,
        own_share,
        other_share,
        [(spread_large, table_large.shape[0], mark, mark, steps - mark)],
        [large_sum, small_sum, sums],
    )
    mine, theirs, gots, feed_got, backs = together(mine, theirs, gots, feed_got, backs)
    add(last, gots)
    feed_tree.terms.append(feed_got)

    joined = add_low(mine, swap_bit(theirs, img, 0))
    joined = sum_group(joined, "img", [2 * m for m in range(1, img // 2)], img)
    last = Tree([jnp.concatenate([tree.terms[number] for tree in last], -1) for number in range(4)], dims[2:])
    tail = [last, feed_tree]
    for axis, bit in blk_bits:
        for tree in tail:
            if (axis, bit) in tree.bits:
                got = swap(tree.cut(axis, bit), axis, bit, sizes)
                tree.terms.append(got)
    joined = sum_group(joined, "blk", range(1, blk), blk)
    other = swap_bit(joined, img, 0)
    joined = jnp.where(core == 0, jnp.stack([joined, other]), jnp.stack([other, joined]))
    joined = joined.reshape(-1, TABLE_LANES).astype(WIDE)
    last_sum, feed_sum = last.total(), feed_tree.total()
    result_large, result_small, grad_large, grad_small = place_results(
        place, backs, [result_small, grad_small], rows, small, smalls, small_rows
    )
    outs = []
    first = 0
    for table, count in zip((table_large, table_small), table_sizes):
        value = joined[first : first + count].reshape(-1, 16, TABLE_LANES)[:, :heads]
        outs.append(jnp.transpose(value, (0, 2, 1)).reshape(-1, heads)[: table.shape[0]])
        first += count
    sums = joined[first:].reshape(-1)
    me = lax.axis_index("img") * blk + blk_me

    def own(place, length=1):
        return lax.dynamic_slice_in_dim(sums, place * width + me * share * length, share * length, 0)

    return (
        result_large,
        result_small,
        grad_large,
        grad_small,
        own(8),
        own(9),
        last_sum,
        own(6),
        own(7),
        outs[0],
        outs[1],
        feed_sum[:, hidden : hidden + width],
        own(5),
        own(4),
        own(2),
        own(3),
        feed_sum[:, :hidden],
        own(10, hidden // width),
        jnp.transpose(feed_sum[:, hidden + width :].reshape(share, -1, width), (1, 0, 2)).reshape(-1, width),
        own(1),
        own(0),
    )


def solution(mesh):
    img, blk = mesh.shape["img"], mesh.shape["blk"]

    def by_device(*args):
        if args[0].shape[0] == blk:
            return image_on_device(img, blk, *args)
        return on_device(*args)

    return jax.shard_map(
        by_device,
        mesh=mesh,
        in_specs=(
            P("img", "blk", None),
            P(("img", "blk"), None, None),
            P("img", "blk", None),
            P(("img", "blk"), None, None),
            P("img"),
            P(("img", "blk")),
            P(),
            P(),
            P(),
            P(),
            P(),
            P(),
            P(),
            P(),
            P(),
            P(),
            P(),
            P(),
            P(),
            P(),
            P(),
            P(),
            P(),
            P(),
            P(),
        ),
        out_specs=(
            P("img", "blk", None),
            P(("img", "blk"), None, None),
            P("img", "blk", None),
            P(("img", "blk"), None, None),
            P(("img", "blk")),
            P(("img", "blk")),
            P(("img", "blk"), None),
            P(("img", "blk")),
            P(("img", "blk")),
            P(),
            P(),
            P(("img", "blk"), None),
            P(("img", "blk")),
            P(("img", "blk")),
            P(("img", "blk")),
            P(("img", "blk")),
            P(("img", "blk"), None),
            P(("img", "blk")),
            P(("img", "blk"), None),
            P(("img", "blk")),
            P(("img", "blk")),
        ),
        check_vma=False,
    )
```

```python
import functools

import jax
import jax.numpy as jnp
from jax import lax
from jax.experimental import pallas as pl
from jax.experimental.pallas import tpu as pltpu
from jax.sharding import PartitionSpec as P

HEAD = 64


NEGATIVE = -1e30
EPSILON = 1e-06
HIGHEST = lax.Precision.HIGHEST


def layer_norm(values, gain, shift):
    center = values - jnp.mean(values, -1, keepdims=True)
    spread = jnp.mean(center * center, -1, keepdims=True)
    return center * lax.rsqrt(spread + EPSILON) * gain + shift


def exact_gelu(values):
    return jax.nn.gelu(values, approximate=False)


def lookup(table, index_block):
    table_codes = jnp.arange(table.shape[0], dtype=jnp.int32)

    def lookup_one_query(index_row):
        selector = (index_row[:, None] == table_codes[None, :]).astype(jnp.bfloat16)
        return jnp.dot(selector, table, preferred_element_type=jnp.float32)

    picked = lax.map(lookup_one_query, index_block, batch_size=8)
    return jnp.transpose(picked, (2, 0, 1))


def table_gradient(grad_full, index_block, table_rows):
    table_codes = jnp.arange(table_rows, dtype=jnp.int32)

    def table_one_query(item):
        index_row, grad_row = item
        selector = (index_row[:, None] == table_codes[None, :]).astype(jnp.float32)
        return jnp.dot(selector.T, grad_row, precision=HIGHEST, preferred_element_type=jnp.float32)

    partials = lax.map(
        table_one_query, (index_block, jnp.transpose(grad_full, (1, 2, 0))), batch_size=8
    )
    return jnp.sum(partials, 0)


def key_mask(lengths, first, count):
    places = first + jnp.arange(count, dtype=jnp.int32)
    return (places[None, :] < lengths[:, None])[:, None, None, :]


def block_scores(queries, key_piece, bias_rows, lengths, first):
    count = key_piece.shape[1]
    scores = jnp.einsum(
        "iqhe,ikhe->ihqk", queries, key_piece, preferred_element_type=jnp.float32
    ) * HEAD ** (-0.5)
    scores = scores + lax.dynamic_slice_in_dim(bias_rows, first, count, 2)[None]
    return (scores, key_mask(lengths, first, count))


def merge_heads(values):
    return jnp.transpose(values, (0, 2, 1, 3)).reshape(-1, values.shape[1] * values.shape[3])


def local_fold(pieces):

    def visit(step, state):
        return step(state, pieces, 0)

    return visit


def forward_attention(queries, bias_rows, lengths, visit):
    images, rows, heads, width = queries.shape

    def absorb(state, pieces, first):
        top, total, summed = state
        key_piece, value_piece = pieces
        scores, valid = block_scores(queries, key_piece, bias_rows, lengths, first)
        scores = jnp.where(valid, scores, NEGATIVE)
        new_top = jnp.maximum(top, jnp.max(scores, -1))
        weights = jnp.where(valid, jnp.exp(scores - new_top[..., None]), 0.0)
        factor = jnp.exp(top - new_top)
        total = total * factor + jnp.sum(weights, -1)
        update = jnp.einsum(
            "ihqk,ikhe->ihqe", weights, value_piece.astype(jnp.float32), precision=HIGHEST
        )
        return (new_top, total, summed * factor[..., None] + update)

    start_state = (
        jnp.full((images, heads, rows), NEGATIVE, jnp.float32),
        jnp.zeros((images, heads, rows), jnp.float32),
        jnp.zeros((images, heads, rows, width), jnp.float32),
    )
    top, total, summed = visit(absorb, start_state)
    return (summed / total[..., None], top + jnp.log(total))


def key_pass(queries, bias_rows, lengths, grad_out, inner, log_total, visit):
    images, rows, heads, width = queries.shape
    length = bias_rows.shape[2]
    grad_wide = grad_out.astype(jnp.float32)

    def collect(state, pieces, first):
        key_piece, value_piece = pieces
        scores, valid = block_scores(queries, key_piece, bias_rows, lengths, first)
        probs = jnp.where(valid, jnp.exp(scores - log_total[..., None]), 0.0)
        grad_probs = jnp.einsum(
            "iqhe,ikhe->ihqk", grad_out, value_piece, preferred_element_type=jnp.float32
        )
        grad_scores = (probs * (grad_probs - inner[..., None])).astype(jnp.bfloat16)
        grad_query = state[0] + jnp.einsum(
            "ihqk,ikhe->ihqe", grad_scores, key_piece, preferred_element_type=jnp.float32
        ) * HEAD ** (-0.5)
        bias_full = lax.dynamic_update_slice_in_dim(
            state[1], jnp.sum(grad_scores.astype(jnp.float32), 0), first, 2
        )
        key_part = jnp.einsum(
            "ihqk,iqhe->ikhe", grad_scores, queries, preferred_element_type=jnp.float32
        ) * HEAD ** (-0.5)
        value_part = jnp.einsum("ihqk,iqhe->ikhe", probs, grad_wide, precision=HIGHEST)
        key_full = lax.dynamic_update_slice_in_dim(state[2], key_part, first, 1)
        value_full = lax.dynamic_update_slice_in_dim(state[3], value_part, first, 1)
        return (grad_query, bias_full, key_full, value_full)

    start_state = (
        jnp.zeros((images, heads, rows, width), jnp.float32),
        jnp.zeros((heads, rows, length), jnp.float32),
    )
    start_state = start_state + (
        jnp.zeros((images, length, heads, width), jnp.float32),
        jnp.zeros((images, length, heads, width), jnp.float32),
    )
    return visit(collect, start_state)


def on_device(
    images_large,
    images_small,
    cotan_large,
    cotan_small,
    lengths_large,
    lengths_small,
    index_large,
    index_small,
    attn_gain,
    attn_shift,
    qkv_weight,
    query_bias,
    value_bias,
    table_large,
    table_small,
    proj_weight,
    proj_bias,
    attn_scale,
    mlp_gain,
    mlp_shift,
    inner_weight,
    inner_bias,
    outer_weight,
    outer_bias,
    mlp_scale,
):
    wide = jnp.float32
    narrow = jnp.bfloat16
    width = attn_gain.shape[0]
    heads = table_large.shape[1]
    large_count, large_rows = (images_large.shape[0], images_large.shape[1])
    small_count, small_rows = (images_small.shape[0], images_small.shape[1])
    split_at = large_count * large_rows
    first_key = lax.axis_index("blk") * large_rows
    flat = jnp.concatenate(
        [images_large.reshape(-1, width), images_small.reshape(-1, width)], 0
    ).astype(wide)
    normed, attn_norm_back = jax.vjp(
        layer_norm, flat, attn_gain.astype(wide), attn_shift.astype(wide)
    )
    normed_low = normed.astype(narrow)
    bias_vector = jnp.concatenate(
        [query_bias.astype(wide), jnp.zeros((width,), wide), value_bias.astype(wide)]
    )
    projected = (jnp.dot(normed_low, qkv_weight, preferred_element_type=wide) + bias_vector).astype(
        narrow
    )
    large_parts = projected[:split_at].reshape(large_count, large_rows, 3, heads, -1)
    large_query, large_key, large_value = (
        large_parts[:, :, 0],
        large_parts[:, :, 1],
        large_parts[:, :, 2],
    )
    large_index = lax.dynamic_slice_in_dim(index_large, first_key, large_rows, 0)
    large_bias = lookup(table_large, large_index)

    def forward_visit(step, state):
        return step(
            state,
            (
                lax.all_gather(large_key, "blk", axis=1, tiled=True),
                lax.all_gather(large_value, "blk", axis=1, tiled=True),
            ),
            jnp.int32(0),
        )

    def backward_visit(step, state):
        return step(
            state,
            (
                lax.all_gather(large_key, "blk", axis=1, tiled=True),
                lax.all_gather(large_value, "blk", axis=1, tiled=True),
            ),
            jnp.int32(0),
        )

    large_attended, large_log = forward_attention(
        large_query, large_bias, lengths_large, forward_visit
    )
    small_parts = projected[split_at:].reshape(small_count, small_rows, 3, heads, -1)
    small_query, small_key, small_value = (
        small_parts[:, :, 0],
        small_parts[:, :, 1],
        small_parts[:, :, 2],
    )
    small_bias = lookup(table_small, index_small)
    small_visit = local_fold((small_key, small_value))
    small_attended, small_log = forward_attention(
        small_query, small_bias, lengths_small, small_visit
    )
    attended_low = jnp.concatenate(
        [merge_heads(large_attended), merge_heads(small_attended)], 0
    ).astype(narrow)
    branch = jnp.dot(attended_low, proj_weight, preferred_element_type=wide) + proj_bias.astype(
        wide
    )
    middle = flat + attn_scale.astype(wide) * branch
    normed_mlp, mlp_norm_back = jax.vjp(
        layer_norm, middle, mlp_gain.astype(wide), mlp_shift.astype(wide)
    )
    normed_mlp_low = normed_mlp.astype(narrow)
    pre_act = jnp.dot(
        normed_mlp_low, inner_weight, preferred_element_type=wide
    ) + inner_bias.astype(wide)
    activated, gelu_back = jax.vjp(exact_gelu, pre_act)
    activated_low = activated.astype(narrow)
    outer = jnp.dot(activated_low, outer_weight, preferred_element_type=wide) + outer_bias.astype(
        wide
    )
    result_low = (middle + mlp_scale.astype(wide) * outer).astype(narrow)
    cotan = jnp.concatenate(
        [cotan_large.reshape(-1, width), cotan_small.reshape(-1, width)], 0
    ).astype(wide)
    grad_mlp_scale = jnp.sum(cotan * outer, 0)
    grad_outer = (mlp_scale.astype(wide) * cotan).astype(narrow)
    grad_outer_bias = jnp.sum(grad_outer.astype(wide), 0)
    grad_outer_weight = jnp.dot(activated_low.T, grad_outer, preferred_element_type=wide)
    grad_activated = jnp.dot(grad_outer, outer_weight.T, preferred_element_type=wide)
    grad_pre = gelu_back(grad_activated)[0].astype(narrow)
    grad_inner_bias = jnp.sum(grad_pre.astype(wide), 0)
    grad_inner_weight = jnp.dot(normed_mlp_low.T, grad_pre, preferred_element_type=wide)
    grad_normed_mlp = jnp.dot(grad_pre, inner_weight.T, preferred_element_type=wide)
    grad_middle_part, grad_mlp_gain, grad_mlp_shift = mlp_norm_back(grad_normed_mlp)
    grad_middle = cotan + grad_middle_part
    grad_attn_scale = jnp.sum(grad_middle * branch, 0)
    grad_branch = (attn_scale.astype(wide) * grad_middle).astype(narrow)
    grad_proj_bias = jnp.sum(grad_branch.astype(wide), 0)
    grad_proj_weight = jnp.dot(attended_low.T, grad_branch, preferred_element_type=wide)
    grad_attended = jnp.dot(grad_branch, proj_weight.T, preferred_element_type=wide).astype(narrow)
    large_grad_out = grad_attended[:split_at].reshape(large_count, large_rows, heads, -1)
    large_inner = jnp.einsum("iqhe,ihqe->ihq", large_grad_out.astype(wide), large_attended)
    large_grad_query, large_bias_full, key_full, value_full = key_pass(
        large_query,
        large_bias,
        lengths_large,
        large_grad_out,
        large_inner,
        large_log,
        backward_visit,
    )
    large_key_grad, large_value_grad = (
        lax.psum_scatter(
            key_full.astype(jnp.bfloat16), "blk", scatter_dimension=1, tiled=True
        ).astype(jnp.float32),
        lax.psum_scatter(
            value_full.astype(jnp.bfloat16), "blk", scatter_dimension=1, tiled=True
        ).astype(jnp.float32),
    )
    large_grads = jnp.stack(
        [jnp.transpose(large_grad_query, (0, 2, 1, 3)), large_key_grad, large_value_grad], 2
    ).reshape(split_at, 3 * width)
    large_table_grad = table_gradient(large_bias_full, large_index, table_large.shape[0])
    small_grad_out = grad_attended[split_at:].reshape(small_count, small_rows, heads, -1)
    small_inner = jnp.einsum("iqhe,ihqe->ihq", small_grad_out.astype(wide), small_attended)
    small_grad_query, small_bias_full, small_key_grad, small_value_grad = key_pass(
        small_query, small_bias, lengths_small, small_grad_out, small_inner, small_log, small_visit
    )
    small_grads = jnp.stack(
        [jnp.transpose(small_grad_query, (0, 2, 1, 3)), small_key_grad, small_value_grad], 2
    ).reshape(small_count * small_rows, 3 * width)
    small_table_grad = table_gradient(small_bias_full, index_small, table_small.shape[0])
    grad_projected = jnp.concatenate([large_grads, small_grads], 0).astype(narrow)
    grad_query_bias = jnp.sum(grad_projected[:, :width].astype(wide), 0)
    grad_value_bias = jnp.sum(grad_projected[:, 2 * width :].astype(wide), 0)
    grad_qkv_weight = jnp.dot(normed_low.T, grad_projected, preferred_element_type=wide)
    grad_normed = jnp.dot(grad_projected, qkv_weight.T, preferred_element_type=wide)
    grad_flat_part, grad_attn_gain, grad_attn_shift = attn_norm_back(grad_normed)
    grad_flat = (grad_middle + grad_flat_part).astype(narrow)
    summed = (
        lax.psum_scatter(grad_attn_gain, ("img", "blk"), scatter_dimension=0, tiled=True),
        lax.psum_scatter(grad_attn_shift, ("img", "blk"), scatter_dimension=0, tiled=True),
        lax.psum_scatter(grad_qkv_weight, ("img", "blk"), scatter_dimension=0, tiled=True),
        lax.psum_scatter(grad_query_bias, ("img", "blk"), scatter_dimension=0, tiled=True),
        lax.psum_scatter(grad_value_bias, ("img", "blk"), scatter_dimension=0, tiled=True),
        lax.psum_scatter(grad_proj_weight, ("img", "blk"), scatter_dimension=0, tiled=True),
        lax.psum_scatter(grad_proj_bias, ("img", "blk"), scatter_dimension=0, tiled=True),
        lax.psum_scatter(grad_attn_scale, ("img", "blk"), scatter_dimension=0, tiled=True),
        lax.psum_scatter(grad_mlp_gain, ("img", "blk"), scatter_dimension=0, tiled=True),
        lax.psum_scatter(grad_mlp_shift, ("img", "blk"), scatter_dimension=0, tiled=True),
        lax.psum_scatter(grad_inner_weight, ("img", "blk"), scatter_dimension=0, tiled=True),
        lax.psum_scatter(grad_inner_bias, ("img", "blk"), scatter_dimension=0, tiled=True),
        lax.psum_scatter(grad_outer_weight, ("img", "blk"), scatter_dimension=0, tiled=True),
        lax.psum_scatter(grad_outer_bias, ("img", "blk"), scatter_dimension=0, tiled=True),
        lax.psum_scatter(grad_mlp_scale, ("img", "blk"), scatter_dimension=0, tiled=True),
    )
    table_sum_large, table_sum_small = lax.psum(
        (large_table_grad, small_table_grad), ("img", "blk")
    )
    return (
        result_low[:split_at].reshape(large_count, large_rows, width),
        result_low[split_at:].reshape(small_count, small_rows, width),
        grad_flat[:split_at].reshape(large_count, large_rows, width),
        grad_flat[split_at:].reshape(small_count, small_rows, width),
        summed[0],
        summed[1],
        summed[2],
        summed[3],
        summed[4],
        table_sum_large,
        table_sum_small,
        summed[5],
        summed[6],
        summed[7],
        summed[8],
        summed[9],
        summed[10],
        summed[11],
        summed[12],
        summed[13],
        summed[14],
    )


NT = (((1,), (1,)), ((), ()))
TN = (((0,), (0,)), ((), ()))
WIDE = jnp.float32
NARROW = jnp.bfloat16
LANES = 128
TERM = jnp.float8_e4m3fn
MEGA = 1 << 20


def round_up(count, step):
    return -(-count // step) * step


def params(limit, *names):
    return pltpu.CompilerParams(vmem_limit_bytes=limit * MEGA, dimension_semantics=("arbitrary",))


def cost(micros):
    return pl.CostEstimate(flops=int(micros * 1.15e9), bytes_accessed=int(micros * 3.2e6), transcendentals=0)


def whole(*shape):
    return pl.BlockSpec(shape, lambda *steps: (0,) * len(shape), pipeline_mode=pl.Buffered(1))


def whole_of(value):
    return whole(*value.shape)


BLK, CORE = 0, 1


def assemble(held_ref, me, part, mine, gots, small_ref, large, small):
    held_ref[...] = jnp.zeros_like(held_ref)
    size = len(gots) + 1
    for shift, piece in enumerate([mine] + [got[...] for got in gots]):
        start = pl.multiple_of(lax.rem(me + (size - shift), size) * part, 8)
        held_ref[pl.ds(start, piece.shape[0]), :] = piece.astype(WIDE)
    for number in range(small_ref.shape[0]):
        start = large + number * small
        held_ref[start : start + small_ref.shape[1], :] = small_ref[number].astype(WIDE)


def dismantle(held_ref, me, part, piece_refs, small_ref, large):
    size = len(piece_refs)
    for shift, piece_ref in enumerate(piece_refs):
        start = pl.multiple_of(lax.rem(me + shift, size) * part, 8)
        piece_ref[...] = held_ref[pl.ds(start, part), :].astype(NARROW)
    small_ref[...] = held_ref[large:, :].astype(NARROW)


def deal_rows(value, half, is_first, mine_ref, theirs_ref):
    for number in range(value.shape[0] // (2 * half)):
        start = 2 * half * number
        first, second = value[start : start + half], value[start + half : start + 2 * half]
        rows = slice(half * number, half * number + half)
        mine_ref[rows, :] = jnp.where(is_first, first, second)
        theirs_ref[rows, :] = jnp.where(is_first, second, first)


def row_norm(values):
    center = values - jnp.mean(values, -1, keepdims=True)
    spread = jnp.mean(center * center, -1, keepdims=True)
    inverse = lax.rsqrt(spread + EPSILON)
    return center * inverse, inverse


def norm_backward(grad, normal, inverse, gain):
    scaled = grad * gain
    first = jnp.mean(scaled, -1, keepdims=True)
    second = jnp.mean(scaled * normal, -1, keepdims=True)
    return inverse * (scaled - first - normal * second)


def bias_kernel(heads, groups, place_ref, table_ref, index_ref, out_ref):
    rows = index_ref.shape[0]
    for first in range(0, rows, 16):
        found = []
        for half in (0, 8):
            index = index_ref[first + half : first + half + 8, :]
            low = lax.bitwise_and(index, LANES - 1)
            high = lax.shift_right_logical(index, 7)
            picked = [None] * heads
            for group in range(groups):
                here = high == group
                for head in range(heads):
                    value = jnp.take_along_axis(table_ref[group * heads + head], low, axis=1)
                    picked[head] = value if group == 0 else jnp.where(here, value, picked[head])
            found.append(picked)
        for head in range(heads):
            both = jnp.concatenate([found[0][head], found[1][head]], 0)
            out_ref[head, first : first + 16, :] = both.astype(NARROW)


def spread_kernel(pieces, length, piece, index_ref, out_ref):
    out_ref[...] = jnp.zeros_like(out_ref)
    turned = jnp.transpose(index_ref[...])
    for key in range(pieces):
        for query in range(pieces):
            out_ref[key * piece : key * piece + length, query * piece : query * piece + length] = turned[
                key * length : (key + 1) * length, query * length : (query + 1) * length
            ]


def spread_index(index, pieces, piece, rows, lanes):
    length = index.shape[0] // pieces
    return pl.pallas_call(
        functools.partial(spread_kernel, pieces, length, piece),
        out_shape=jax.ShapeDtypeStruct((rows, lanes), jnp.int32),
        compiler_params=pltpu.CompilerParams(vmem_limit_bytes=32 * MEGA),
        cost_estimate=cost(rows * lanes * 1e-5),
        name="spread_index",
    )(index)


def bias_lookup(place, table, index, shares):
    heads = table.shape[1]
    groups = round_up(table.shape[0], LANES) // LANES
    table = jnp.pad(table.astype(WIDE), ((0, groups * LANES - table.shape[0]), (0, 0)))
    table = jnp.transpose(table.reshape(groups, LANES, heads), (0, 2, 1)).reshape(-1, 1, LANES)
    table = jnp.broadcast_to(table, (groups * heads, 8, LANES))
    rows, lanes = index.shape
    rows //= shares
    return pl.pallas_call(
        functools.partial(bias_kernel, heads, groups),
        grid_spec=pltpu.PrefetchScalarGridSpec(
            num_scalar_prefetch=1,
            grid=(lanes // LANES,),
            in_specs=[
                pl.BlockSpec((groups * heads, 8, LANES), lambda i, place: (0, 0, 0)),
                pl.BlockSpec((rows, LANES), lambda i, place: (place[CORE] if shares > 1 else 0, i)),
            ],
            out_specs=pl.BlockSpec((heads, rows, LANES), lambda i, place: (0, 0, i)),
        ),
        out_shape=jax.ShapeDtypeStruct((heads, rows, lanes), NARROW),
        compiler_params=params(32),
        cost_estimate=cost(rows * lanes * groups * heads * 6e-7),
        name="bias_lookup",
    )(place, table, index)


def split_pairs(value, pairs_ref):
    for pair in range(pairs_ref.shape[0]):
        pairs_ref[pair] = value[:, pair * LANES : (pair + 1) * LANES]


def join_pairs(pairs_ref):
    return jnp.concatenate([pairs_ref[pair] for pair in range(pairs_ref.shape[0])], 1)


def qkv_kernel(
    part,
    large,
    small,
    gots,
    place_ref,
    mine_ref,
    *refs,
):
    got_refs = refs[:gots]
    small_ref, gain_ref, shift_ref, weight_ref, bias_ref, x_ref, h_ref, p_ref, held_ref = refs[gots:]

    @pl.when(pl.program_id(0) == 0)
    def _():
        assemble(held_ref, place_ref[BLK], part, mine_ref[...], got_refs, small_ref, large, small)
        x = held_ref[...]
        x_ref[...] = x.astype(NARROW)
        normal, _ = row_norm(x)
        h_ref[...] = (normal * gain_ref[...] + shift_ref[...]).astype(NARROW)

    product = jnp.dot(h_ref[...], weight_ref[...], preferred_element_type=WIDE)
    split_pairs((product + bias_ref[...]).astype(NARROW), p_ref)


def qkv_forward(place, pieces, gots, smalls, gain, shift, weight, bias, part, large, small):
    width = smalls.shape[2]
    tokens = large + smalls.shape[0] * small
    total = weight.shape[1]
    return pl.pallas_call(
        functools.partial(qkv_kernel, part, large, small, len(gots)),
        grid_spec=pltpu.PrefetchScalarGridSpec(
            num_scalar_prefetch=1,
            grid=(total // width,),
            in_specs=[pl.BlockSpec((None,) + pieces.shape[1:], lambda i, place: (place[BLK], 0, 0))]
            + [whole_of(got) for got in gots]
            + [
                whole_of(smalls),
                whole(1, width),
                whole(1, width),
                pl.BlockSpec((width, width), lambda i, place: (0, i)),
                pl.BlockSpec((1, width), lambda i, place: (0, i)),
            ],
            out_specs=[
                whole(tokens, width),
                whole(tokens, width),
                pl.BlockSpec((width // LANES, tokens, LANES), lambda i, place: (i, 0, 0)),
            ],
            scratch_shapes=[pltpu.VMEM((tokens, width), WIDE)],
        ),
        out_shape=[
            jax.ShapeDtypeStruct((tokens, width), NARROW),
            jax.ShapeDtypeStruct((tokens, width), NARROW),
            jax.ShapeDtypeStruct((total // LANES, tokens, LANES), NARROW),
        ],
        compiler_params=params(48),
        cost_estimate=cost(tokens * width * total * 5e-9),
        name="qkv_forward",
    )(place, pieces, *gots, smalls, gain, shift, weight, bias)


def head_parts(first_half, value, other):
    return jnp.where(first_half, value, other), jnp.where(first_half, other, value)


def attention_forward_kernel(
    images,
    place_ref,
    q_ref,
    k_ref,
    v_ref,
    mask_ref,
    own_bias_ref,
    other_bias_ref,
    small_bias_ref,
    o_ref,
    large_p_ref,
    small_p_ref,
):
    is_first = place_ref[CORE] == 0
    lane = lax.broadcasted_iota(jnp.int32, (1, LANES), 1)
    first_half = lane < HEAD
    for number, (start, rows) in enumerate(images):
        here = slice(start, start + rows)
        query = q_ref[here, :] * jnp.asarray(HEAD ** (-0.5), NARROW)
        ones = jnp.where(lane % HEAD == 0, 1.0, 0.0).astype(NARROW)
        ones = jnp.broadcast_to(ones, query.shape)
        queries = head_parts(first_half, query, ones)
        keys = head_parts(first_half, k_ref[here, :], mask_ref[here, :])
        value = v_ref[here, :]
        outs = []
        for head in range(2):
            if number == 0:
                own, other = own_bias_ref[head, :, :rows], other_bias_ref[head, :, :rows]
                bias = jnp.concatenate([jnp.where(is_first, own, other), jnp.where(is_first, other, own)], 0)
            else:
                bias = small_bias_ref[head, :rows, :rows]
            scores = lax.dot_general(keys[head], queries[head], NT, preferred_element_type=WIDE)
            scores = scores + bias.astype(WIDE)
            weights = jnp.exp(scores - jnp.max(scores, 0, keepdims=True))
            probs = (weights * (1.0 / jnp.sum(weights, 0, keepdims=True))).astype(NARROW)
            if number == 0:
                large_p_ref[head] = probs
            else:
                small_p_ref[head, number - 1] = probs
            outs.append(lax.dot_general(probs, value, TN, preferred_element_type=WIDE))
        o_ref[here, :] = jnp.where(first_half, outs[0], outs[1]).astype(NARROW)


def attention_forward(place, p, mask, own_bias, other_bias, small_bias, images):
    tokens = p.shape[1]
    heads = small_bias.shape[0]
    pairs = heads // 2
    large, small, smalls = images[0][1], images[1][1], len(images) - 1
    area = large * large + smalls * small * small

    def column(offset):
        return pl.BlockSpec((None, tokens, LANES), lambda i, place: (offset + i, 0, 0))

    def by_pair(*shape):
        return pl.BlockSpec((2,) + shape, lambda i, place: (i,) + (0,) * len(shape))

    return pl.pallas_call(
        functools.partial(attention_forward_kernel, images),
        grid_spec=pltpu.PrefetchScalarGridSpec(
            num_scalar_prefetch=1,
            grid=(pairs,),
            in_specs=[
                column(0),
                column(pairs),
                column(2 * pairs),
                pl.BlockSpec((tokens, LANES), lambda i, place: (0, 0)),
                by_pair(*own_bias.shape[1:]),
                by_pair(*other_bias.shape[1:]),
                by_pair(*small_bias.shape[1:]),
            ],
            out_specs=[
                column(0),
                by_pair(large, large),
                by_pair(smalls, small, small),
            ],
        ),
        out_shape=[
            jax.ShapeDtypeStruct((pairs, tokens, LANES), NARROW),
            jax.ShapeDtypeStruct((heads, large, large), NARROW),
            jax.ShapeDtypeStruct((heads, smalls, small, small), NARROW),
        ],
        compiler_params=params(60),
        cost_estimate=cost(heads * area * 3.8e-6),
        name="attention_forward",
    )(place, p, p, p, mask, own_bias, other_bias, small_bias)


def attention_backward_kernel(
    images,
    place_ref,
    q_ref,
    k_ref,
    v_ref,
    do_ref,
    o_ref,
    large_p_ref,
    small_p_ref,
    dp_ref,
    mine_ref,
    theirs_ref,
):
    is_first = place_ref[CORE] == 0
    mine_ref[...] = jnp.zeros_like(mine_ref)
    theirs_ref[...] = jnp.zeros_like(theirs_ref)
    large_half = images[0][1] // 2

    def deal(head, grad_scores, start, half):
        count, lanes = grad_scores.shape
        lower = grad_scores[:half]
        upper = grad_scores[half:]
        rest = count - half
        rows = slice(start, start + rest)
        mine_ref[head, rows, :lanes] = jnp.where(is_first, lower[:rest], upper)
        theirs_ref[head, rows, :lanes] = jnp.where(is_first, upper, lower[:rest])
        if rest < half:
            zeros = jnp.zeros((half - rest, lanes), NARROW)
            rows = slice(start + rest, start + half)
            mine_ref[head, rows, :lanes] = jnp.where(is_first, lower[rest:], zeros)
            theirs_ref[head, rows, :lanes] = jnp.where(is_first, zeros, lower[rest:])

    lane = lax.broadcasted_iota(jnp.int32, (1, LANES), 1)
    first_half = lane < HEAD
    small_sum = [None, None]
    scale = HEAD ** (-0.5)
    for number, (start, rows) in enumerate(images):
        here = slice(start, start + rows)
        query = q_ref[here, :] * jnp.asarray(scale, NARROW)
        key = k_ref[here, :]
        value = v_ref[here, :]
        grad = do_ref[here, :]
        product = jnp.transpose(grad.astype(WIDE) * o_ref[here, :].astype(WIDE))
        grads = head_parts(first_half, grad, jnp.zeros_like(grad))
        parts = []
        for head in range(2):
            inner = jnp.sum(product[head * HEAD : (head + 1) * HEAD], 0, keepdims=True)
            probs = large_p_ref[head] if number == 0 else small_p_ref[head, number - 1]
            grad_probs = lax.dot_general(value, grads[head], NT, preferred_element_type=WIDE)
            grad_scores = (probs.astype(WIDE) * (grad_probs - inner)).astype(NARROW)
            if number == 0:
                deal(head, grad_scores, 0, large_half)
            elif small_sum[head] is None:
                small_sum[head] = grad_scores.astype(WIDE)
            else:
                small_sum[head] = small_sum[head] + grad_scores.astype(WIDE)
            parts.append(
                (
                    lax.dot_general(grad_scores, key, TN, preferred_element_type=WIDE) * scale,
                    jnp.dot(grad_scores, query, preferred_element_type=WIDE),
                    jnp.dot(probs, grad, preferred_element_type=WIDE),
                )
            )
        for which in range(3):
            dp_ref[which, here, :] = jnp.where(first_half, parts[0][which], parts[1][which]).astype(NARROW)
    for head in range(2):
        deal(head, small_sum[head].astype(NARROW), large_half, mine_ref.shape[1] - large_half)


def attention_backward(place, p, grad_out, out, large_p, small_p, images, share, first, count):
    tokens = p.shape[1]
    pairs = large_p.shape[0] // 2
    large, small, smalls = images[0][1], images[1][1], len(images) - 1
    area = large * large + smalls * small * small

    def column(offset):
        return pl.BlockSpec((None, tokens, LANES), lambda i, place: (offset + first + i, 0, 0))

    def by_pair(*shape):
        return pl.BlockSpec((2,) + shape, lambda i, place: (first + i,) + (0,) * len(shape))

    share_spec = pl.BlockSpec((2,) + share, lambda i, place: (i, 0, 0))
    return pl.pallas_call(
        functools.partial(attention_backward_kernel, images),
        grid_spec=pltpu.PrefetchScalarGridSpec(
            num_scalar_prefetch=1,
            grid=(count,),
            in_specs=[
                column(0),
                column(pairs),
                column(2 * pairs),
                column(0),
                column(0),
                by_pair(large, large),
                by_pair(smalls, small, small),
            ],
            out_specs=[pl.BlockSpec((3, None, tokens, LANES), lambda i, place: (0, i, 0, 0)), share_spec, share_spec],
        ),
        out_shape=[jax.ShapeDtypeStruct((3, count, tokens, LANES), NARROW)]
        + [jax.ShapeDtypeStruct((2 * count,) + share, NARROW)] * 2,
        compiler_params=params(60),
        cost_estimate=cost(2 * count * area * 4.2e-6),
        name="attention_backward",
    )(place, p, p, p, grad_out, out, large_p, small_p)


def gelu_parts(value):
    size = jnp.abs(value)
    inverse = 1.0 / (1.0 + (0.3275911 * 0.7071067811865476) * size)
    series = inverse * (
        0.127414796
        + inverse
        * (-0.142248368 + inverse * (0.7107068705 + inverse * (-0.7265760135 + inverse * 0.5307027145)))
    )
    bell = jnp.exp(-0.5 * value * value)
    tail = series * bell
    share = jnp.where(value < 0, tail, 1.0 - tail)
    return value * share, share + value * (bell * 0.3989422804014327)


def mlp_kernel(
    part,
    large,
    small,
    share,
    gots,
    place_ref,
    mine_ref,
    *refs,
):
    got_refs, refs = refs[:gots], refs[gots:]
    small_ref, o_ref, x_ref, proj_ref, vector_ref, inner_ref, inner_bias_ref, outer_ref = refs[:8]
    back_refs, refs = refs[8 : 9 + gots], refs[9 + gots :]
    small_back_ref, dm_ref, do_ref, weights_ref, dvector_ref, dbias_ref = refs[:6]
    r_ref, g_ref, dy_ref, dz_ref, z_ref, dg_ref, wide_ref, tall_ref, sems = refs[6:]
    step = pl.program_id(0)
    steps = pl.num_programs(0) - 1
    me = place_ref[BLK]
    proj_bias, attn_scale, gain, shift, outer_bias, mlp_scale = (vector_ref[i : i + 1, :] for i in range(6))
    tokens = x_ref.shape[0]
    chunk = next(c for c in (128, 64, 32, 16) if tokens % c == 0)
    width = x_ref.shape[1]
    pieces = tall_ref.shape[1] // width

    def wide_copy(number):
        columns = pl.ds(pl.multiple_of(number * width, LANES), width)
        return pltpu.make_async_copy(wide_ref, weights_ref.at[:, columns], sems.at[0])

    def tall_copy(number):
        count = tall_ref.shape[0]
        rows = pl.ds(pl.multiple_of(number * count, 16), count)
        columns = slice(weights_ref.shape[1] - tall_ref.shape[1], weights_ref.shape[1])
        return pltpu.make_async_copy(tall_ref, weights_ref.at[rows, columns], sems.at[1])

    @pl.when(step == 0)
    def _():
        r_ref[...] = jnp.dot(join_pairs(o_ref), proj_ref[...], preferred_element_type=WIDE) + proj_bias
        assemble(z_ref, me, part, mine_ref[...], got_refs, small_ref, large, small)

        @pl.loop(0, tokens // chunk)
        def _(i):
            rows = pl.ds(pl.multiple_of(i * chunk, chunk), chunk)
            middle = x_ref[rows, :].astype(WIDE) + attn_scale * r_ref[rows, :]
            normal, _ = row_norm(middle)
            g_ref[rows, :] = (normal * gain + shift).astype(NARROW)
            dy = z_ref[rows, :]
            dy_ref[rows, :] = dy.astype(NARROW)
            dz_ref[rows, :] = (mlp_scale * dy).astype(NARROW)

    @pl.when(step < pl.num_programs(0) - 1)
    def _():
        pre = jnp.dot(g_ref[...], inner_ref[...], preferred_element_type=WIDE) + inner_bias_ref[...]
        active, slope = gelu_parts(pre)
        active = active.astype(NARROW)
        dz = dz_ref[...]
        dactive = lax.dot_general(dz, outer_ref[...], NT, preferred_element_type=WIDE)
        dpre = (dactive * slope).astype(NARROW)
        douter = lax.dot_general(active, dz, TN, preferred_element_type=WIDE)
        dinner = lax.dot_general(g_ref[...], dpre, TN, preferred_element_type=WIDE).astype(NARROW)

        @pl.when(step > 0)
        def _():
            wide_copy(step - 1).wait()
            tall_copy(step - 1).wait()

        wide_ref[...] = dinner
        wide_copy(step).start()
        douter = douter.reshape(-1, pieces, share, width)
        for piece in range(pieces):
            tall_ref[:, piece * width : (piece + 1) * width] = (
                douter[:, piece].reshape(tall_ref.shape[0], width).astype(NARROW)
            )
        tall_copy(step).start()
        dbias_ref[...] = jnp.sum(dpre.astype(WIDE), 0, keepdims=True)
        z = jnp.dot(active, outer_ref[...], preferred_element_type=WIDE)
        dg = lax.dot_general(dpre, inner_ref[...], NT, preferred_element_type=WIDE)

        @pl.when(step == 0)
        def _():
            z_ref[...] = z
            dg_ref[...] = dg

        @pl.when(step > 0)
        def _():
            z_ref[...] += z
            dg_ref[...] += dg

    @pl.when(step == pl.num_programs(0) - 1)
    def _():
        dvector_ref[...] = jnp.zeros_like(dvector_ref)

        @pl.loop(0, tokens // chunk)
        def _(i):
            rows = pl.ds(pl.multiple_of(i * chunk, chunk), chunk)
            branch = r_ref[rows, :]
            middle = x_ref[rows, :].astype(WIDE) + attn_scale * branch
            normal, inverse = row_norm(middle)
            outer = z_ref[rows, :] + outer_bias
            dy = dy_ref[rows, :].astype(WIDE)
            r_ref[rows, :] = middle + mlp_scale * outer
            grad = dg_ref[rows, :]
            dm = dy + norm_backward(grad, normal, inverse, gain)
            dm_ref[rows, :] = dm
            dr = (attn_scale * dm).astype(NARROW)
            g_ref[rows, :] = dr
            sums = [
                dy * outer,
                dz_ref[rows, :].astype(WIDE),
                grad * normal,
                grad,
                dm * branch,
                dr.astype(WIDE),
            ]
            for place, term in enumerate(sums):
                dvector_ref[place : place + 1, :] += jnp.sum(term, 0, keepdims=True)

        dr = g_ref[...]
        dproj = lax.dot_general(join_pairs(o_ref), dr, TN, preferred_element_type=WIDE).astype(NARROW)
        wide_copy(steps - 1).wait()
        tall_copy(steps - 1).wait()
        wide_ref[...] = dproj
        wide_copy(steps).start()
        split_pairs(lax.dot_general(dr, proj_ref[...], NT, preferred_element_type=WIDE).astype(NARROW), do_ref)
        dismantle(r_ref, me, part, back_refs, small_back_ref, large)
        wide_copy(steps).wait()


def mlp_pass(place, pieces, gots, smalls, out, x, proj, vectors, inner, inner_bias, outer, part, large, small, devices):
    tokens, width = x.shape
    hidden = inner.shape[1]
    steps = hidden // width
    blk = len(gots) + 1
    share = width // devices
    tall = steps * width

    def feed(i):
        return jnp.minimum(i, steps - 1)

    shapes = [jax.ShapeDtypeStruct((part, width), NARROW)] * blk + [
        jax.ShapeDtypeStruct((tokens - large, width), NARROW),
        jax.ShapeDtypeStruct((tokens, width), WIDE),
        jax.ShapeDtypeStruct(out.shape, NARROW),
        jax.ShapeDtypeStruct((width, hidden + width + tall), NARROW),
        jax.ShapeDtypeStruct((8, width), WIDE),
        jax.ShapeDtypeStruct((steps, 1, width), WIDE),
    ]
    return pl.pallas_call(
        functools.partial(mlp_kernel, part, large, small, share, len(gots)),
        grid_spec=pltpu.PrefetchScalarGridSpec(
            num_scalar_prefetch=1,
            grid=(steps + 1,),
            in_specs=[
                pl.BlockSpec(
                    (None,) + pieces.shape[1:],
                    lambda i, place: (place[BLK], 0, 0),
                    pipeline_mode=pl.Buffered(1),
                )
            ]
            + [whole_of(got) for got in gots]
            + [
                whole_of(smalls),
                whole_of(out),
                whole(tokens, width),
                whole(width, width),
                whole(8, width),
                pl.BlockSpec((width, width), lambda i, place: (0, feed(i))),
                pl.BlockSpec((1, width), lambda i, place: (0, feed(i))),
                pl.BlockSpec((width, width), lambda i, place: (feed(i), 0)),
            ],
            out_specs=[whole(part, width)] * blk
            + [
                whole(tokens - large, width),
                whole(tokens, width),
                whole_of(out),
                pl.BlockSpec(memory_space=pl.ANY),
                whole(8, width),
                pl.BlockSpec((None, 1, width), lambda i, place: (feed(i), 0, 0)),
            ],
            scratch_shapes=[
                pltpu.VMEM((tokens, width), WIDE),
                pltpu.VMEM((tokens, width), NARROW),
                pltpu.VMEM((tokens, width), NARROW),
                pltpu.VMEM((tokens, width), NARROW),
                pltpu.VMEM((tokens, width), WIDE),
                pltpu.VMEM((tokens, width), WIDE),
                pltpu.VMEM((width, width), NARROW),
                pltpu.VMEM((width // steps, tall), NARROW),
                pltpu.SemaphoreType.DMA((2,)),
            ],
        ),
        out_shape=shapes,
        compiler_params=params(60),
        cost_estimate=cost(tokens * width * hidden * 2.4e-8),
        name="mlp_pass",
    )(place, pieces, *gots, smalls, out, x, proj, vectors, inner, inner_bias, outer)


def qkv_backward_kernel(part, large, half, pieces, place_ref, *refs):
    result_refs, refs = refs[:pieces], refs[pieces:]
    dp_ref, h_ref, x_ref, dm_ref, gain_ref, weight_ref, mine_ref, theirs_ref = refs[:8]
    back_refs = refs[8 : 8 + pieces]
    small_back_ref, dvector_ref, dh_ref = refs[8 + pieces :]
    step = pl.program_id(0)
    grad = join_pairs(dp_ref)
    dweight = lax.dot_general(h_ref[...], grad, TN, preferred_element_type=WIDE).astype(NARROW)
    deal_rows(dweight, half, place_ref[CORE] == 0, mine_ref, theirs_ref)
    term = lax.dot_general(grad, weight_ref[...], NT, preferred_element_type=WIDE)
    column_sum = jnp.sum(grad.astype(WIDE), 0, keepdims=True)
    tokens = x_ref.shape[0]
    chunk = next(c for c in (128, 64, 32, 16) if tokens % c == 0)

    @pl.when(step == 0)
    def _():
        dvector_ref[...] = jnp.zeros_like(dvector_ref)
        dh_ref[...] = term
        dvector_ref[0:1, :] = column_sum

    @pl.when(step > 0)
    def _():
        dh_ref[...] += term

    @pl.when(step == pl.num_programs(0) - 1)
    def _():
        dvector_ref[1:2, :] = column_sum

        @pl.loop(0, tokens // chunk)
        def _(i):
            rows = pl.ds(pl.multiple_of(i * chunk, chunk), chunk)
            normal, inverse = row_norm(x_ref[rows, :].astype(WIDE))
            dh = dh_ref[rows, :]
            dh_ref[rows, :] = dm_ref[rows, :] + norm_backward(dh, normal, inverse, gain_ref[...])
            dvector_ref[2:3, :] += jnp.sum(dh * normal, 0, keepdims=True)
            dvector_ref[3:4, :] += jnp.sum(dh, 0, keepdims=True)

        for back_ref, result_ref in zip(back_refs, result_refs):
            back_ref[0] = result_ref[...]
        dismantle(dh_ref, place_ref[BLK], part, [back_ref.at[1] for back_ref in back_refs], small_back_ref, large)


def qkv_backward(place, results, dp, h, x, dm, gain, weight, part, large, devices):
    blk = len(results)
    tokens, width = x.shape
    half_spec = pl.BlockSpec((width // 2, width), lambda i, place: (0, i))
    return pl.pallas_call(
        functools.partial(qkv_backward_kernel, part, large, blk * width // devices, blk),
        grid_spec=pltpu.PrefetchScalarGridSpec(
            num_scalar_prefetch=1,
            grid=(3,),
            in_specs=[whole_of(result) for result in results]
            + [
                pl.BlockSpec((None,) + dp.shape[1:], lambda i, place: (i, 0, 0, 0)),
                whole(tokens, width),
                whole(tokens, width),
                whole(tokens, width),
                whole(1, width),
                pl.BlockSpec((width, width), lambda i, place: (0, i)),
            ],
            out_specs=[half_spec, half_spec]
            + [whole(2, part, width)] * blk
            + [whole(tokens - large, width), whole(8, width)],
            scratch_shapes=[pltpu.VMEM((tokens, width), WIDE)],
        ),
        out_shape=[jax.ShapeDtypeStruct((width // 2, 3 * width), NARROW)] * 2
        + [jax.ShapeDtypeStruct((2, part, width), NARROW)] * blk
        + [
            jax.ShapeDtypeStruct((tokens - large, width), NARROW),
            jax.ShapeDtypeStruct((8, width), WIDE),
        ],
        compiler_params=params(48),
        cost_estimate=cost(tokens * width * width * 2.5e-8),
        name="qkv_backward",
    )(place, *results, dp, h, x, dm, gain, weight)


def place_kernel(rows, small, smalls, pieces, place_ref, *refs):
    backs, refs = refs[:pieces], refs[pieces:]
    still, outs = refs[:2], refs[2:]
    me = place_ref[BLK]
    for which in range(2):
        for shift in range(pieces):
            source = lax.rem(me + (pieces - shift), pieces)
            outs[2 * which][pl.ds(source, 1)] = backs[shift][which, :rows, :][None]
        for number in range(smalls):
            out_ref = outs[2 * which + 1]
            out_ref[number] = still[which][number * small : number * small + out_ref.shape[1], :]


def place_results(place, backs, still, rows, small, smalls, small_rows):
    width = still[0].shape[1]
    pieces = len(backs)
    shapes = [(pieces, rows, width), (smalls, small_rows, width)] * 2
    return pl.pallas_call(
        functools.partial(place_kernel, rows, small, smalls, pieces),
        grid_spec=pltpu.PrefetchScalarGridSpec(
            num_scalar_prefetch=1,
            grid=(1,),
            in_specs=[whole_of(value) for value in backs + still],
            out_specs=[whole(*shape) for shape in shapes],
        ),
        out_shape=[jax.ShapeDtypeStruct(shape, NARROW) for shape in shapes],
        compiler_params=params(32),
        cost_estimate=cost(3),
        name="place_results",
    )(place, *backs, *still)


TABLE_LANES = 256


def table_shape(table_rows, heads):
    groups = round_up(table_rows, TABLE_LANES) // TABLE_LANES
    unit = 2 * round_up(heads, 4)
    return groups, unit, round_up(groups * unit, 32)


def table_rows(own_ref, other_ref, index_ref, out_ref, turned_ref, left_ref, right_ref, unit, batch):
    rows, lanes = index_ref.shape
    height = out_ref.shape[0]
    half = unit // 2
    top = jnp.zeros((8, lanes), WIDE)
    for head in range(own_ref.shape[0]):
        value = own_ref[head].astype(WIDE) + other_ref[head].astype(WIDE)
        turned_ref[:, head, :lanes] = value
        size = jnp.abs(value)
        for first in range(0, rows, 8):
            top = jnp.maximum(top, size[first : first + 8])
    peak = jnp.maximum(jnp.max(top, keepdims=True), 1e-30)
    scale = 256.0 / peak
    back = peak * (1.0 / 256.0)
    zero = jnp.zeros((), TERM)
    one = jnp.ones((), TERM)
    codes = (lax.broadcasted_iota(jnp.int32, (TABLE_LANES, LANES), 0) - 128).astype(jnp.int8)
    is_upper = lax.broadcasted_iota(jnp.int32, (unit, LANES), 0) < half
    row_group = lax.broadcasted_iota(jnp.int32, (height, LANES), 0) // unit
    columns = slice(0, batch * lanes)

    def some_rows(part, carry):
        for within in range(batch):
            row = part * batch + within
            index = index_ref[pl.ds(row, 1), :]
            low = lax.bitwise_and(index, TABLE_LANES - 1) - 128
            high = lax.shift_right_logical(index, 8)
            for first in range(0, lanes, LANES):
                here = slice(first, first + LANES)
                there = slice(within * lanes + first, within * lanes + first + LANES)
                chosen = jnp.broadcast_to(low[:, here], (TABLE_LANES, LANES)).astype(jnp.int8)
                right_ref[:, there] = jnp.where(codes == chosen, one, zero)
                value = turned_ref[row, :, here] * scale
                value = jnp.concatenate([value[:half], value[:half]], 0)
                upper = value.astype(TERM).astype(WIDE)
                value = jnp.where(is_upper, upper, (value - upper) * 16.0)
                eighths = [value[eight : eight + 8] for eight in range(0, unit, 8)]
                wide_high = jnp.broadcast_to(high[:, here], (32, LANES)).astype(jnp.int8)
                turns = {}
                for tile in range(height // 32):
                    turn = tile * 4 % len(eighths)
                    if turn not in turns:
                        picked = [eighths[(turn + place) % len(eighths)] for place in range(4)]
                        turns[turn] = jnp.concatenate(picked, 0).astype(TERM)
                    group = row_group[tile * 32 : tile * 32 + 32].astype(jnp.int8)
                    left_ref[tile * 32 : tile * 32 + 32, there] = jnp.where(wide_high == group, turns[turn], zero)
        left = left_ref[:height, columns]
        term = lax.dot_general(left, right_ref[:, columns], NT, preferred_element_type=WIDE)
        out_ref[...] += term * back
        return carry

    lax.fori_loop(0, rows // batch, some_rows, 0)


def table_kernel(slots, counts, shapes, heads, batch, last, place_ref, *refs):
    ins, refs = refs[: 3 * len(counts)], refs[3 * len(counts) :]
    if last:
        before, (vector_ref, mine_ref, theirs_ref), refs = refs[: len(shapes)], refs[len(shapes) :][:3], refs[len(shapes) + 3 :]
    totals, scratch = refs[: len(shapes)], refs[len(shapes) :]
    step = pl.program_id(0)

    @pl.when(step == 0)
    def _():
        scratch[0][...] = jnp.zeros_like(scratch[0])
        for number, total_ref in enumerate(totals):
            total_ref[...] = before[number][...] if last else jnp.zeros_like(total_ref)

    start = 0
    for job, count in enumerate(counts):

        @pl.when((step >= start) & (step < start + count))
        def _():
            slot = slots[job]
            table_rows(*ins[3 * job : 3 * job + 3], totals[slot], *scratch, shapes[slot][1], batch)

        start += count

    if last:

        @pl.when(step == start - 1)
        def _():
            rows = []
            for total_ref, (groups, unit, _) in zip(totals, shapes):
                for group in range(groups):
                    first, second = group * unit, group * unit + unit // 2
                    rows.append(total_ref[first : first + heads, :] + total_ref[second : second + heads, :] * (1 / 16))
            rows = jnp.concatenate(rows + [vector_ref[...]], 0)
            half = rows.shape[0] // 2
            is_first = place_ref[CORE] == 0
            mine_ref[...] = jnp.where(is_first, rows[:half], rows[half:]).astype(NARROW)
            theirs_ref[...] = jnp.where(is_first, rows[half:], rows[:half]).astype(NARROW)


def table_gradients(place, own, other, tables, jobs, before=None, vectors=None):
    step, batch = 16, 8
    heads = own.shape[0]
    last = before is not None
    in_specs, args = [], []
    shapes = [table_shape(rows, heads) for rows in tables]
    slots = [job[0] for job in jobs]
    lanes = [job[1].shape[1] for job in jobs]
    counts = [job[-1] for job in jobs]
    start = 0
    for (_, index, share_first, index_first, count), width in zip(jobs, lanes):
        total = index.shape[0] // 2 // step

        def local(i, start=start, count=count):
            return jnp.clip(i - start, 0, count - 1)

        for value in (own, other):
            in_specs.append(
                pl.BlockSpec(
                    (heads, step, width),
                    lambda i, place, local=local, first=share_first: (0, first + local(i), 0),
                )
            )
        in_specs.append(
            pl.BlockSpec(
                (step, width),
                lambda i, place, local=local, first=index_first, total=total: (
                    first + local(i) + place[CORE] * total,
                    0,
                ),
            )
        )
        args += [own, other, index]
        start += count
    tall = max(height for *_, height in shapes)
    sums = [jax.ShapeDtypeStruct((height, TABLE_LANES), WIDE) for *_, height in shapes]
    scratch = [
        pltpu.VMEM((step, 16, max(lanes)), WIDE),
        pltpu.VMEM((tall, batch * max(lanes)), TERM),
        pltpu.VMEM((TABLE_LANES, batch * max(lanes)), TERM),
    ]
    if last:
        args += before + [vectors]
        in_specs += [whole_of(value) for value in before + [vectors]]
        rows = sum(groups * heads for groups, *_ in shapes) + vectors.shape[0]
        out_shape = [jax.ShapeDtypeStruct((rows // 2, TABLE_LANES), NARROW)] * 2
        scratch = [pltpu.VMEM(value.shape, WIDE) for value in sums] + scratch
    else:
        out_shape = sums
    return pl.pallas_call(
        functools.partial(table_kernel, slots, counts, shapes, heads, batch, last),
        grid_spec=pltpu.PrefetchScalarGridSpec(
            num_scalar_prefetch=1,
            grid=(start,),
            in_specs=in_specs,
            out_specs=[whole_of(value) for value in out_shape],
            scratch_shapes=scratch,
        ),
        out_shape=out_shape,
        compiler_params=params(48),
        cost_estimate=cost(start * step * max(lanes) * 1.6e-4),
        name="table_gradients",
    )(place, *args)


def rotate(value, axis, size, shift):
    return lax.ppermute(value, axis, [(i, (i + shift) % size) for i in range(size)])


def swap_bit(value, size, bit):
    return lax.ppermute(value, "img", [(i, i ^ (1 << bit)) for i in range(size)])


def send_round(pieces, size):
    return [rotate(piece, "blk", size, shift + 1) for shift, piece in enumerate(pieces)]


def other_pieces(value, size):
    me = lax.axis_index("blk")
    return [lax.dynamic_index_in_dim(value, lax.rem(me + shift, size), 0, False) for shift in range(1, size)]


def add_low(first, second):
    return (first.astype(WIDE) + second.astype(WIDE)).astype(NARROW)


def sum_group(value, axis, patterns, size):
    terms = [value.astype(WIDE)]
    for pattern in patterns:
        got = lax.ppermute(value, axis, [(i, i ^ pattern) for i in range(size)])
        terms.append(got.astype(WIDE))
    while len(terms) > 1:
        terms = [one + two for one, two in zip(terms[::2], terms[1::2])]
    return terms[0].astype(NARROW)


class Tree:
    def __init__(self, terms, bits):
        self.bits = list(bits)
        cuts = (2,) * len(self.bits)
        self.terms = [
            term if term.shape[:-2] == cuts else term.reshape(cuts + (-1, term.shape[-1])) for term in terms
        ]

    def cut(self, axis, bit):
        position = self.bits.index((axis, bit))
        mine = lax.rem(lax.div(lax.axis_index(axis), 1 << bit), 2)
        send = [lax.dynamic_index_in_dim(term, 1 - mine, position, False) for term in self.terms]
        self.terms = [lax.dynamic_index_in_dim(term, mine, position, False) for term in self.terms]
        self.bits.remove((axis, bit))
        if len(send) == 1:
            return send[0]
        return sum([term.astype(WIDE) for term in send[1:]], send[0].astype(WIDE)).astype(NARROW)

    def total(self):
        return sum([term.astype(WIDE) for term in self.terms[1:]], self.terms[0].astype(WIDE))


def swap(value, axis, bit, sizes):
    return lax.ppermute(value, axis, [(i, i ^ (1 << bit)) for i in range(sizes[axis])])


def together(*values):
    return lax.optimization_barrier(values)


def image_on_device(
    img,
    blk,
    images_large,
    images_small,
    cotan_large,
    cotan_small,
    lengths_large,
    lengths_small,
    index_large,
    index_small,
    attn_gain,
    attn_shift,
    qkv_weight,
    query_bias,
    value_bias,
    table_large,
    table_small,
    proj_weight,
    proj_bias,
    attn_scale,
    mlp_gain,
    mlp_shift,
    inner_weight,
    inner_bias,
    outer_weight,
    outer_bias,
    mlp_scale,
):
    width = attn_gain.shape[0]
    heads = table_large.shape[1]
    hidden = inner_bias.shape[0]
    rows = images_large.shape[1]
    smalls, small_rows = images_small.shape[:2]
    part = round_up(rows, 8)
    while part * blk % 16:
        part += 8
    large = part * blk
    small = round_up(small_rows, 16)
    tokens = large + smalls * small
    images = ((0, large),) + tuple((large + i * small, small) for i in range(smalls))
    lanes_large = round_up(large, LANES)
    lanes_small = round_up(small, LANES)
    double = round_up(small, 32)
    blk_me = lax.axis_index("blk")
    core = lax.rem(lax.axis_index("img"), 2)
    place = jnp.stack([blk_me, core])
    shape = (part, large, small)

    sends = other_pieces(images_large, blk)
    gots = send_round(sends, blk)
    spread_large = spread_index(index_large, blk, part, large, lanes_large)
    spread_small = spread_index(index_small, 1, small, double, lanes_small)
    small_bias = bias_lookup(place, table_small, spread_small, 1)
    own_bias = bias_lookup(place, table_large, together(spread_large, small_bias)[0], 2)
    gots, own_bias, images_small, cotan_large, cotan_small, lengths_large, lengths_small = together(
        gots, own_bias, images_small, cotan_large, cotan_small, lengths_large, lengths_small
    )
    other_bias = swap_bit(own_bias, img, 0)

    token = jnp.arange(large, dtype=jnp.int32)
    own_length = lax.dynamic_index_in_dim(lengths_large, blk_me, 0, False)
    inside = (token % part < rows) & (token // part * rows + token % part < own_length)
    small_token = jnp.arange(small, dtype=jnp.int32)
    small_inside = (small_token[None, :] < lengths_small[:, None]).reshape(-1)
    mask = jnp.where(jnp.concatenate([inside, small_inside]), 0.0, NEGATIVE).astype(NARROW)
    mask = jnp.broadcast_to(mask[:, None], (tokens, LANES))

    def row(vector):
        return vector.astype(WIDE)[None, :]

    bias_row = row(jnp.concatenate([query_bias, jnp.zeros_like(query_bias), value_bias]))
    x, h, p = qkv_forward(
        place, images_large, gots, images_small, row(attn_gain), row(attn_shift), qkv_weight, bias_row, *shape
    )
    sends = other_pieces(cotan_large, blk)
    x, h, p, other_bias, sends = together(x, h, p, other_bias, sends)
    gots = send_round(sends, blk)
    out, large_p, small_p = attention_forward(place, p, mask, own_bias, other_bias, small_bias, images)
    out, large_p, small_p, gots = together(out, large_p, small_p, gots)
    zeros = jnp.zeros_like(proj_bias)
    vectors = jnp.stack(
        [proj_bias, attn_scale, mlp_gain, mlp_shift, outer_bias, mlp_scale, zeros, zeros]
    ).astype(WIDE)
    devices = img * blk
    share = width // devices
    found = mlp_pass(
        place,
        cotan_large,
        gots,
        cotan_small,
        out,
        x,
        proj_weight,
        vectors,
        inner_weight,
        row(inner_bias),
        outer_weight,
        *shape,
        devices,
    )
    results, found = list(found[:blk]), found[blk:]
    result_small, dm, grad_out, feed, mlp_sums, dinner_bias = found
    sizes = {"img": img, "blk": blk}
    bits = [("img", bit) for bit in range(1, img.bit_length() - 1)]
    blk_bits = [("blk", bit) for bit in range(blk.bit_length() - 1)]
    dims = bits[::-1] + blk_bits[::-1]
    orders = [bits + blk_bits, bits[::-1] + blk_bits]

    def cut(trees, level):
        return [tree.cut(*order[level]) for tree, order in zip(trees, orders)]

    def move(level, sends):
        return [swap(send, *order[level], sizes) for order, send in zip(orders, sends)]

    def add(trees, gots):
        for tree, got in zip(trees, gots):
            tree.terms.append(got)

    grad_out, feed = together(grad_out, feed)
    feed_part = lax.psum_scatter(feed, "img", scatter_dimension=0, tiled=True)
    share_rows = large // 2 + double // 2
    dp, own_share, theirs = attention_backward(
        place, p, grad_out, out, large_p, small_p, images, (share_rows, lanes_large), 0, heads // 2
    )
    other_share = swap_bit(theirs, img, 0)
    found = qkv_backward(place, results, dp, h, x, dm, row(attn_gain), qkv_weight, part, large, devices)
    qkv_mine, qkv_theirs, backs, grad_small, qkv_sums = found[0], found[1], list(found[2:-2]), found[-2], found[-1]
    qkv_mine, qkv_theirs, backs, qkv_sums, other_share, spread_large, spread_small = together(
        qkv_mine, qkv_theirs, backs, qkv_sums, other_share, spread_large, spread_small
    )

    qkv_got = swap_bit(qkv_theirs, img, 0)
    backs[1:] = send_round(backs[1:], blk)
    sums = jnp.concatenate([mlp_sums[:6], qkv_sums[:4], dinner_bias[:, 0]], 0).reshape(-1, TABLE_LANES)
    table_sizes = [heads * table_shape(table.shape[0], heads)[0] for table in (table_large, table_small)]
    sums = jnp.pad(sums, ((0, -(sums.shape[0] + sum(table_sizes)) % 32), (0, 0)))
    middle = 3 * width // 2
    columns = (slice(0, middle), slice(middle, None))
    trees = [Tree([qkv_mine[:, part], qkv_got[:, part]], dims) for part in columns]
    sends = cut(trees, 0)
    sends, sums, spread_large, spread_small = together(sends, sums, spread_large, spread_small)
    gots = move(0, sends)
    tables = [table_small.shape[0], table_large.shape[0]]
    steps = large // 32
    mark = steps * 4 // 7
    small_total, large_total = table_gradients(
        place,
        own_share,
        other_share,
        tables,
        [(0, spread_small, steps, 0, double // 32), (1, spread_large, 0, 0, mark)],
    )
    small_total, large_total, gots, spread_large, sums, feed_part = together(
        small_total, large_total, gots, spread_large, sums, feed_part
    )
    add(trees, gots)
    feed_sum = lax.psum_scatter(feed_part, "blk", scatter_dimension=0, tiled=True)
    sends = cut(trees, 1)
    sends, sums, spread_large = together(sends, sums, spread_large)
    gots = move(1, sends)
    mine, theirs = table_gradients(
        place,
        own_share,
        other_share,
        tables,
        [(1, spread_large, mark, mark, steps - mark)],
        [small_total, large_total],
        sums,
    )
    mine, theirs, gots, backs = together(mine, theirs, gots, backs)

    core_got = swap_bit(theirs, img, 0)
    add(trees, gots)
    last = Tree([jnp.concatenate([tree.terms[number] for tree in trees], -1) for number in range(4)], dims[2:])
    send = last.cut(*blk_bits[0])
    send, core_got = together(send, core_got)
    got = swap(send, *blk_bits[0], sizes)
    joined = sum_group(add_low(mine, core_got), "img", [2 * m for m in range(1, img // 2)], img)
    joined, got, feed_sum = together(joined, got, feed_sum)
    last.terms.append(got)
    send = last.cut(*blk_bits[1])
    last.terms.append(swap(send, *blk_bits[1], sizes))
    joined = sum_group(joined, "blk", range(1, blk), blk)
    other = swap_bit(joined, img, 0)
    last_sum, feed_sum = last.total(), feed_sum.astype(WIDE)
    result_large, result_small, grad_large, grad_small = place_results(
        place, backs, [result_small, grad_small], rows, small, smalls, small_rows
    )
    joined = jnp.where(core == 0, jnp.stack([joined, other]), jnp.stack([other, joined]))
    joined = joined.reshape(-1, TABLE_LANES).astype(WIDE)
    outs = []
    outs = []
    first = 0
    table_sizes.reverse()
    for table, count in zip((table_small, table_large), table_sizes):
        value = joined[first : first + count].reshape(-1, heads, TABLE_LANES)
        outs.append(jnp.transpose(value, (0, 2, 1)).reshape(-1, heads)[: table.shape[0]])
        first += count
    sums = joined[first:].reshape(-1)
    me = lax.axis_index("img") * blk + blk_me

    def own(place, length=1):
        return lax.dynamic_slice_in_dim(sums, place * width + me * share * length, share * length, 0)

    return (
        result_large,
        result_small,
        grad_large,
        grad_small,
        own(8),
        own(9),
        last_sum,
        own(6),
        own(7),
        outs[1],
        outs[0],
        feed_sum[:, hidden : hidden + width],
        own(5),
        own(4),
        own(2),
        own(3),
        feed_sum[:, :hidden],
        own(10, hidden // width),
        jnp.transpose(feed_sum[:, hidden + width :].reshape(share, -1, width), (1, 0, 2)).reshape(-1, width),
        own(1),
        own(0),
    )


def solution(mesh):
    img, blk = mesh.shape["img"], mesh.shape["blk"]

    def by_device(*args):
        if args[0].shape[0] == blk:
            return image_on_device(img, blk, *args)
        return on_device(*args)

    return jax.shard_map(
        by_device,
        mesh=mesh,
        in_specs=(
            P("img", "blk", None),
            P(("img", "blk"), None, None),
            P("img", "blk", None),
            P(("img", "blk"), None, None),
            P("img"),
            P(("img", "blk")),
            P(),
            P(),
            P(),
            P(),
            P(),
            P(),
            P(),
            P(),
            P(),
            P(),
            P(),
            P(),
            P(),
            P(),
            P(),
            P(),
            P(),
            P(),
            P(),
        ),
        out_specs=(
            P("img", "blk", None),
            P(("img", "blk"), None, None),
            P("img", "blk", None),
            P(("img", "blk"), None, None),
            P(("img", "blk")),
            P(("img", "blk")),
            P(("img", "blk"), None),
            P(("img", "blk")),
            P(("img", "blk")),
            P(),
            P(),
            P(("img", "blk"), None),
            P(("img", "blk")),
            P(("img", "blk")),
            P(("img", "blk")),
            P(("img", "blk")),
            P(("img", "blk"), None),
            P(("img", "blk")),
            P(("img", "blk"), None),
            P(("img", "blk")),
            P(("img", "blk")),
        ),
        check_vma=False,
    )
```

```python
import functools

import jax
import jax.numpy as jnp
from jax import lax
from jax.experimental import pallas as pl
from jax.experimental.pallas import tpu as pltpu
from jax.sharding import PartitionSpec as P

HEAD = 64


NEGATIVE = -1e30
EPSILON = 1e-06
HIGHEST = lax.Precision.HIGHEST


def layer_norm(values, gain, shift):
    center = values - jnp.mean(values, -1, keepdims=True)
    spread = jnp.mean(center * center, -1, keepdims=True)
    return center * lax.rsqrt(spread + EPSILON) * gain + shift


def exact_gelu(values):
    return jax.nn.gelu(values, approximate=False)


def lookup(table, index_block):
    table_codes = jnp.arange(table.shape[0], dtype=jnp.int32)

    def lookup_one_query(index_row):
        selector = (index_row[:, None] == table_codes[None, :]).astype(jnp.bfloat16)
        return jnp.dot(selector, table, preferred_element_type=jnp.float32)

    picked = lax.map(lookup_one_query, index_block, batch_size=8)
    return jnp.transpose(picked, (2, 0, 1))


def table_gradient(grad_full, index_block, table_rows):
    table_codes = jnp.arange(table_rows, dtype=jnp.int32)

    def table_one_query(item):
        index_row, grad_row = item
        selector = (index_row[:, None] == table_codes[None, :]).astype(jnp.float32)
        return jnp.dot(selector.T, grad_row, precision=HIGHEST, preferred_element_type=jnp.float32)

    partials = lax.map(
        table_one_query, (index_block, jnp.transpose(grad_full, (1, 2, 0))), batch_size=8
    )
    return jnp.sum(partials, 0)


def key_mask(lengths, first, count):
    places = first + jnp.arange(count, dtype=jnp.int32)
    return (places[None, :] < lengths[:, None])[:, None, None, :]


def block_scores(queries, key_piece, bias_rows, lengths, first):
    count = key_piece.shape[1]
    scores = jnp.einsum(
        "iqhe,ikhe->ihqk", queries, key_piece, preferred_element_type=jnp.float32
    ) * HEAD ** (-0.5)
    scores = scores + lax.dynamic_slice_in_dim(bias_rows, first, count, 2)[None]
    return (scores, key_mask(lengths, first, count))


def merge_heads(values):
    return jnp.transpose(values, (0, 2, 1, 3)).reshape(-1, values.shape[1] * values.shape[3])


def local_fold(pieces):

    def visit(step, state):
        return step(state, pieces, 0)

    return visit


def forward_attention(queries, bias_rows, lengths, visit):
    images, rows, heads, width = queries.shape

    def absorb(state, pieces, first):
        top, total, summed = state
        key_piece, value_piece = pieces
        scores, valid = block_scores(queries, key_piece, bias_rows, lengths, first)
        scores = jnp.where(valid, scores, NEGATIVE)
        new_top = jnp.maximum(top, jnp.max(scores, -1))
        weights = jnp.where(valid, jnp.exp(scores - new_top[..., None]), 0.0)
        factor = jnp.exp(top - new_top)
        total = total * factor + jnp.sum(weights, -1)
        update = jnp.einsum(
            "ihqk,ikhe->ihqe", weights, value_piece.astype(jnp.float32), precision=HIGHEST
        )
        return (new_top, total, summed * factor[..., None] + update)

    start_state = (
        jnp.full((images, heads, rows), NEGATIVE, jnp.float32),
        jnp.zeros((images, heads, rows), jnp.float32),
        jnp.zeros((images, heads, rows, width), jnp.float32),
    )
    top, total, summed = visit(absorb, start_state)
    return (summed / total[..., None], top + jnp.log(total))


def key_pass(queries, bias_rows, lengths, grad_out, inner, log_total, visit):
    images, rows, heads, width = queries.shape
    length = bias_rows.shape[2]
    grad_wide = grad_out.astype(jnp.float32)

    def collect(state, pieces, first):
        key_piece, value_piece = pieces
        scores, valid = block_scores(queries, key_piece, bias_rows, lengths, first)
        probs = jnp.where(valid, jnp.exp(scores - log_total[..., None]), 0.0)
        grad_probs = jnp.einsum(
            "iqhe,ikhe->ihqk", grad_out, value_piece, preferred_element_type=jnp.float32
        )
        grad_scores = (probs * (grad_probs - inner[..., None])).astype(jnp.bfloat16)
        grad_query = state[0] + jnp.einsum(
            "ihqk,ikhe->ihqe", grad_scores, key_piece, preferred_element_type=jnp.float32
        ) * HEAD ** (-0.5)
        bias_full = lax.dynamic_update_slice_in_dim(
            state[1], jnp.sum(grad_scores.astype(jnp.float32), 0), first, 2
        )
        key_part = jnp.einsum(
            "ihqk,iqhe->ikhe", grad_scores, queries, preferred_element_type=jnp.float32
        ) * HEAD ** (-0.5)
        value_part = jnp.einsum("ihqk,iqhe->ikhe", probs, grad_wide, precision=HIGHEST)
        key_full = lax.dynamic_update_slice_in_dim(state[2], key_part, first, 1)
        value_full = lax.dynamic_update_slice_in_dim(state[3], value_part, first, 1)
        return (grad_query, bias_full, key_full, value_full)

    start_state = (
        jnp.zeros((images, heads, rows, width), jnp.float32),
        jnp.zeros((heads, rows, length), jnp.float32),
    )
    start_state = start_state + (
        jnp.zeros((images, length, heads, width), jnp.float32),
        jnp.zeros((images, length, heads, width), jnp.float32),
    )
    return visit(collect, start_state)


def on_device(
    images_large,
    images_small,
    cotan_large,
    cotan_small,
    lengths_large,
    lengths_small,
    index_large,
    index_small,
    attn_gain,
    attn_shift,
    qkv_weight,
    query_bias,
    value_bias,
    table_large,
    table_small,
    proj_weight,
    proj_bias,
    attn_scale,
    mlp_gain,
    mlp_shift,
    inner_weight,
    inner_bias,
    outer_weight,
    outer_bias,
    mlp_scale,
):
    wide = jnp.float32
    narrow = jnp.bfloat16
    width = attn_gain.shape[0]
    heads = table_large.shape[1]
    large_count, large_rows = (images_large.shape[0], images_large.shape[1])
    small_count, small_rows = (images_small.shape[0], images_small.shape[1])
    split_at = large_count * large_rows
    first_key = lax.axis_index("blk") * large_rows
    flat = jnp.concatenate(
        [images_large.reshape(-1, width), images_small.reshape(-1, width)], 0
    ).astype(wide)
    normed, attn_norm_back = jax.vjp(
        layer_norm, flat, attn_gain.astype(wide), attn_shift.astype(wide)
    )
    normed_low = normed.astype(narrow)
    bias_vector = jnp.concatenate(
        [query_bias.astype(wide), jnp.zeros((width,), wide), value_bias.astype(wide)]
    )
    projected = (jnp.dot(normed_low, qkv_weight, preferred_element_type=wide) + bias_vector).astype(
        narrow
    )
    large_parts = projected[:split_at].reshape(large_count, large_rows, 3, heads, -1)
    large_query, large_key, large_value = (
        large_parts[:, :, 0],
        large_parts[:, :, 1],
        large_parts[:, :, 2],
    )
    large_index = lax.dynamic_slice_in_dim(index_large, first_key, large_rows, 0)
    large_bias = lookup(table_large, large_index)

    def forward_visit(step, state):
        return step(
            state,
            (
                lax.all_gather(large_key, "blk", axis=1, tiled=True),
                lax.all_gather(large_value, "blk", axis=1, tiled=True),
            ),
            jnp.int32(0),
        )

    def backward_visit(step, state):
        return step(
            state,
            (
                lax.all_gather(large_key, "blk", axis=1, tiled=True),
                lax.all_gather(large_value, "blk", axis=1, tiled=True),
            ),
            jnp.int32(0),
        )

    large_attended, large_log = forward_attention(
        large_query, large_bias, lengths_large, forward_visit
    )
    small_parts = projected[split_at:].reshape(small_count, small_rows, 3, heads, -1)
    small_query, small_key, small_value = (
        small_parts[:, :, 0],
        small_parts[:, :, 1],
        small_parts[:, :, 2],
    )
    small_bias = lookup(table_small, index_small)
    small_visit = local_fold((small_key, small_value))
    small_attended, small_log = forward_attention(
        small_query, small_bias, lengths_small, small_visit
    )
    attended_low = jnp.concatenate(
        [merge_heads(large_attended), merge_heads(small_attended)], 0
    ).astype(narrow)
    branch = jnp.dot(attended_low, proj_weight, preferred_element_type=wide) + proj_bias.astype(
        wide
    )
    middle = flat + attn_scale.astype(wide) * branch
    normed_mlp, mlp_norm_back = jax.vjp(
        layer_norm, middle, mlp_gain.astype(wide), mlp_shift.astype(wide)
    )
    normed_mlp_low = normed_mlp.astype(narrow)
    pre_act = jnp.dot(
        normed_mlp_low, inner_weight, preferred_element_type=wide
    ) + inner_bias.astype(wide)
    activated, gelu_back = jax.vjp(exact_gelu, pre_act)
    activated_low = activated.astype(narrow)
    outer = jnp.dot(activated_low, outer_weight, preferred_element_type=wide) + outer_bias.astype(
        wide
    )
    result_low = (middle + mlp_scale.astype(wide) * outer).astype(narrow)
    cotan = jnp.concatenate(
        [cotan_large.reshape(-1, width), cotan_small.reshape(-1, width)], 0
    ).astype(wide)
    grad_mlp_scale = jnp.sum(cotan * outer, 0)
    grad_outer = (mlp_scale.astype(wide) * cotan).astype(narrow)
    grad_outer_bias = jnp.sum(grad_outer.astype(wide), 0)
    grad_outer_weight = jnp.dot(activated_low.T, grad_outer, preferred_element_type=wide)
    grad_activated = jnp.dot(grad_outer, outer_weight.T, preferred_element_type=wide)
    grad_pre = gelu_back(grad_activated)[0].astype(narrow)
    grad_inner_bias = jnp.sum(grad_pre.astype(wide), 0)
    grad_inner_weight = jnp.dot(normed_mlp_low.T, grad_pre, preferred_element_type=wide)
    grad_normed_mlp = jnp.dot(grad_pre, inner_weight.T, preferred_element_type=wide)
    grad_middle_part, grad_mlp_gain, grad_mlp_shift = mlp_norm_back(grad_normed_mlp)
    grad_middle = cotan + grad_middle_part
    grad_attn_scale = jnp.sum(grad_middle * branch, 0)
    grad_branch = (attn_scale.astype(wide) * grad_middle).astype(narrow)
    grad_proj_bias = jnp.sum(grad_branch.astype(wide), 0)
    grad_proj_weight = jnp.dot(attended_low.T, grad_branch, preferred_element_type=wide)
    grad_attended = jnp.dot(grad_branch, proj_weight.T, preferred_element_type=wide).astype(narrow)
    large_grad_out = grad_attended[:split_at].reshape(large_count, large_rows, heads, -1)
    large_inner = jnp.einsum("iqhe,ihqe->ihq", large_grad_out.astype(wide), large_attended)
    large_grad_query, large_bias_full, key_full, value_full = key_pass(
        large_query,
        large_bias,
        lengths_large,
        large_grad_out,
        large_inner,
        large_log,
        backward_visit,
    )
    large_key_grad, large_value_grad = (
        lax.psum_scatter(
            key_full.astype(jnp.bfloat16), "blk", scatter_dimension=1, tiled=True
        ).astype(jnp.float32),
        lax.psum_scatter(
            value_full.astype(jnp.bfloat16), "blk", scatter_dimension=1, tiled=True
        ).astype(jnp.float32),
    )
    large_grads = jnp.stack(
        [jnp.transpose(large_grad_query, (0, 2, 1, 3)), large_key_grad, large_value_grad], 2
    ).reshape(split_at, 3 * width)
    large_table_grad = table_gradient(large_bias_full, large_index, table_large.shape[0])
    small_grad_out = grad_attended[split_at:].reshape(small_count, small_rows, heads, -1)
    small_inner = jnp.einsum("iqhe,ihqe->ihq", small_grad_out.astype(wide), small_attended)
    small_grad_query, small_bias_full, small_key_grad, small_value_grad = key_pass(
        small_query, small_bias, lengths_small, small_grad_out, small_inner, small_log, small_visit
    )
    small_grads = jnp.stack(
        [jnp.transpose(small_grad_query, (0, 2, 1, 3)), small_key_grad, small_value_grad], 2
    ).reshape(small_count * small_rows, 3 * width)
    small_table_grad = table_gradient(small_bias_full, index_small, table_small.shape[0])
    grad_projected = jnp.concatenate([large_grads, small_grads], 0).astype(narrow)
    grad_query_bias = jnp.sum(grad_projected[:, :width].astype(wide), 0)
    grad_value_bias = jnp.sum(grad_projected[:, 2 * width :].astype(wide), 0)
    grad_qkv_weight = jnp.dot(normed_low.T, grad_projected, preferred_element_type=wide)
    grad_normed = jnp.dot(grad_projected, qkv_weight.T, preferred_element_type=wide)
    grad_flat_part, grad_attn_gain, grad_attn_shift = attn_norm_back(grad_normed)
    grad_flat = (grad_middle + grad_flat_part).astype(narrow)
    summed = (
        lax.psum_scatter(grad_attn_gain, ("img", "blk"), scatter_dimension=0, tiled=True),
        lax.psum_scatter(grad_attn_shift, ("img", "blk"), scatter_dimension=0, tiled=True),
        lax.psum_scatter(grad_qkv_weight, ("img", "blk"), scatter_dimension=0, tiled=True),
        lax.psum_scatter(grad_query_bias, ("img", "blk"), scatter_dimension=0, tiled=True),
        lax.psum_scatter(grad_value_bias, ("img", "blk"), scatter_dimension=0, tiled=True),
        lax.psum_scatter(grad_proj_weight, ("img", "blk"), scatter_dimension=0, tiled=True),
        lax.psum_scatter(grad_proj_bias, ("img", "blk"), scatter_dimension=0, tiled=True),
        lax.psum_scatter(grad_attn_scale, ("img", "blk"), scatter_dimension=0, tiled=True),
        lax.psum_scatter(grad_mlp_gain, ("img", "blk"), scatter_dimension=0, tiled=True),
        lax.psum_scatter(grad_mlp_shift, ("img", "blk"), scatter_dimension=0, tiled=True),
        lax.psum_scatter(grad_inner_weight, ("img", "blk"), scatter_dimension=0, tiled=True),
        lax.psum_scatter(grad_inner_bias, ("img", "blk"), scatter_dimension=0, tiled=True),
        lax.psum_scatter(grad_outer_weight, ("img", "blk"), scatter_dimension=0, tiled=True),
        lax.psum_scatter(grad_outer_bias, ("img", "blk"), scatter_dimension=0, tiled=True),
        lax.psum_scatter(grad_mlp_scale, ("img", "blk"), scatter_dimension=0, tiled=True),
    )
    table_sum_large, table_sum_small = lax.psum(
        (large_table_grad, small_table_grad), ("img", "blk")
    )
    return (
        result_low[:split_at].reshape(large_count, large_rows, width),
        result_low[split_at:].reshape(small_count, small_rows, width),
        grad_flat[:split_at].reshape(large_count, large_rows, width),
        grad_flat[split_at:].reshape(small_count, small_rows, width),
        summed[0],
        summed[1],
        summed[2],
        summed[3],
        summed[4],
        table_sum_large,
        table_sum_small,
        summed[5],
        summed[6],
        summed[7],
        summed[8],
        summed[9],
        summed[10],
        summed[11],
        summed[12],
        summed[13],
        summed[14],
    )


NT = (((1,), (1,)), ((), ()))
TN = (((0,), (0,)), ((), ()))
WIDE = jnp.float32
NARROW = jnp.bfloat16
LANES = 128
TERM = jnp.float8_e4m3fn
MEGA = 1 << 20


def round_up(count, step):
    return -(-count // step) * step


def params(limit, *names):
    return pltpu.CompilerParams(vmem_limit_bytes=limit * MEGA, dimension_semantics=("arbitrary",))


def cost(micros):
    return pl.CostEstimate(flops=int(micros * 1.15e9), bytes_accessed=int(micros * 3.2e6), transcendentals=0)


def whole(*shape):
    return pl.BlockSpec(shape, lambda *steps: (0,) * len(shape), pipeline_mode=pl.Buffered(1))


def whole_of(value):
    return whole(*value.shape)


BLK, CORE = 0, 1


def assemble(held_ref, me, part, mine, gots, small_ref, large, small):
    held_ref[...] = jnp.zeros_like(held_ref)
    size = len(gots) + 1
    for shift, piece in enumerate([mine] + [got[...] for got in gots]):
        start = pl.multiple_of(lax.rem(me + (size - shift), size) * part, 8)
        held_ref[pl.ds(start, piece.shape[0]), :] = piece.astype(WIDE)
    for number in range(small_ref.shape[0]):
        start = large + number * small
        held_ref[start : start + small_ref.shape[1], :] = small_ref[number].astype(WIDE)


def dismantle(held_ref, me, part, piece_refs, small_ref, large):
    size = len(piece_refs)
    for shift, piece_ref in enumerate(piece_refs):
        start = pl.multiple_of(lax.rem(me + shift, size) * part, 8)
        piece_ref[...] = held_ref[pl.ds(start, part), :].astype(NARROW)
    small_ref[...] = held_ref[large:, :].astype(NARROW)


def deal_rows(value, half, is_first, mine_ref, theirs_ref):
    for number in range(value.shape[0] // (2 * half)):
        start = 2 * half * number
        first, second = value[start : start + half], value[start + half : start + 2 * half]
        rows = slice(half * number, half * number + half)
        mine_ref[rows, :] = jnp.where(is_first, first, second)
        theirs_ref[rows, :] = jnp.where(is_first, second, first)


def row_norm(values):
    center = values - jnp.mean(values, -1, keepdims=True)
    spread = jnp.mean(center * center, -1, keepdims=True)
    inverse = lax.rsqrt(spread + EPSILON)
    return center * inverse, inverse


def norm_backward(grad, normal, inverse, gain):
    scaled = grad * gain
    first = jnp.mean(scaled, -1, keepdims=True)
    second = jnp.mean(scaled * normal, -1, keepdims=True)
    return inverse * (scaled - first - normal * second)


def bias_kernel(heads, groups, place_ref, table_ref, index_ref, out_ref):
    rows = index_ref.shape[0]
    for first in range(0, rows, 16):
        found = []
        for half in (0, 8):
            index = index_ref[first + half : first + half + 8, :]
            low = lax.bitwise_and(index, LANES - 1)
            high = lax.shift_right_logical(index, 7)
            picked = [None] * heads
            for group in range(groups):
                here = high == group
                for head in range(heads):
                    value = jnp.take_along_axis(table_ref[group * heads + head], low, axis=1)
                    picked[head] = value if group == 0 else jnp.where(here, value, picked[head])
            found.append(picked)
        for head in range(heads):
            both = jnp.concatenate([found[0][head], found[1][head]], 0)
            out_ref[head, first : first + 16, :] = both.astype(NARROW)


def spread_kernel(pieces, length, piece, index_ref, out_ref):
    out_ref[...] = jnp.zeros_like(out_ref)
    turned = jnp.transpose(index_ref[...])
    for key in range(pieces):
        for query in range(pieces):
            out_ref[key * piece : key * piece + length, query * piece : query * piece + length] = turned[
                key * length : (key + 1) * length, query * length : (query + 1) * length
            ]


def spread_index(index, pieces, piece, rows, lanes):
    length = index.shape[0] // pieces
    return pl.pallas_call(
        functools.partial(spread_kernel, pieces, length, piece),
        out_shape=jax.ShapeDtypeStruct((rows, lanes), jnp.int32),
        compiler_params=pltpu.CompilerParams(vmem_limit_bytes=32 * MEGA),
        cost_estimate=cost(rows * lanes * 1e-5),
        name="spread_index",
    )(index)


def bias_lookup(place, table, index, shares):
    heads = table.shape[1]
    groups = round_up(table.shape[0], LANES) // LANES
    table = jnp.pad(table.astype(WIDE), ((0, groups * LANES - table.shape[0]), (0, 0)))
    table = jnp.transpose(table.reshape(groups, LANES, heads), (0, 2, 1)).reshape(-1, 1, LANES)
    table = jnp.broadcast_to(table, (groups * heads, 8, LANES))
    rows, lanes = index.shape
    rows //= shares
    return pl.pallas_call(
        functools.partial(bias_kernel, heads, groups),
        grid_spec=pltpu.PrefetchScalarGridSpec(
            num_scalar_prefetch=1,
            grid=(lanes // LANES,),
            in_specs=[
                pl.BlockSpec((groups * heads, 8, LANES), lambda i, place: (0, 0, 0)),
                pl.BlockSpec((rows, LANES), lambda i, place: (place[CORE] if shares > 1 else 0, i)),
            ],
            out_specs=pl.BlockSpec((heads, rows, LANES), lambda i, place: (0, 0, i)),
        ),
        out_shape=jax.ShapeDtypeStruct((heads, rows, lanes), NARROW),
        compiler_params=params(32),
        cost_estimate=cost(rows * lanes * groups * heads * 6e-7),
        name="bias_lookup",
    )(place, table, index)


def split_pairs(value, pairs_ref):
    for pair in range(pairs_ref.shape[0]):
        pairs_ref[pair] = value[:, pair * LANES : (pair + 1) * LANES]


def join_pairs(pairs_ref):
    return jnp.concatenate([pairs_ref[pair] for pair in range(pairs_ref.shape[0])], 1)


def qkv_kernel(
    part,
    large,
    small,
    gots,
    place_ref,
    mine_ref,
    *refs,
):
    got_refs = refs[:gots]
    small_ref, gain_ref, shift_ref, weight_ref, bias_ref, x_ref, h_ref, p_ref, held_ref = refs[gots:]

    @pl.when(pl.program_id(0) == 0)
    def _():
        assemble(held_ref, place_ref[BLK], part, mine_ref[...], got_refs, small_ref, large, small)
        x = held_ref[...]
        x_ref[...] = x.astype(NARROW)
        normal, _ = row_norm(x)
        h_ref[...] = (normal * gain_ref[...] + shift_ref[...]).astype(NARROW)

    product = jnp.dot(h_ref[...], weight_ref[...], preferred_element_type=WIDE)
    split_pairs((product + bias_ref[...]).astype(NARROW), p_ref)


def qkv_forward(place, pieces, gots, smalls, gain, shift, weight, bias, part, large, small):
    width = smalls.shape[2]
    tokens = large + smalls.shape[0] * small
    total = weight.shape[1]
    return pl.pallas_call(
        functools.partial(qkv_kernel, part, large, small, len(gots)),
        grid_spec=pltpu.PrefetchScalarGridSpec(
            num_scalar_prefetch=1,
            grid=(total // width,),
            in_specs=[pl.BlockSpec((None,) + pieces.shape[1:], lambda i, place: (place[BLK], 0, 0))]
            + [whole_of(got) for got in gots]
            + [
                whole_of(smalls),
                whole(1, width),
                whole(1, width),
                pl.BlockSpec((width, width), lambda i, place: (0, i)),
                pl.BlockSpec((1, width), lambda i, place: (0, i)),
            ],
            out_specs=[
                whole(tokens, width),
                whole(tokens, width),
                pl.BlockSpec((width // LANES, tokens, LANES), lambda i, place: (i, 0, 0)),
            ],
            scratch_shapes=[pltpu.VMEM((tokens, width), WIDE)],
        ),
        out_shape=[
            jax.ShapeDtypeStruct((tokens, width), NARROW),
            jax.ShapeDtypeStruct((tokens, width), NARROW),
            jax.ShapeDtypeStruct((total // LANES, tokens, LANES), NARROW),
        ],
        compiler_params=params(48),
        cost_estimate=cost(tokens * width * total * 5e-9),
        name="qkv_forward",
    )(place, pieces, *gots, smalls, gain, shift, weight, bias)


def head_parts(first_half, value, other):
    return jnp.where(first_half, value, other), jnp.where(first_half, other, value)


def attention_forward_kernel(
    images,
    place_ref,
    q_ref,
    k_ref,
    v_ref,
    mask_ref,
    own_bias_ref,
    other_bias_ref,
    small_bias_ref,
    o_ref,
    large_p_ref,
    small_p_ref,
):
    is_first = place_ref[CORE] == 0
    lane = lax.broadcasted_iota(jnp.int32, (1, LANES), 1)
    first_half = lane < HEAD
    for number, (start, rows) in enumerate(images):
        here = slice(start, start + rows)
        query = q_ref[here, :] * jnp.asarray(HEAD ** (-0.5), NARROW)
        ones = jnp.where(lane % HEAD == 0, 1.0, 0.0).astype(NARROW)
        ones = jnp.broadcast_to(ones, query.shape)
        queries = head_parts(first_half, query, ones)
        keys = head_parts(first_half, k_ref[here, :], mask_ref[here, :])
        value = v_ref[here, :]
        outs = []
        for head in range(2):
            if number == 0:
                own, other = own_bias_ref[head, :, :rows], other_bias_ref[head, :, :rows]
                bias = jnp.concatenate([jnp.where(is_first, own, other), jnp.where(is_first, other, own)], 0)
            else:
                bias = small_bias_ref[head, :rows, :rows]
            scores = lax.dot_general(keys[head], queries[head], NT, preferred_element_type=WIDE)
            scores = scores + bias.astype(WIDE)
            weights = jnp.exp(scores - jnp.max(scores, 0, keepdims=True))
            probs = (weights * (1.0 / jnp.sum(weights, 0, keepdims=True))).astype(NARROW)
            if number == 0:
                large_p_ref[head] = probs
            else:
                small_p_ref[head, number - 1] = probs
            outs.append(lax.dot_general(probs, value, TN, preferred_element_type=WIDE))
        o_ref[here, :] = jnp.where(first_half, outs[0], outs[1]).astype(NARROW)


def attention_forward(place, p, mask, own_bias, other_bias, small_bias, images):
    tokens = p.shape[1]
    heads = small_bias.shape[0]
    pairs = heads // 2
    large, small, smalls = images[0][1], images[1][1], len(images) - 1
    area = large * large + smalls * small * small

    def column(offset):
        return pl.BlockSpec((None, tokens, LANES), lambda i, place: (offset + i, 0, 0))

    def by_pair(*shape):
        return pl.BlockSpec((2,) + shape, lambda i, place: (i,) + (0,) * len(shape))

    return pl.pallas_call(
        functools.partial(attention_forward_kernel, images),
        grid_spec=pltpu.PrefetchScalarGridSpec(
            num_scalar_prefetch=1,
            grid=(pairs,),
            in_specs=[
                column(0),
                column(pairs),
                column(2 * pairs),
                pl.BlockSpec((tokens, LANES), lambda i, place: (0, 0)),
                by_pair(*own_bias.shape[1:]),
                by_pair(*other_bias.shape[1:]),
                by_pair(*small_bias.shape[1:]),
            ],
            out_specs=[
                column(0),
                by_pair(large, large),
                by_pair(smalls, small, small),
            ],
        ),
        out_shape=[
            jax.ShapeDtypeStruct((pairs, tokens, LANES), NARROW),
            jax.ShapeDtypeStruct((heads, large, large), NARROW),
            jax.ShapeDtypeStruct((heads, smalls, small, small), NARROW),
        ],
        compiler_params=params(60),
        cost_estimate=cost(heads * area * 3.8e-6),
        name="attention_forward",
    )(place, p, p, p, mask, own_bias, other_bias, small_bias)


def attention_backward_kernel(
    images,
    place_ref,
    q_ref,
    k_ref,
    v_ref,
    do_ref,
    o_ref,
    large_p_ref,
    small_p_ref,
    dp_ref,
    mine_ref,
    theirs_ref,
):
    is_first = place_ref[CORE] == 0
    mine_ref[...] = jnp.zeros_like(mine_ref)
    theirs_ref[...] = jnp.zeros_like(theirs_ref)
    large_half = images[0][1] // 2

    def deal(head, grad_scores, start, half):
        count, lanes = grad_scores.shape
        lower = grad_scores[:half]
        upper = grad_scores[half:]
        rest = count - half
        rows = slice(start, start + rest)
        mine_ref[head, rows, :lanes] = jnp.where(is_first, lower[:rest], upper)
        theirs_ref[head, rows, :lanes] = jnp.where(is_first, upper, lower[:rest])
        if rest < half:
            zeros = jnp.zeros((half - rest, lanes), NARROW)
            rows = slice(start + rest, start + half)
            mine_ref[head, rows, :lanes] = jnp.where(is_first, lower[rest:], zeros)
            theirs_ref[head, rows, :lanes] = jnp.where(is_first, zeros, lower[rest:])

    lane = lax.broadcasted_iota(jnp.int32, (1, LANES), 1)
    first_half = lane < HEAD
    small_sum = [None, None]
    scale = HEAD ** (-0.5)
    for number, (start, rows) in enumerate(images):
        here = slice(start, start + rows)
        query = q_ref[here, :] * jnp.asarray(scale, NARROW)
        key = k_ref[here, :]
        value = v_ref[here, :]
        grad = do_ref[here, :]
        product = jnp.transpose(grad.astype(WIDE) * o_ref[here, :].astype(WIDE))
        grads = head_parts(first_half, grad, jnp.zeros_like(grad))
        parts = []
        for head in range(2):
            inner = jnp.sum(product[head * HEAD : (head + 1) * HEAD], 0, keepdims=True)
            probs = large_p_ref[head] if number == 0 else small_p_ref[head, number - 1]
            grad_probs = lax.dot_general(value, grads[head], NT, preferred_element_type=WIDE)
            grad_scores = (probs.astype(WIDE) * (grad_probs - inner)).astype(NARROW)
            if number == 0:
                deal(head, grad_scores, 0, large_half)
            elif small_sum[head] is None:
                small_sum[head] = grad_scores.astype(WIDE)
            else:
                small_sum[head] = small_sum[head] + grad_scores.astype(WIDE)
            parts.append(
                (
                    lax.dot_general(grad_scores, key, TN, preferred_element_type=WIDE) * scale,
                    jnp.dot(grad_scores, query, preferred_element_type=WIDE),
                    jnp.dot(probs, grad, preferred_element_type=WIDE),
                )
            )
        for which in range(3):
            dp_ref[which, here, :] = jnp.where(first_half, parts[0][which], parts[1][which]).astype(NARROW)
    for head in range(2):
        deal(head, small_sum[head].astype(NARROW), large_half, mine_ref.shape[1] - large_half)


def attention_backward(place, p, grad_out, out, large_p, small_p, images, share, first, count):
    tokens = p.shape[1]
    pairs = large_p.shape[0] // 2
    large, small, smalls = images[0][1], images[1][1], len(images) - 1
    area = large * large + smalls * small * small

    def column(offset):
        return pl.BlockSpec((None, tokens, LANES), lambda i, place: (offset + first + i, 0, 0))

    def by_pair(*shape):
        return pl.BlockSpec((2,) + shape, lambda i, place: (first + i,) + (0,) * len(shape))

    share_spec = pl.BlockSpec((2,) + share, lambda i, place: (i, 0, 0))
    return pl.pallas_call(
        functools.partial(attention_backward_kernel, images),
        grid_spec=pltpu.PrefetchScalarGridSpec(
            num_scalar_prefetch=1,
            grid=(count,),
            in_specs=[
                column(0),
                column(pairs),
                column(2 * pairs),
                column(0),
                column(0),
                by_pair(large, large),
                by_pair(smalls, small, small),
            ],
            out_specs=[pl.BlockSpec((3, None, tokens, LANES), lambda i, place: (0, i, 0, 0)), share_spec, share_spec],
        ),
        out_shape=[jax.ShapeDtypeStruct((3, count, tokens, LANES), NARROW)]
        + [jax.ShapeDtypeStruct((2 * count,) + share, NARROW)] * 2,
        compiler_params=params(60),
        cost_estimate=cost(2 * count * area * 4.2e-6),
        name="attention_backward",
    )(place, p, p, p, grad_out, out, large_p, small_p)


def gelu_parts(value):
    size = jnp.abs(value)
    inverse = 1.0 / (1.0 + (0.3275911 * 0.7071067811865476) * size)
    series = inverse * (
        0.127414796
        + inverse
        * (-0.142248368 + inverse * (0.7107068705 + inverse * (-0.7265760135 + inverse * 0.5307027145)))
    )
    bell = jnp.exp(-0.5 * value * value)
    tail = series * bell
    share = jnp.where(value < 0, tail, 1.0 - tail)
    return value * share, share + value * (bell * 0.3989422804014327)


def mlp_kernel(
    part,
    large,
    small,
    share,
    gots,
    place_ref,
    mine_ref,
    *refs,
):
    got_refs, refs = refs[:gots], refs[gots:]
    small_ref, o_ref, x_ref, proj_ref, vector_ref, inner_ref, inner_bias_ref, outer_ref = refs[:8]
    back_refs, refs = refs[8 : 9 + gots], refs[9 + gots :]
    small_back_ref, dm_ref, do_ref, weights_ref, dvector_ref, dbias_ref = refs[:6]
    r_ref, g_ref, dy_ref, dz_ref, z_ref, dg_ref, wide_ref, tall_ref, sems = refs[6:]
    step = pl.program_id(0)
    steps = pl.num_programs(0) - 1
    me = place_ref[BLK]
    proj_bias, attn_scale, gain, shift, outer_bias, mlp_scale = (vector_ref[i : i + 1, :] for i in range(6))
    tokens = x_ref.shape[0]
    chunk = next(c for c in (256, 128, 64, 32, 16) if tokens % c == 0)
    width = x_ref.shape[1]
    pieces = tall_ref.shape[1] // width

    def wide_copy(number):
        columns = pl.ds(pl.multiple_of(number * width, LANES), width)
        return pltpu.make_async_copy(wide_ref, weights_ref.at[:, columns], sems.at[0])

    def tall_copy(number):
        count = tall_ref.shape[0]
        rows = pl.ds(pl.multiple_of(number * count, 16), count)
        columns = slice(weights_ref.shape[1] - tall_ref.shape[1], weights_ref.shape[1])
        return pltpu.make_async_copy(tall_ref, weights_ref.at[rows, columns], sems.at[1])

    @pl.when(step == 0)
    def _():
        r_ref[...] = jnp.dot(join_pairs(o_ref), proj_ref[...], preferred_element_type=WIDE) + proj_bias
        assemble(z_ref, me, part, mine_ref[...], got_refs, small_ref, large, small)

        @pl.loop(0, tokens // chunk)
        def _(i):
            rows = pl.ds(pl.multiple_of(i * chunk, chunk), chunk)
            middle = x_ref[rows, :].astype(WIDE) + attn_scale * r_ref[rows, :]
            normal, _ = row_norm(middle)
            g_ref[rows, :] = (normal * gain + shift).astype(NARROW)
            dy = z_ref[rows, :]
            dy_ref[rows, :] = dy.astype(NARROW)
            dz_ref[rows, :] = (mlp_scale * dy).astype(NARROW)

    @pl.when(step < pl.num_programs(0) - 1)
    def _():
        pre = jnp.dot(g_ref[...], inner_ref[...], preferred_element_type=WIDE) + inner_bias_ref[...]
        active, slope = gelu_parts(pre)
        active = active.astype(NARROW)
        dz = dz_ref[...]
        dactive = lax.dot_general(dz, outer_ref[...], NT, preferred_element_type=WIDE)
        dpre = (dactive * slope).astype(NARROW)
        douter = lax.dot_general(active, dz, TN, preferred_element_type=WIDE)
        dinner = lax.dot_general(g_ref[...], dpre, TN, preferred_element_type=WIDE).astype(NARROW)

        @pl.when(step > 0)
        def _():
            wide_copy(step - 1).wait()
            tall_copy(step - 1).wait()

        wide_ref[...] = dinner
        wide_copy(step).start()
        douter = douter.reshape(-1, pieces, share, width)
        for piece in range(pieces):
            tall_ref[:, piece * width : (piece + 1) * width] = (
                douter[:, piece].reshape(tall_ref.shape[0], width).astype(NARROW)
            )
        tall_copy(step).start()
        dbias_ref[...] = jnp.sum(dpre.astype(WIDE), 0, keepdims=True)
        z = jnp.dot(active, outer_ref[...], preferred_element_type=WIDE)
        dg = lax.dot_general(dpre, inner_ref[...], NT, preferred_element_type=WIDE)

        @pl.when(step == 0)
        def _():
            z_ref[...] = z
            dg_ref[...] = dg

        @pl.when(step > 0)
        def _():
            z_ref[...] += z
            dg_ref[...] += dg

    @pl.when(step == pl.num_programs(0) - 1)
    def _():
        dvector_ref[...] = jnp.zeros_like(dvector_ref)

        @pl.loop(0, tokens // chunk)
        def _(i):
            rows = pl.ds(pl.multiple_of(i * chunk, chunk), chunk)
            branch = r_ref[rows, :]
            middle = x_ref[rows, :].astype(WIDE) + attn_scale * branch
            normal, inverse = row_norm(middle)
            outer = z_ref[rows, :] + outer_bias
            dy = dy_ref[rows, :].astype(WIDE)
            r_ref[rows, :] = middle + mlp_scale * outer
            grad = dg_ref[rows, :]
            dm = dy + norm_backward(grad, normal, inverse, gain)
            dm_ref[rows, :] = dm
            dr = (attn_scale * dm).astype(NARROW)
            g_ref[rows, :] = dr
            sums = [
                dy * outer,
                dz_ref[rows, :].astype(WIDE),
                grad * normal,
                grad,
                dm * branch,
                dr.astype(WIDE),
            ]
            for place, term in enumerate(sums):
                dvector_ref[place : place + 1, :] += jnp.sum(term, 0, keepdims=True)

        dr = g_ref[...]
        dproj = lax.dot_general(join_pairs(o_ref), dr, TN, preferred_element_type=WIDE).astype(NARROW)
        wide_copy(steps - 1).wait()
        tall_copy(steps - 1).wait()
        wide_ref[...] = dproj
        wide_copy(steps).start()
        split_pairs(lax.dot_general(dr, proj_ref[...], NT, preferred_element_type=WIDE).astype(NARROW), do_ref)
        dismantle(r_ref, me, part, back_refs, small_back_ref, large)
        wide_copy(steps).wait()


def mlp_pass(place, pieces, gots, smalls, out, x, proj, vectors, inner, inner_bias, outer, part, large, small, devices):
    tokens, width = x.shape
    hidden = inner.shape[1]
    steps = hidden // width
    blk = len(gots) + 1
    share = width // devices
    tall = steps * width

    def feed(i):
        return jnp.minimum(i, steps - 1)

    shapes = [jax.ShapeDtypeStruct((part, width), NARROW)] * blk + [
        jax.ShapeDtypeStruct((tokens - large, width), NARROW),
        jax.ShapeDtypeStruct((tokens, width), WIDE),
        jax.ShapeDtypeStruct(out.shape, NARROW),
        jax.ShapeDtypeStruct((width, hidden + width + tall), NARROW),
        jax.ShapeDtypeStruct((8, width), WIDE),
        jax.ShapeDtypeStruct((steps, 1, width), WIDE),
    ]
    return pl.pallas_call(
        functools.partial(mlp_kernel, part, large, small, share, len(gots)),
        grid_spec=pltpu.PrefetchScalarGridSpec(
            num_scalar_prefetch=1,
            grid=(steps + 1,),
            in_specs=[
                pl.BlockSpec(
                    (None,) + pieces.shape[1:],
                    lambda i, place: (place[BLK], 0, 0),
                    pipeline_mode=pl.Buffered(1),
                )
            ]
            + [whole_of(got) for got in gots]
            + [
                whole_of(smalls),
                whole_of(out),
                whole(tokens, width),
                whole(width, width),
                whole(8, width),
                pl.BlockSpec((width, width), lambda i, place: (0, feed(i))),
                pl.BlockSpec((1, width), lambda i, place: (0, feed(i))),
                pl.BlockSpec((width, width), lambda i, place: (feed(i), 0)),
            ],
            out_specs=[whole(part, width)] * blk
            + [
                whole(tokens - large, width),
                whole(tokens, width),
                whole_of(out),
                pl.BlockSpec(memory_space=pl.ANY),
                whole(8, width),
                pl.BlockSpec((None, 1, width), lambda i, place: (feed(i), 0, 0)),
            ],
            scratch_shapes=[
                pltpu.VMEM((tokens, width), WIDE),
                pltpu.VMEM((tokens, width), NARROW),
                pltpu.VMEM((tokens, width), NARROW),
                pltpu.VMEM((tokens, width), NARROW),
                pltpu.VMEM((tokens, width), WIDE),
                pltpu.VMEM((tokens, width), WIDE),
                pltpu.VMEM((width, width), NARROW),
                pltpu.VMEM((width // steps, tall), NARROW),
                pltpu.SemaphoreType.DMA((2,)),
            ],
        ),
        out_shape=shapes,
        compiler_params=params(60),
        cost_estimate=cost(tokens * width * hidden * 2.4e-8),
        name="mlp_pass",
    )(place, pieces, *gots, smalls, out, x, proj, vectors, inner, inner_bias, outer)


def qkv_backward_kernel(part, large, half, pieces, place_ref, *refs):
    result_refs, refs = refs[:pieces], refs[pieces:]
    dp_ref, h_ref, x_ref, dm_ref, gain_ref, weight_ref, mine_ref, theirs_ref = refs[:8]
    back_refs = refs[8 : 8 + pieces]
    small_back_ref, dvector_ref, dh_ref = refs[8 + pieces :]
    step = pl.program_id(0)
    grad = join_pairs(dp_ref)
    dweight = lax.dot_general(h_ref[...], grad, TN, preferred_element_type=WIDE).astype(NARROW)
    deal_rows(dweight, half, place_ref[CORE] == 0, mine_ref, theirs_ref)
    term = lax.dot_general(grad, weight_ref[...], NT, preferred_element_type=WIDE)
    column_sum = jnp.sum(grad.astype(WIDE), 0, keepdims=True)
    tokens = x_ref.shape[0]
    chunk = next(c for c in (256, 128, 64, 32, 16) if tokens % c == 0)

    @pl.when(step == 0)
    def _():
        dvector_ref[...] = jnp.zeros_like(dvector_ref)
        dh_ref[...] = term
        dvector_ref[0:1, :] = column_sum

    @pl.when(step > 0)
    def _():
        dh_ref[...] += term

    @pl.when(step == pl.num_programs(0) - 1)
    def _():
        dvector_ref[1:2, :] = column_sum

        @pl.loop(0, tokens // chunk)
        def _(i):
            rows = pl.ds(pl.multiple_of(i * chunk, chunk), chunk)
            normal, inverse = row_norm(x_ref[rows, :].astype(WIDE))
            dh = dh_ref[rows, :]
            dh_ref[rows, :] = dm_ref[rows, :] + norm_backward(dh, normal, inverse, gain_ref[...])
            dvector_ref[2:3, :] += jnp.sum(dh * normal, 0, keepdims=True)
            dvector_ref[3:4, :] += jnp.sum(dh, 0, keepdims=True)

        for back_ref, result_ref in zip(back_refs, result_refs):
            back_ref[0] = result_ref[...]
        dismantle(dh_ref, place_ref[BLK], part, [back_ref.at[1] for back_ref in back_refs], small_back_ref, large)


def qkv_backward(place, results, dp, h, x, dm, gain, weight, part, large, devices):
    blk = len(results)
    tokens, width = x.shape
    half_spec = pl.BlockSpec((width // 2, width), lambda i, place: (0, i))
    return pl.pallas_call(
        functools.partial(qkv_backward_kernel, part, large, blk * width // devices, blk),
        grid_spec=pltpu.PrefetchScalarGridSpec(
            num_scalar_prefetch=1,
            grid=(3,),
            in_specs=[whole_of(result) for result in results]
            + [
                pl.BlockSpec((None,) + dp.shape[1:], lambda i, place: (i, 0, 0, 0)),
                whole(tokens, width),
                whole(tokens, width),
                whole(tokens, width),
                whole(1, width),
                pl.BlockSpec((width, width), lambda i, place: (0, i)),
            ],
            out_specs=[half_spec, half_spec]
            + [whole(2, part, width)] * blk
            + [whole(tokens - large, width), whole(8, width)],
            scratch_shapes=[pltpu.VMEM((tokens, width), WIDE)],
        ),
        out_shape=[jax.ShapeDtypeStruct((width // 2, 3 * width), NARROW)] * 2
        + [jax.ShapeDtypeStruct((2, part, width), NARROW)] * blk
        + [
            jax.ShapeDtypeStruct((tokens - large, width), NARROW),
            jax.ShapeDtypeStruct((8, width), WIDE),
        ],
        compiler_params=params(48),
        cost_estimate=cost(tokens * width * width * 2.5e-8),
        name="qkv_backward",
    )(place, *results, dp, h, x, dm, gain, weight)


def place_kernel(rows, small, smalls, pieces, place_ref, *refs):
    backs, refs = refs[:pieces], refs[pieces:]
    still, outs = refs[:2], refs[2:]
    me = place_ref[BLK]
    for which in range(2):
        for shift in range(pieces):
            source = lax.rem(me + (pieces - shift), pieces)
            outs[2 * which][pl.ds(source, 1)] = backs[shift][which, :rows, :][None]
        for number in range(smalls):
            out_ref = outs[2 * which + 1]
            out_ref[number] = still[which][number * small : number * small + out_ref.shape[1], :]


def place_results(place, backs, still, rows, small, smalls, small_rows):
    width = still[0].shape[1]
    pieces = len(backs)
    shapes = [(pieces, rows, width), (smalls, small_rows, width)] * 2
    return pl.pallas_call(
        functools.partial(place_kernel, rows, small, smalls, pieces),
        grid_spec=pltpu.PrefetchScalarGridSpec(
            num_scalar_prefetch=1,
            grid=(1,),
            in_specs=[whole_of(value) for value in backs + still],
            out_specs=[whole(*shape) for shape in shapes],
        ),
        out_shape=[jax.ShapeDtypeStruct(shape, NARROW) for shape in shapes],
        compiler_params=params(32),
        cost_estimate=cost(3),
        name="place_results",
    )(place, *backs, *still)


TABLE_LANES = 256


def table_shape(table_rows, heads):
    groups = round_up(table_rows, TABLE_LANES) // TABLE_LANES
    unit = 2 * round_up(heads, 4)
    return groups, unit, round_up(groups * unit, 32)


def table_rows(own_ref, other_ref, index_ref, out_ref, turned_ref, left_ref, right_ref, unit, batch):
    rows, lanes = index_ref.shape
    height = out_ref.shape[0]
    half = unit // 2
    top = jnp.zeros((8, lanes), WIDE)
    for head in range(own_ref.shape[0]):
        value = own_ref[head].astype(WIDE) + other_ref[head].astype(WIDE)
        turned_ref[:, head, :lanes] = value
        size = jnp.abs(value)
        for first in range(0, rows, 8):
            top = jnp.maximum(top, size[first : first + 8])
    peak = jnp.maximum(jnp.max(top, keepdims=True), 1e-30)
    scale = 256.0 / peak
    back = peak * (1.0 / 256.0)
    zero = jnp.zeros((), TERM)
    one = jnp.ones((), TERM)
    codes = (lax.broadcasted_iota(jnp.int32, (TABLE_LANES, LANES), 0) - 128).astype(jnp.int8)
    is_upper = lax.broadcasted_iota(jnp.int32, (unit, LANES), 0) < half
    row_group = lax.broadcasted_iota(jnp.int32, (height, LANES), 0) // unit
    columns = slice(0, batch * lanes)

    def some_rows(part, carry):
        for within in range(batch):
            row = part * batch + within
            index = index_ref[pl.ds(row, 1), :]
            low = lax.bitwise_and(index, TABLE_LANES - 1) - 128
            high = lax.shift_right_logical(index, 8)
            for first in range(0, lanes, LANES):
                here = slice(first, first + LANES)
                there = slice(within * lanes + first, within * lanes + first + LANES)
                chosen = jnp.broadcast_to(low[:, here], (TABLE_LANES, LANES)).astype(jnp.int8)
                right_ref[:, there] = jnp.where(codes == chosen, one, zero)
                value = turned_ref[row, :, here] * scale
                value = jnp.concatenate([value[:half], value[:half]], 0)
                upper = value.astype(TERM).astype(WIDE)
                value = jnp.where(is_upper, upper, (value - upper) * 16.0)
                eighths = [value[eight : eight + 8] for eight in range(0, unit, 8)]
                wide_high = jnp.broadcast_to(high[:, here], (32, LANES)).astype(jnp.int8)
                turns = {}
                for tile in range(height // 32):
                    turn = tile * 4 % len(eighths)
                    if turn not in turns:
                        picked = [eighths[(turn + place) % len(eighths)] for place in range(4)]
                        turns[turn] = jnp.concatenate(picked, 0).astype(TERM)
                    group = row_group[tile * 32 : tile * 32 + 32].astype(jnp.int8)
                    left_ref[tile * 32 : tile * 32 + 32, there] = jnp.where(wide_high == group, turns[turn], zero)
        left = left_ref[:height, columns]
        term = lax.dot_general(left, right_ref[:, columns], NT, preferred_element_type=WIDE)
        out_ref[...] += term * back
        return carry

    lax.fori_loop(0, rows // batch, some_rows, 0)


def table_kernel(slots, counts, shapes, heads, batch, last, place_ref, *refs):
    ins, refs = refs[: 3 * len(counts)], refs[3 * len(counts) :]
    if last:
        before, (vector_ref, mine_ref, theirs_ref), refs = refs[: len(shapes)], refs[len(shapes) :][:3], refs[len(shapes) + 3 :]
    totals, scratch = refs[: len(shapes)], refs[len(shapes) :]
    step = pl.program_id(0)

    @pl.when(step == 0)
    def _():
        scratch[0][...] = jnp.zeros_like(scratch[0])
        for number, total_ref in enumerate(totals):
            total_ref[...] = before[number][...] if last else jnp.zeros_like(total_ref)

    start = 0
    for job, count in enumerate(counts):

        @pl.when((step >= start) & (step < start + count))
        def _():
            slot = slots[job]
            table_rows(*ins[3 * job : 3 * job + 3], totals[slot], *scratch, shapes[slot][1], batch)

        start += count

    if last:

        @pl.when(step == start - 1)
        def _():
            rows = []
            for total_ref, (groups, unit, _) in zip(totals, shapes):
                for group in range(groups):
                    first, second = group * unit, group * unit + unit // 2
                    rows.append(total_ref[first : first + heads, :] + total_ref[second : second + heads, :] * (1 / 16))
            rows = jnp.concatenate(rows + [vector_ref[...]], 0)
            half = rows.shape[0] // 2
            is_first = place_ref[CORE] == 0
            mine_ref[...] = jnp.where(is_first, rows[:half], rows[half:]).astype(NARROW)
            theirs_ref[...] = jnp.where(is_first, rows[half:], rows[:half]).astype(NARROW)


def table_gradients(place, own, other, tables, jobs, before=None, vectors=None):
    step, batch = 16, 8
    heads = own.shape[0]
    last = before is not None
    in_specs, args = [], []
    shapes = [table_shape(rows, heads) for rows in tables]
    slots = [job[0] for job in jobs]
    lanes = [job[1].shape[1] for job in jobs]
    counts = [job[-1] for job in jobs]
    start = 0
    for (_, index, share_first, index_first, count), width in zip(jobs, lanes):
        total = index.shape[0] // 2 // step

        def local(i, start=start, count=count):
            return jnp.clip(i - start, 0, count - 1)

        for value in (own, other):
            in_specs.append(
                pl.BlockSpec(
                    (heads, step, width),
                    lambda i, place, local=local, first=share_first: (0, first + local(i), 0),
                )
            )
        in_specs.append(
            pl.BlockSpec(
                (step, width),
                lambda i, place, local=local, first=index_first, total=total: (
                    first + local(i) + place[CORE] * total,
                    0,
                ),
            )
        )
        args += [own, other, index]
        start += count
    tall = max(height for *_, height in shapes)
    sums = [jax.ShapeDtypeStruct((height, TABLE_LANES), WIDE) for *_, height in shapes]
    scratch = [
        pltpu.VMEM((step, 16, max(lanes)), WIDE),
        pltpu.VMEM((tall, batch * max(lanes)), TERM),
        pltpu.VMEM((TABLE_LANES, batch * max(lanes)), TERM),
    ]
    if last:
        args += before + [vectors]
        in_specs += [whole_of(value) for value in before + [vectors]]
        rows = sum(groups * heads for groups, *_ in shapes) + vectors.shape[0]
        out_shape = [jax.ShapeDtypeStruct((rows // 2, TABLE_LANES), NARROW)] * 2
        scratch = [pltpu.VMEM(value.shape, WIDE) for value in sums] + scratch
    else:
        out_shape = sums
    return pl.pallas_call(
        functools.partial(table_kernel, slots, counts, shapes, heads, batch, last),
        grid_spec=pltpu.PrefetchScalarGridSpec(
            num_scalar_prefetch=1,
            grid=(start,),
            in_specs=in_specs,
            out_specs=[whole_of(value) for value in out_shape],
            scratch_shapes=scratch,
        ),
        out_shape=out_shape,
        compiler_params=params(48),
        cost_estimate=cost(start * step * max(lanes) * 1.6e-4),
        name="table_gradients",
    )(place, *args)


def rotate(value, axis, size, shift):
    return lax.ppermute(value, axis, [(i, (i + shift) % size) for i in range(size)])


def swap_bit(value, size, bit):
    return lax.ppermute(value, "img", [(i, i ^ (1 << bit)) for i in range(size)])


def send_round(pieces, size):
    return [rotate(piece, "blk", size, shift + 1) for shift, piece in enumerate(pieces)]


def other_pieces(value, size):
    me = lax.axis_index("blk")
    return [lax.dynamic_index_in_dim(value, lax.rem(me + shift, size), 0, False) for shift in range(1, size)]


def add_low(first, second):
    return (first.astype(WIDE) + second.astype(WIDE)).astype(NARROW)


def sum_group(value, axis, patterns, size):
    terms = [value.astype(WIDE)]
    for pattern in patterns:
        got = lax.ppermute(value, axis, [(i, i ^ pattern) for i in range(size)])
        terms.append(got.astype(WIDE))
    while len(terms) > 1:
        terms = [one + two for one, two in zip(terms[::2], terms[1::2])]
    return terms[0].astype(NARROW)


class Tree:
    def __init__(self, terms, bits):
        self.bits = list(bits)
        cuts = (2,) * len(self.bits)
        self.terms = [
            term if term.shape[:-2] == cuts else term.reshape(cuts + (-1, term.shape[-1])) for term in terms
        ]

    def cut(self, axis, bit):
        position = self.bits.index((axis, bit))
        mine = lax.rem(lax.div(lax.axis_index(axis), 1 << bit), 2)
        send = [lax.dynamic_index_in_dim(term, 1 - mine, position, False) for term in self.terms]
        self.terms = [lax.dynamic_index_in_dim(term, mine, position, False) for term in self.terms]
        self.bits.remove((axis, bit))
        if len(send) == 1:
            return send[0]
        return sum([term.astype(WIDE) for term in send[1:]], send[0].astype(WIDE)).astype(NARROW)

    def total(self):
        return sum([term.astype(WIDE) for term in self.terms[1:]], self.terms[0].astype(WIDE))


def swap(value, axis, bit, sizes):
    return lax.ppermute(value, axis, [(i, i ^ (1 << bit)) for i in range(sizes[axis])])


def together(*values):
    return lax.optimization_barrier(values)


def image_on_device(
    img,
    blk,
    images_large,
    images_small,
    cotan_large,
    cotan_small,
    lengths_large,
    lengths_small,
    index_large,
    index_small,
    attn_gain,
    attn_shift,
    qkv_weight,
    query_bias,
    value_bias,
    table_large,
    table_small,
    proj_weight,
    proj_bias,
    attn_scale,
    mlp_gain,
    mlp_shift,
    inner_weight,
    inner_bias,
    outer_weight,
    outer_bias,
    mlp_scale,
):
    width = attn_gain.shape[0]
    heads = table_large.shape[1]
    hidden = inner_bias.shape[0]
    rows = images_large.shape[1]
    smalls, small_rows = images_small.shape[:2]
    part = round_up(rows, 8)
    while part * blk % 16:
        part += 8
    large = part * blk
    small = round_up(small_rows, 16)
    tokens = large + smalls * small
    images = ((0, large),) + tuple((large + i * small, small) for i in range(smalls))
    lanes_large = round_up(large, LANES)
    lanes_small = round_up(small, LANES)
    double = round_up(small, 32)
    blk_me = lax.axis_index("blk")
    core = lax.rem(lax.axis_index("img"), 2)
    place = jnp.stack([blk_me, core])
    shape = (part, large, small)

    sends = other_pieces(images_large, blk)
    gots = send_round(sends, blk)
    spread_large = spread_index(index_large, blk, part, large, lanes_large)
    spread_small = spread_index(index_small, 1, small, double, lanes_small)
    small_bias = bias_lookup(place, table_small, spread_small, 1)
    own_bias = bias_lookup(place, table_large, together(spread_large, small_bias)[0], 2)
    gots, own_bias, images_small, cotan_large, cotan_small, lengths_large, lengths_small = together(
        gots, own_bias, images_small, cotan_large, cotan_small, lengths_large, lengths_small
    )
    other_bias = swap_bit(own_bias, img, 0)

    token = jnp.arange(large, dtype=jnp.int32)
    own_length = lax.dynamic_index_in_dim(lengths_large, blk_me, 0, False)
    inside = (token % part < rows) & (token // part * rows + token % part < own_length)
    small_token = jnp.arange(small, dtype=jnp.int32)
    small_inside = (small_token[None, :] < lengths_small[:, None]).reshape(-1)
    mask = jnp.where(jnp.concatenate([inside, small_inside]), 0.0, NEGATIVE).astype(NARROW)
    mask = jnp.broadcast_to(mask[:, None], (tokens, LANES))

    def row(vector):
        return vector.astype(WIDE)[None, :]

    bias_row = row(jnp.concatenate([query_bias, jnp.zeros_like(query_bias), value_bias]))
    x, h, p = qkv_forward(
        place, images_large, gots, images_small, row(attn_gain), row(attn_shift), qkv_weight, bias_row, *shape
    )
    sends = other_pieces(cotan_large, blk)
    x, h, p, other_bias, sends = together(x, h, p, other_bias, sends)
    gots = send_round(sends, blk)
    out, large_p, small_p = attention_forward(place, p, mask, own_bias, other_bias, small_bias, images)
    out, large_p, small_p, gots = together(out, large_p, small_p, gots)
    zeros = jnp.zeros_like(proj_bias)
    vectors = jnp.stack(
        [proj_bias, attn_scale, mlp_gain, mlp_shift, outer_bias, mlp_scale, zeros, zeros]
    ).astype(WIDE)
    devices = img * blk
    share = width // devices
    found = mlp_pass(
        place,
        cotan_large,
        gots,
        cotan_small,
        out,
        x,
        proj_weight,
        vectors,
        inner_weight,
        row(inner_bias),
        outer_weight,
        *shape,
        devices,
    )
    results, found = list(found[:blk]), found[blk:]
    result_small, dm, grad_out, feed, mlp_sums, dinner_bias = found
    sizes = {"img": img, "blk": blk}
    bits = [("img", bit) for bit in range(1, img.bit_length() - 1)]
    blk_bits = [("blk", bit) for bit in range(blk.bit_length() - 1)]
    dims = bits[::-1] + blk_bits[::-1]
    orders = [bits + blk_bits, bits[::-1] + blk_bits]

    def cut(trees, level):
        return [tree.cut(*order[level]) for tree, order in zip(trees, orders)]

    def move(level, sends):
        return [swap(send, *order[level], sizes) for order, send in zip(orders, sends)]

    def add(trees, gots):
        for tree, got in zip(trees, gots):
            tree.terms.append(got)

    grad_out, feed = together(grad_out, feed)
    feed_part = lax.psum_scatter(feed, "img", scatter_dimension=0, tiled=True)
    share_rows = large // 2 + double // 2
    dp, own_share, theirs = attention_backward(
        place, p, grad_out, out, large_p, small_p, images, (share_rows, lanes_large), 0, heads // 2
    )
    other_share = swap_bit(theirs, img, 0)
    found = qkv_backward(place, results, dp, h, x, dm, row(attn_gain), qkv_weight, part, large, devices)
    qkv_mine, qkv_theirs, backs, grad_small, qkv_sums = found[0], found[1], list(found[2:-2]), found[-2], found[-1]
    qkv_mine, qkv_theirs, backs, qkv_sums, other_share, spread_large, spread_small = together(
        qkv_mine, qkv_theirs, backs, qkv_sums, other_share, spread_large, spread_small
    )

    qkv_got = swap_bit(qkv_theirs, img, 0)
    backs[1:] = send_round(backs[1:], blk)
    sums = jnp.concatenate([mlp_sums[:6], qkv_sums[:4], dinner_bias[:, 0]], 0).reshape(-1, TABLE_LANES)
    table_sizes = [heads * table_shape(table.shape[0], heads)[0] for table in (table_large, table_small)]
    sums = jnp.pad(sums, ((0, -(sums.shape[0] + sum(table_sizes)) % 32), (0, 0)))
    middle = 3 * width // 2
    columns = (slice(0, middle), slice(middle, None))
    trees = [Tree([qkv_mine[:, part], qkv_got[:, part]], dims) for part in columns]
    sends = cut(trees, 0)
    sends, sums, spread_large, spread_small = together(sends, sums, spread_large, spread_small)
    gots = move(0, sends)
    tables = [table_small.shape[0], table_large.shape[0]]
    steps = large // 32
    mark = steps * 2 // 3
    small_total, large_total = table_gradients(
        place,
        own_share,
        other_share,
        tables,
        [(0, spread_small, steps, 0, double // 32), (1, spread_large, 0, 0, mark)],
    )
    small_total, large_total, gots, spread_large, sums, feed_part = together(
        small_total, large_total, gots, spread_large, sums, feed_part
    )
    add(trees, gots)
    feed_sum = lax.psum_scatter(feed_part, "blk", scatter_dimension=0, tiled=True)
    sends = cut(trees, 1)
    sends, sums, spread_large = together(sends, sums, spread_large)
    gots = move(1, sends)
    mine, theirs = table_gradients(
        place,
        own_share,
        other_share,
        tables,
        [(1, spread_large, mark, mark, steps - mark)],
        [small_total, large_total],
        sums,
    )
    mine, theirs, gots, backs = together(mine, theirs, gots, backs)

    core_got = swap_bit(theirs, img, 0)
    add(trees, gots)
    last = Tree([jnp.concatenate([tree.terms[number] for tree in trees], -1) for number in range(4)], dims[2:])
    send = last.cut(*blk_bits[0])
    send, core_got = together(send, core_got)
    got = swap(send, *blk_bits[0], sizes)
    joined = sum_group(add_low(mine, core_got), "img", [2 * m for m in range(1, img // 2)], img)
    joined, feed_sum = together(joined, feed_sum)
    last.terms.append(got)
    send = last.cut(*blk_bits[1])
    last.terms.append(swap(send, *blk_bits[1], sizes))
    joined = sum_group(joined, "blk", range(1, blk), blk)
    other = swap_bit(joined, img, 0)
    last_sum, feed_sum = last.total(), feed_sum.astype(WIDE)
    result_large, result_small, grad_large, grad_small = place_results(
        place, backs, [result_small, grad_small], rows, small, smalls, small_rows
    )
    joined = jnp.where(core == 0, jnp.stack([joined, other]), jnp.stack([other, joined]))
    joined = joined.reshape(-1, TABLE_LANES).astype(WIDE)
    outs = []
    outs = []
    first = 0
    table_sizes.reverse()
    for table, count in zip((table_small, table_large), table_sizes):
        value = joined[first : first + count].reshape(-1, heads, TABLE_LANES)
        outs.append(jnp.transpose(value, (0, 2, 1)).reshape(-1, heads)[: table.shape[0]])
        first += count
    sums = joined[first:].reshape(-1)
    me = lax.axis_index("img") * blk + blk_me

    def own(place, length=1):
        return lax.dynamic_slice_in_dim(sums, place * width + me * share * length, share * length, 0)

    return (
        result_large,
        result_small,
        grad_large,
        grad_small,
        own(8),
        own(9),
        last_sum,
        own(6),
        own(7),
        outs[1],
        outs[0],
        feed_sum[:, hidden : hidden + width],
        own(5),
        own(4),
        own(2),
        own(3),
        feed_sum[:, :hidden],
        own(10, hidden // width),
        jnp.transpose(feed_sum[:, hidden + width :].reshape(share, -1, width), (1, 0, 2)).reshape(-1, width),
        own(1),
        own(0),
    )


def solution(mesh):
    img, blk = mesh.shape["img"], mesh.shape["blk"]

    def by_device(*args):
        if args[0].shape[0] == blk:
            return image_on_device(img, blk, *args)
        return on_device(*args)

    return jax.shard_map(
        by_device,
        mesh=mesh,
        in_specs=(
            P("img", "blk", None),
            P(("img", "blk"), None, None),
            P("img", "blk", None),
            P(("img", "blk"), None, None),
            P("img"),
            P(("img", "blk")),
            P(),
            P(),
            P(),
            P(),
            P(),
            P(),
            P(),
            P(),
            P(),
            P(),
            P(),
            P(),
            P(),
            P(),
            P(),
            P(),
            P(),
            P(),
            P(),
        ),
        out_specs=(
            P("img", "blk", None),
            P(("img", "blk"), None, None),
            P("img", "blk", None),
            P(("img", "blk"), None, None),
            P(("img", "blk")),
            P(("img", "blk")),
            P(("img", "blk"), None),
            P(("img", "blk")),
            P(("img", "blk")),
            P(),
            P(),
            P(("img", "blk"), None),
            P(("img", "blk")),
            P(("img", "blk")),
            P(("img", "blk")),
            P(("img", "blk")),
            P(("img", "blk"), None),
            P(("img", "blk")),
            P(("img", "blk"), None),
            P(("img", "blk")),
            P(("img", "blk")),
        ),
        check_vma=False,
    )
```
